32 devices in a mesh: batch: 4 (over x, core), seq: 8 (over z, y).
Axes of the slice: x: 2, y: 2, z: 4, core: 2. Of those that a mesh axis runs over, the one named last changes fastest.
Arguments:
- inputs: bfloat16 [3, 4, 2048, 1024], P(None, 'batch', 'seq'), may hold values from -6 to 6
- lengths: int32 [3, 4], P(None, 'batch'), may hold values from 1024 to 2048, as said below
- cotangent: bfloat16 [3, 4, 2048, 1024], P(None, 'batch', 'seq'), may hold values from -6 to 6
- norm1_gain: bfloat16 [1024], P(('batch', 'seq')), may hold values from 0.099609375 to 1.8984375
- norm1_bias: bfloat16 [1024], P(('batch', 'seq')), may hold values from -1.5 to 1.5
- step_size: bfloat16 [1024], P(('batch', 'seq')), may hold values from 0 to 1, as said below
- state_out: bfloat16 [2, 1024, 64], P(None, ('batch', 'seq')), may hold values from -128 to 128
- skip_gain: bfloat16 [1024], P(('batch', 'seq')), may hold values from -4 to 4
- glu_weight: bfloat16 [1024, 2048], P(('batch', 'seq')), may hold values from -0.1875 to 0.1875
- glu_bias: bfloat16 [2048], P(('batch', 'seq')), may hold values from -1.5 to 1.5
- norm2_gain: bfloat16 [1024], P(('batch', 'seq')), may hold values from 0.099609375 to 1.8984375
- norm2_bias: bfloat16 [1024], P(('batch', 'seq')), may hold values from -1.5 to 1.5
- ffn_in_weight: bfloat16 [1024, 4096], P(('batch', 'seq')), may hold values from -0.1875 to 0.1875
- ffn_in_bias: bfloat16 [4096], P(('batch', 'seq')), may hold values from -1.5 to 1.5
- ffn_out_weight: bfloat16 [4096, 1024], P(('batch', 'seq')), may hold values from -0.09375 to 0.09375
- ffn_out_bias: bfloat16 [1024], P(('batch', 'seq')), may hold values from -1.5 to 1.5
Outputs:
- output: bfloat16 [3, 4, 2048, 1024], P(None, 'batch', 'seq')
- input_grad: bfloat16 [3, 4, 2048, 1024], P(None, 'batch', 'seq')
- grad_norm1_gain: float32 [1024], P(('batch', 'seq'))
- grad_norm1_bias: float32 [1024], P(('batch', 'seq'))
- grad_state_out: float32 [2, 1024, 64], P(None, ('batch', 'seq'))
- grad_skip_gain: float32 [1024], P(('batch', 'seq'))
- grad_glu_weight: float32 [1024, 2048], P(('batch', 'seq'))
- grad_glu_bias: float32 [2048], P(('batch', 'seq'))
- grad_norm2_gain: float32 [1024], P(('batch', 'seq'))
- grad_norm2_bias: float32 [1024], P(('batch', 'seq'))
- grad_ffn_in_weight: float32 [1024, 4096], P(('batch', 'seq'))
- grad_ffn_in_bias: float32 [4096], P(('batch', 'seq'))
- grad_ffn_out_weight: float32 [4096, 1024], P(('batch', 'seq'))
- grad_ffn_out_bias: float32 [1024], P(('batch', 'seq'))
The draws below stay inside these ranges and needn't reach their ends.
Inputs may be any that keep to these rules, and one draw needn't show every extreme that they name: `lengths`: in every column one of the 3 contexts has the full length 2048. `step_size`: positive step sizes.
All inputs are finite; a program needn't handle non-finite values.
Results may differ from the reference program's by a relative error of at most 0.006.
Values may be sent and summed in bfloat16 or wider, within the bound.
No kernel may reach another device: no remote copies, remote signals or barrier semaphores. Data moves between devices by JAX's collectives and lax.ppermute only.
A program may use at most 448 MiB of HBM per device.

```python
import math
import jax
import jax.numpy as jnp
from jax import lax

D = 1024
N = 64
FF = 4096
MICRO = 3
L = 2048
SEQS = 4


def channel_steps(key, lowest, top_value):
    key = jax.random.fold_in(key, 11)
    share = jax.random.uniform(key, (D,), jnp.float32)
    low_log = jnp.log(jnp.float32(lowest))
    return jnp.exp(low_log + share * (jnp.log(jnp.float32(top_value)) - low_log))


def draw_step_size(key, part):
    top_value = 0.1
    return channel_steps(key, 0.1 / L, top_value).astype(jnp.bfloat16)


def draw_state_out(key, part):
    top_value = 0.1
    steps_drawn = channel_steps(key, 0.1 / L, top_value)
    key = jax.random.fold_in(key, 5)
    noise = jax.random.truncated_normal(key, -4.0, 4.0, (2, D, N), jnp.float32)
    return (0.7 * noise * jax.lax.rsqrt(N * steps_drawn)[None, :, None]).astype(jnp.bfloat16)


def draw_lengths(key, part):
    key = jax.random.fold_in(key, 7)
    pick_key, size_key = jax.random.split(key)
    whole_row = jax.random.randint(pick_key, (1, SEQS), 0, MICRO)
    drawn = jax.random.randint(size_key, (MICRO, SEQS), L // 2, L + 1)
    micro_rows = jnp.arange(MICRO, dtype=jnp.int32)[:, None]
    return jnp.where(micro_rows == whole_row, L, drawn).astype(jnp.int32)


def steps_of(stream_key, extent, cuts, smallest, high):
    gain, own = 1.0, jax.random.fold_in(stream_key, 6)
    for position, parts in cuts:
        draws = jnp.exp(jax.random.uniform(jax.random.fold_in(own, position), (parts,), jnp.float32, smallest / len(cuts), high / len(cuts)))
        gain = gain * jnp.repeat(draws, extent[position] // parts).reshape([-1 if axis == position else 1 for axis in range(len(extent))])
    return gain


def bell_draw(own_key, shape, width, bound, cuts=(), kind=jnp.bfloat16):
    array = width * jax.random.normal(own_key, shape, jnp.float32)
    if cuts:
        array = array * steps_of(own_key, shape, cuts, -0.22, 0.18)
    return jnp.clip(array, -bound, bound).astype(kind)


def setup_inputs(seed: int = 0) -> dict:
    streams_of = jax.random.split(jax.random.key(seed), 17)
    inputs = bell_draw(streams_of[0], (MICRO, SEQS, L, D), 1.0, 6.0, ((1, 4), (2, 8)))
    lengths = draw_lengths(jax.random.fold_in(streams_of[16], 71), 0)
    cotangent = bell_draw(streams_of[2], (MICRO, SEQS, L, D), 1.0, 6.0, ((1, 4), (2, 8)))
    norm1_gain = jnp.clip(1.0 + 0.18 * jax.random.normal(streams_of[3], (D,), jnp.float32), 0.099609375, 1.8984375).astype(jnp.bfloat16)
    norm1_bias = bell_draw(streams_of[4], (D,), 0.3, 1.5, ((0, 32),))
    step_size = draw_step_size(jax.random.fold_in(streams_of[16], 71), 0)
    state_out = draw_state_out(jax.random.fold_in(streams_of[16], 71), 0)
    skip_gain = bell_draw(streams_of[7], (D,), 1.0, 4.0, ((0, 32),))
    glu_weight = bell_draw(streams_of[8], (D, 2 * D), D ** -0.5, 0.1875, ((0, 32),))
    glu_bias = bell_draw(streams_of[9], (2 * D,), 0.3, 1.5, ((0, 32),))
    norm2_gain = jnp.clip(1.0 + 0.18 * jax.random.normal(streams_of[10], (D,), jnp.float32), 0.099609375, 1.8984375).astype(jnp.bfloat16)
    norm2_bias = bell_draw(streams_of[11], (D,), 0.3, 1.5, ((0, 32),))
    ffn_in_weight = bell_draw(streams_of[12], (D, FF), D ** -0.5, 0.1875, ((0, 32),))
    ffn_in_bias = bell_draw(streams_of[13], (FF,), 0.3, 1.5, ((0, 32),))
    ffn_out_weight = bell_draw(streams_of[14], (FF, D), FF ** -0.5, 0.09375, ((0, 32),))
    ffn_out_bias = bell_draw(streams_of[15], (D,), 0.3, 1.5, ((0, 32),))
    return {"inputs": inputs, "lengths": lengths, "cotangent": cotangent, "norm1_gain": norm1_gain, "norm1_bias": norm1_bias, "step_size": step_size, "state_out": state_out, "skip_gain": skip_gain, "glu_weight": glu_weight, "glu_bias": glu_bias, "norm2_gain": norm2_gain, "norm2_bias": norm2_bias, "ffn_in_weight": ffn_in_weight, "ffn_in_bias": ffn_in_bias, "ffn_out_weight": ffn_out_weight, "ffn_out_bias": ffn_out_bias}


@jax.custom_vjp
def low(v):
    return lax.optimization_barrier(v.astype(jnp.bfloat16)).astype(jnp.float32)

@jax.custom_vjp
def low_back(v):
    return v

def low_keep(v):
    return (low(v), None)

def low_pass(kept, grad):
    return (grad,)

def back_keep(v):
    return (v, None)

def back_low(kept, grad):
    return (low(grad),)
low.defvjp(low_keep, low_pass)
low_back.defvjp(back_keep, back_low)
norm_eps = 1e-05
channel_block = 256
highest = lax.Precision.HIGHEST

def layer_norm(values):
    centered = values - lax.optimization_barrier(jnp.mean(values, axis=-1, keepdims=True))
    return centered * lax.rsqrt(lax.optimization_barrier(jnp.mean(centered * centered, axis=-1, keepdims=True)) + norm_eps)

def matmul(left_side, right_side):
    return jnp.einsum('...d,de->...e', left_side, right_side, precision=highest)

def kernel_block(pieces):
    state_re, state_im, step_len = pieces
    mode_count = state_re.shape[1]
    turn_rate = math.pi * jnp.arange(mode_count, dtype=state_re.dtype)[None, :]
    decay_rate = -0.5 * step_len[:, None]
    phase_rate = turn_rate * step_len[:, None]
    magnitude = jnp.exp(decay_rate)
    step_im = magnitude * jnp.sin(phase_rate)
    minus_one = jnp.expm1(decay_rate) * jnp.cos(phase_rate) - 2.0 * jnp.sin(0.5 * phase_rate) ** 2
    denominator = 0.25 + turn_rate ** 2
    input_re = (-0.5 * minus_one + step_im * turn_rate) / denominator
    input_im = (-0.5 * step_im - minus_one * turn_rate) / denominator
    joint_re = state_re * input_re - state_im * input_im
    joint_im = state_re * input_im + state_im * input_re
    positions = jnp.arange(L, dtype=state_re.dtype)
    fading = jnp.exp(decay_rate[:, :, None] * positions)
    phase = phase_rate[:, :, None] * positions
    terms = fading * (joint_re[:, :, None] * jnp.cos(phase) - joint_im[:, :, None] * jnp.sin(phase))
    return lax.optimization_barrier(jnp.sum(terms, axis=1))

def state_conv(driven, state_out, step_len):
    block_count = step_len.shape[0] // channel_block
    state_re = state_out[0].reshape(block_count, channel_block, -1)
    state_im = state_out[1].reshape(block_count, channel_block, -1)
    steps_split = step_len.reshape(block_count, channel_block)
    kernel = lax.map(jax.checkpoint(kernel_block), (state_re, state_im, steps_split)).reshape(-1, L)
    drive_spec = jnp.fft.rfft(driven, n=2 * L, axis=1)
    kernel_spec = jnp.fft.rfft(kernel.T, n=2 * L, axis=0)
    return jnp.fft.irfft(drive_spec * kernel_spec[None], n=2 * L, axis=1)[:, :L]

def layer_block(residual_in, valid_rows, weights, step_len):
    gain_one, bias_one, state_out, skip_gain, glu_weight, glu_bias, gain_two, bias_two, in_weight, in_bias, out_weight, out_bias = weights
    width_all = residual_in.shape[-1]
    driven = valid_rows[..., None] * (layer_norm(residual_in) * gain_one + bias_one)
    mixed_out = state_conv(driven, state_out, step_len) + skip_gain * driven
    activated = low(jax.nn.gelu(mixed_out))
    gated_pre = low_back(matmul(activated, glu_weight) + glu_bias)
    residual = residual_in + gated_pre[..., :width_all] * jax.nn.sigmoid(gated_pre[..., width_all:])
    normed_two = low(layer_norm(residual) * gain_two + bias_two)
    hidden = low_back(matmul(normed_two, in_weight) + in_bias)
    spread = low(jax.nn.gelu(hidden))
    return residual + low_back(matmul(spread, out_weight) + out_bias)

def reference(inputs, lengths, cotangent, norm1_gain, norm1_bias, step_size, state_out, skip_gain, glu_weight, glu_bias, norm2_gain, norm2_bias, ffn_in_weight, ffn_in_bias, ffn_out_weight, ffn_out_bias):
    params = tuple((element.astype(jnp.float32) for element in (norm1_gain, norm1_bias, state_out, skip_gain, glu_weight, glu_bias, norm2_gain, norm2_bias, ffn_in_weight, ffn_in_bias, ffn_out_weight, ffn_out_bias)))
    step_len = step_size.astype(jnp.float32)
    positions = jnp.arange(L, dtype=jnp.int32)
    valid = (positions[None, None, :] < lengths[:, :, None]).astype(jnp.float32)
    start_rows = inputs.astype(jnp.float32)

    def forward(values, weights):

        def one_micro(carry, element):
            return (carry, layer_block(element[0], element[1], weights, step_len))
        return lax.scan(jax.checkpoint(one_micro), jnp.zeros((), jnp.float32), (values, valid))[1]
    result, back_fn = jax.vjp(forward, start_rows, params)
    grad_rows, grads = back_fn(valid[..., None] * cotangent.astype(jnp.float32))
    return (result.astype(jnp.bfloat16), grad_rows.astype(jnp.bfloat16), grads[0], grads[1], grads[2], grads[3], grads[4], grads[5], grads[6], grads[7], grads[8], grads[9], grads[10], grads[11])
```

```python
import functools
import math

import jax
import jax.numpy as jnp
import numpy as np
from jax import lax
from jax.experimental import pallas as pl
from jax.experimental.pallas import tpu as pltpu
from jax.sharding import PartitionSpec as P

f32 = jnp.float32
bf16 = jnp.bfloat16
norm_eps = 1e-05
near_span = 64
vmem_limit = 60 * 1024 * 1024
gelu_scale = math.sqrt(2.0 / math.pi)
gelu_cubic = 0.044715


def after(value, *tokens):
    return jax.tree.map(lambda v: lax.optimization_barrier((v, tokens))[0], value)


together = lax.optimization_barrier


def bits_of(size):
    count = size.bit_length() - 1
    if (1 << count) != size:
        raise ValueError("axis size")
    return count


def reverse_bits(value, count):
    result = 0
    for bit in range(count):
        result = result | (((value >> bit) & 1) << (count - 1 - bit))
    return result


def swap(value, axis, bit):
    size = lax.axis_size(axis)
    return lax.ppermute(value, axis, [(i, i ^ bit) for i in range(size)])


def gather_first(shard):
    return swap(shard[None], "seq", lax.axis_size("seq") // 2)


def gather_direct(shard):
    size = lax.axis_size("seq")
    return [swap(shard[None], "seq", bits) for bits in (size // 2, size // 4, size // 2 + size // 4)]


def gather_more(joined, lowest):
    size = lax.axis_size("seq")
    while joined.shape[0] << lowest < size:
        bit = size // joined.shape[0] // 2
        joined = jnp.concatenate([joined, swap(joined, "seq", bit)], axis=0)
    return joined


class Sum:
    def __init__(self, *terms):
        self.terms = list(terms)

    def total(self, start=0, stop=None):
        values = [term[start:stop].astype(f32) for term in self.terms]
        return functools.reduce(lambda a, b: a + b, values)

    def upper(self):
        return self.total(self.terms[0].shape[0] // 2).astype(bf16)

    def keep(self, came):
        half = self.terms[0].shape[0] // 2
        self.terms = [term[:half] for term in self.terms] + [came]

    def add(self, came):
        self.terms.append(came)

    def middle(self):
        for bit in range(2, bits_of(lax.axis_size("seq")) - 1):
            self.keep(swap(self.upper(), "seq", 1 << bit))


def swap_batch(pieces, bit):
    return [swap(piece, "batch", 1 << bit) for piece in pieces]


def gather_batch(part):
    pieces = [part]
    for bit in reversed(range(bits_of(lax.axis_size("batch")))):
        pieces = pieces + swap_batch(pieces, bit)
    return pieces


def reduce_batch(value):
    for bit in range(bits_of(lax.axis_size("batch"))):
        half = value.shape[0] // 2
        value = value[:half] + swap(value[half:], "batch", 1 << bit)
    return value[0]


def exchange(parts):
    return lax.all_to_all(parts, "seq", 0, 0)


def gelu_parts(values):
    square = values * values
    tanh = jnp.tanh(gelu_scale * values * (1.0 + gelu_cubic * square))
    half = 0.5 * (1.0 + tanh)
    return tanh, square, half


def gelu_value(values):
    return values * gelu_parts(values)[2]


def gelu_slope(values):
    tanh, square, half = gelu_parts(values)
    return half + 0.5 * values * (1.0 - tanh * tanh) * (
        gelu_scale * (1.0 + 3.0 * gelu_cubic * square)
    )


def gelu_both(values):
    tanh, square, half = gelu_parts(values)
    slope = half + 0.5 * values * (1.0 - tanh * tanh) * (
        gelu_scale * (1.0 + 3.0 * gelu_cubic * square)
    )
    return values * half, slope


def layer_stats(values):
    centered = values - jnp.mean(values, axis=-1, keepdims=True)
    scale_inv = lax.rsqrt(jnp.mean(centered * centered, axis=-1, keepdims=True) + norm_eps)
    return centered * scale_inv, scale_inv


def norm_back(grad_normed, normed, scale_inv):
    first_mean = jnp.mean(grad_normed, axis=-1, keepdims=True)
    second_mean = jnp.mean(grad_normed * normed, axis=-1, keepdims=True)
    return scale_inv * (grad_normed - first_mean - normed * second_mean)


def dot(left, right):
    return jnp.dot(left, right, preferred_element_type=f32)


def dot_left_t(left, right):
    return lax.dot_general(left, right, (((0,), (0,)), ((), ())), preferred_element_type=f32)


def dot_right_t(left, right):
    return lax.dot_general(left, right, (((1,), (1,)), ((), ())), preferred_element_type=f32)


def stack_split(values):
    high = values.astype(bf16)
    low = (values - high.astype(f32)).astype(bf16)
    return jnp.concatenate([high, high, low], axis=0)


def table_split(table):
    high = table.astype(jnp.bfloat16)
    low = (table - high.astype(np.float64)).astype(jnp.bfloat16)
    return np.concatenate([high, low, high], axis=1)


def transform_tables(span):
    freqs = np.arange(span, dtype=np.float64) + 0.5
    phase = 2.0 * math.pi / (2 * span) * freqs[:, None] * np.arange(span, dtype=np.float64)[None]
    forward = np.concatenate([np.cos(phase), -np.sin(phase)], axis=0)
    backward = np.concatenate([np.cos(phase).T, -np.sin(phase).T], axis=1) / span
    return table_split(forward), table_split(backward)


def loop(count, body):
    if count <= 8:
        for index in range(count):
            body(index)
    else:
        lax.fori_loop(0, count, lambda index, carry: (body(index), carry)[1], 0)


def sum_loop(first, last, body, init):
    if isinstance(first, int) and isinstance(last, int):
        for index in range(first, last):
            init = body(index, init)
        return init
    return lax.fori_loop(first, last, body, init)


def full_spec(shape, buffered=True):
    zeros = (0,) * len(shape)
    if buffered:
        return pl.BlockSpec(shape, lambda *_: zeros, pipeline_mode=pl.Buffered(1))
    return pl.BlockSpec(shape, lambda *_: zeros)


def parted(parts, span, chan):
    return pl.BlockSpec((parts, span, chan), lambda m, _: (0, m, 0))


def call(kernel, grid, meta, in_specs, operands, out_specs, out_shape, scratch, flops, name):
    return pl.pallas_call(
        kernel,
        grid_spec=pltpu.PrefetchScalarGridSpec(
            num_scalar_prefetch=1,
            grid=grid,
            in_specs=in_specs,
            out_specs=out_specs,
            scratch_shapes=scratch,
        ),
        out_shape=out_shape,
        compiler_params=pltpu.CompilerParams(
            vmem_limit_bytes=vmem_limit, dimension_semantics=("arbitrary",) * len(grid)
        ),
        cost_estimate=pl.CostEstimate(
            flops=int(flops * 0.02), bytes_accessed=int(flops * 0.02 / 400), transcendentals=0
        ),
        name=name,
    )(meta, *operands)


def norm_kernel(batch_bits, shard_rows, seq_size, meta, x_ref, extra_ref, out_ref, perm_ref):
    width = x_ref.shape[2]
    chan = out_ref.shape[-1]

    @pl.when(pl.program_id(0) == 0)
    def _():
        lane = lax.broadcasted_iota(jnp.int32, (width, width), 1)
        piece = (lane & (chan - 1)) // shard_rows
        source = (
            (reverse_bits(piece, batch_bits) ^ meta[0]) * seq_size + lane // chan
        ) * shard_rows + (lane & (shard_rows - 1))
        row = lax.broadcasted_iota(jnp.int32, (width, width), 0)
        perm_ref[...] = jnp.where(row == source, 1.0, 0.0).astype(bf16)
        for d in range(out_ref.shape[0]):
            out_ref[d, pl.ds(out_ref.shape[1] - extra_ref.shape[0], extra_ref.shape[0]), :] = (
                extra_ref[...]
            )

    span = x_ref.shape[1]
    rows = pl.ds(pl.multiple_of(pl.program_id(0) * span, span), span)
    normed, _ = layer_stats(x_ref[0].astype(f32))
    spread = dot(normed.astype(bf16), perm_ref[...]).astype(bf16)
    for d in range(out_ref.shape[0]):
        out_ref[d, rows, :] = spread[:, d * chan : (d + 1) * chan]


def norm_call(meta, x, extra, batch_bits, shard_rows, parts):
    micro, span, width = x.shape
    chan = width // parts
    return call(
        functools.partial(norm_kernel, batch_bits, shard_rows, parts),
        (micro,),
        meta,
        [pl.BlockSpec((1, span, width), lambda m, _: (m, 0, 0)), full_spec(extra.shape)],
        (x, extra),
        [full_spec((parts, micro * span + extra.shape[0], chan)), full_spec((width, width))],
        [
            jax.ShapeDtypeStruct((parts, micro * span + extra.shape[0], chan), bf16),
            jax.ShapeDtypeStruct((width, width), bf16),
        ],
        [],
        2 * micro * span * width * width,
        "norm_one",
    )


def kernel_kernel(meta, lift_re, lift_im, near_re, near_im, fwd_ref, out_ref, series, spec):
    modes, span_near, chan = near_re.shape
    far_count = lift_re.shape[1]
    blocks, _, span, _ = out_ref.shape
    group = 2

    def far_group(index, carry):
        def one_mode(n, acc):
            near_r, near_i = near_re[n], near_im[n]
            result = []
            for g in range(group):
                row = index * group + g
                a = lift_re[n, pl.ds(row, 1), :]
                b = lift_im[n, pl.ds(row, 1), :]
                result.append(acc[g] + (a * near_r - b * near_i))
            return tuple(result)

        zero = jnp.zeros((span_near, chan), f32)
        acc = lax.fori_loop(0, modes, one_mode, (zero,) * group, unroll=4)
        for g in range(group):
            start = pl.multiple_of((index * group + g) * span_near, span_near)
            series[pl.ds(start, span_near), :] = acc[g]
        return carry

    lax.fori_loop(0, far_count // group, far_group, 0)

    def one_pair(index):
        first = index * 2 * span
        pair = [series[pl.ds(first + k * span, span), :] for k in range(2)]
        both = dot(fwd_ref[...], stack_split(jnp.concatenate(pair, axis=1)))
        for k in range(2):
            spec[index * 2 + k] = both[:, k * chan : (k + 1) * chan]

    loop(blocks // 2, one_pair)
    rows = lax.broadcasted_iota(jnp.int32, (span, chan), 0)
    sign = 1.0 - 2.0 * (rows & 1).astype(f32)

    def one_block(d):
        real, imag = spec[d, :span], spec[d, span:]
        before = d - 1 if isinstance(d, int) else jnp.maximum(d - 1, 0)
        if isinstance(d, int) and d == 0:
            out_ref[0, 0], out_ref[0, 1] = real, imag
            return
        keep = 1.0 if isinstance(d, int) else jnp.where(d > 0, 1.0, 0.0)
        out_ref[d, 0] = real - keep * (sign * spec[before, span:])
        out_ref[d, 1] = imag + keep * (sign * spec[before, :span])

    loop(blocks, one_block)


def kernel_call(meta, lift, near, fwd, blocks, span):
    chan = near[0].shape[-1]
    operands = (lift[0], lift[1], near[0], near[1], fwd)
    return call(
        kernel_kernel,
        (1,),
        meta,
        [full_spec(a.shape) for a in operands],
        operands,
        full_spec((blocks, 2, span, chan)),
        jax.ShapeDtypeStruct((blocks, 2, span, chan), f32),
        [pltpu.VMEM((blocks * span, chan), f32), pltpu.VMEM((blocks, 2 * span, chan), f32)],
        1.1e10,
        "state_kernel",
    )


def mask_of(meta, m, block, span, chan):
    rows = block * span + lax.broadcasted_iota(jnp.int32, (span, chan), 0)
    return (rows < meta[1 + m]).astype(f32)


freq_tile = 64


def conv_kernel(
    meta,
    normed_ref,
    vec_ref,
    spec_ref,
    fwd_ref,
    inv_ref,
    drive_ref,
    mixed_ref,
    out_ref,
    drive,
    spectrum,
):
    m = pl.program_id(0)
    blocks, span, chan = drive.shape
    gain, bias, skip = vec_ref[0:1, :], vec_ref[1:2, :], vec_ref[2:3, :]

    def drive_pair(pair):
        values = []
        for k in range(2):
            block = 2 * pair + k
            normed = normed_ref[block].astype(f32)
            u = mask_of(meta, m, block, span, chan) * (normed * gain + bias)
            drive[block] = u
            values.append(u)
        both = dot(fwd_ref[...], stack_split(jnp.concatenate(values, axis=1)))
        for k in range(2):
            drive_ref[0, 2 * pair + k] = both[:, k * chan : (k + 1) * chan]

    loop(blocks // 2, drive_pair)

    def one_pair(index):
        for k in range(2):
            i = index * 2 + k

            def one_tile(tile, carry):
                low = pl.ds(pl.multiple_of(tile * freq_tile, freq_tile), freq_tile)
                high = pl.ds(pl.multiple_of(span + tile * freq_tile, freq_tile), freq_tile)

                def one_term(j, acc):
                    xr, xi = drive_ref[0, j, low], drive_ref[0, j, high]
                    gr, gi = spec_ref[i - j, 0, low], spec_ref[i - j, 1, low]
                    return (acc[0] + (xr * gr - xi * gi), acc[1] + (xr * gi + xi * gr))

                zero = jnp.zeros((freq_tile, chan), f32)
                acc = sum_loop(0, i + 1, one_term, (zero, zero))
                spectrum[k, low] = acc[0]
                spectrum[k, high] = acc[1]
                return carry

            lax.fori_loop(0, span // freq_tile, one_tile, 0)
        both = dot(
            inv_ref[...], stack_split(jnp.concatenate([spectrum[0], spectrum[1]], axis=1))
        )
        for k in range(2):
            i = index * 2 + k
            mixed = both[:, k * chan : (k + 1) * chan] + skip * drive[i]
            mixed_ref[0, i] = mixed
            out_ref[i] = gelu_value(mixed).astype(bf16)

    loop(blocks // 2, one_pair)


def conv_call(meta, micro, normed, vec, spec, fwd, inv):
    parts, _, chan = normed.shape
    span = spec.shape[2]
    wide = lambda rows: pl.BlockSpec((1, parts, rows, chan), lambda m, _: (m, 0, 0, 0))
    return call(
        conv_kernel,
        (micro,),
        meta,
        [parted(parts, span, chan)] + [full_spec(a.shape) for a in (vec, spec, fwd, inv)],
        (normed, vec, spec, fwd, inv),
        [wide(2 * span), wide(span), parted(parts, span, chan)],
        [
            jax.ShapeDtypeStruct((micro, parts, 2 * span, chan), f32),
            jax.ShapeDtypeStruct((micro, parts, span, chan), f32),
            jax.ShapeDtypeStruct((parts, micro * span, chan), bf16),
        ],
        [
            pltpu.VMEM((parts, span, chan), f32),
            pltpu.VMEM((2, 2 * span, chan), f32),
        ],
        1.5e10,
        "state_conv",
    )


def back_kernel(
    meta,
    grads_ref,
    normed_ref,
    drive_ref,
    mixed_ref,
    vec_ref,
    spec_ref,
    fwd_ref,
    inv_ref,
    extra_ref,
    out_ref,
    cross_ref,
    sums_ref,
    grad_mixed,
    grad_spec,
    spectrum,
):
    m = pl.program_id(0)
    blocks, span, chan = grad_mixed.shape
    gain, bias, skip = vec_ref[0:1, :], vec_ref[1:2, :], vec_ref[2:3, :]

    @pl.when(m == 0)
    def _():
        cross_ref[...] = jnp.zeros_like(cross_ref)
        sums_ref[...] = jnp.zeros_like(sums_ref)
        extra = extra_ref.shape[1]
        out_ref[:, pl.ds(out_ref.shape[1] - extra, extra), :] = extra_ref[...]

    def grad_pair(pair):
        values = []
        for k in range(2):
            block = 2 * pair + k
            normed = normed_ref[block].astype(f32)
            u = mask_of(meta, m, block, span, chan) * (normed * gain + bias)
            gm = grads_ref[block].astype(f32) * gelu_slope(mixed_ref[0, block])
            sums_ref[0:1, :] += jnp.sum(gm * u, axis=0, keepdims=True)
            grad_mixed[block] = gm
            values.append(gm)
        both = dot(fwd_ref[...], stack_split(jnp.concatenate(values, axis=1)))
        for k in range(2):
            grad_spec[2 * pair + k] = both[:, k * chan : (k + 1) * chan]

    loop(blocks // 2, grad_pair)

    def tiles_of(body):
        def one_tile(tile, carry):
            low = pl.ds(pl.multiple_of(tile * freq_tile, freq_tile), freq_tile)
            high = pl.ds(pl.multiple_of(span + tile * freq_tile, freq_tile), freq_tile)
            body(low, high)
            return carry

        lax.fori_loop(0, span // freq_tile, one_tile, 0)

    zero = jnp.zeros((freq_tile, chan), f32)

    def one_pair(index):
        for k in range(2):
            j = index * 2 + k

            def body(low, high):
                def one_term(i, acc):
                    mr, mi = grad_spec[i, low], grad_spec[i, high]
                    gr, gi = spec_ref[i - j, 0, low], spec_ref[i - j, 1, low]
                    return (acc[0] + (mr * gr + mi * gi), acc[1] + (mi * gr - mr * gi))

                acc = sum_loop(j, blocks, one_term, (zero, zero))
                spectrum[k, low] = acc[0]
                spectrum[k, high] = acc[1]

            tiles_of(body)
        both = dot(
            inv_ref[...], stack_split(jnp.concatenate([spectrum[0], spectrum[1]], axis=1))
        )
        for k in range(2):
            j = index * 2 + k
            grad_mixed[j] = both[:, k * chan : (k + 1) * chan] + skip * grad_mixed[j]

    loop(blocks // 2, one_pair)

    def finish(block):
        g = mask_of(meta, m, block, span, chan) * grad_mixed[block]
        normed = normed_ref[block].astype(f32)
        sums_ref[1:2, :] += jnp.sum(g * normed, axis=0, keepdims=True)
        sums_ref[2:3, :] += jnp.sum(g, axis=0, keepdims=True)
        out_ref[block, pl.ds(pl.multiple_of(m * span, span), span), :] = (g * gain).astype(bf16)

    loop(blocks, finish)

    def one_lag(d):
        def body(low, high):
            def one_term(j, acc):
                mr, mi = grad_spec[j + d, low], grad_spec[j + d, high]
                xr, xi = drive_ref[0, j, low], drive_ref[0, j, high]
                return (acc[0] + (mr * xr + mi * xi), acc[1] + (mi * xr - mr * xi))

            acc = sum_loop(0, blocks - d, one_term, (cross_ref[d, low], cross_ref[d, high]))
            cross_ref[d, low] = acc[0]
            cross_ref[d, high] = acc[1]

        tiles_of(body)

    loop(blocks, one_lag)


def back_call(meta, grads, normed, drive, mixed, vec, spec, fwd, inv, extra):
    parts, _, chan = normed.shape
    micro, _, span, _ = mixed.shape
    total = micro * span + extra.shape[1]
    mode = None if parts <= 8 else pl.Buffered(1)
    wide = lambda rows: pl.BlockSpec(
        (1, parts, rows, chan), lambda m, _: (m, 0, 0, 0), pipeline_mode=mode
    )
    return call(
        back_kernel,
        (micro,),
        meta,
        [parted(parts, span, chan)] * 2
        + [wide(2 * span), wide(span)]
        + [full_spec(a.shape) for a in (vec, spec, fwd, inv, extra)],
        (grads, normed, drive, mixed, vec, spec, fwd, inv, extra),
        [
            full_spec((parts, total, chan)),
            full_spec((parts, 2 * span, chan)),
            full_spec((8, chan)),
        ],
        [
            jax.ShapeDtypeStruct((parts, total, chan), bf16),
            jax.ShapeDtypeStruct((parts, 2 * span, chan), f32),
            jax.ShapeDtypeStruct((8, chan), f32),
        ],
        [
            pltpu.VMEM((parts, span, chan), f32),
            pltpu.VMEM((parts, 2 * span, chan), f32),
            pltpu.VMEM((2, 2 * span, chan), f32),
        ],
        2e10,
        "state_back",
    )


def modes_kernel(meta, cross_ref, far_re, far_im, near_re, near_im, inv_ref, out_ref, series):
    modes, span_near, chan = near_re.shape
    far_count = far_re.shape[1]
    blocks, double, _ = cross_ref.shape
    span = double // 2
    rows = lax.broadcasted_iota(jnp.int32, (span, chan), 0)
    sign = 1.0 - 2.0 * (rows & 1).astype(f32)

    def one_pair(index):
        pair = []
        for k in range(2):
            d = index * 2 + k
            real, imag = cross_ref[d, :span], cross_ref[d, span:]
            if isinstance(d, int):
                keep = 1.0 if d + 1 < blocks else 0.0
                after = min(d + 1, blocks - 1)
            else:
                keep = jnp.where(d + 1 < blocks, 1.0, 0.0)
                after = jnp.minimum(d + 1, blocks - 1)
            real = real + keep * (sign * cross_ref[after, span:])
            imag = imag - keep * (sign * cross_ref[after, :span])
            pair.append(jnp.concatenate([real, imag], axis=0))
        both = dot(inv_ref[...], stack_split(jnp.concatenate(pair, axis=1)))
        for k in range(2):
            series[pl.ds((index * 2 + k) * span, span), :] = both[:, k * chan : (k + 1) * chan]

    loop(blocks // 2, one_pair)
    group = 2

    def mode_group(index, carry):
        def one_far(i, acc):
            values = series[pl.ds(pl.multiple_of(i * span_near, span_near), span_near), :]
            result = []
            for g in range(group):
                n = index * group + g
                a = far_re[n, pl.ds(i, 1), :]
                b = far_im[n, pl.ds(i, 1), :]
                result.append((acc[g][0] + a * values, acc[g][1] + b * values))
            return tuple(result)

        zero = jnp.zeros((span_near, chan), f32)
        acc = lax.fori_loop(0, far_count, one_far, ((zero, zero),) * group, unroll=4)
        for g in range(group):
            n = index * group + g
            near_r, near_i = near_re[n], near_im[n]
            re, im = acc[g]
            out_ref[0, pl.ds(n, 1), :] = jnp.sum(re * near_r - im * near_i, axis=0, keepdims=True)
            out_ref[1, pl.ds(n, 1), :] = jnp.sum(re * near_i + im * near_r, axis=0, keepdims=True)
        return carry

    lax.fori_loop(0, modes // group, mode_group, 0)


def modes_call(meta, cross, far, near, inv):
    modes, _, chan = near[0].shape
    blocks, double, _ = cross.shape
    operands = (cross, far[0], far[1], near[0], near[1], inv)
    return call(
        modes_kernel,
        (1,),
        meta,
        [full_spec(a.shape) for a in operands],
        operands,
        full_spec((2, modes, chan)),
        jax.ShapeDtypeStruct((2, modes, chan), f32),
        [pltpu.VMEM((blocks * double // 2, chan), f32)],
        1.1e10,
        "state_modes",
    )


class Rows:
    def __init__(self, width, shard_rows, seq_size, batch_size, table):
        self.width = width
        self.shard_rows = shard_rows
        self.seq_size = seq_size
        self.batch_size = batch_size
        self.table = table
        self.piece_rows = shard_rows * seq_size
        self.by_block = shard_rows % 16 == 0

    def natural(self, meta, p, q):
        start = meta[self.table + p * self.seq_size + q] * self.shard_rows
        return pl.ds(pl.multiple_of(start, self.shard_rows), self.shard_rows)

    def order(self, meta, place):
        shape = (self.width, self.width)
        relative = lax.broadcasted_iota(jnp.int32, shape, 0)
        piece = relative // self.piece_rows
        position = (relative % self.piece_rows) // self.shard_rows
        shard = (reverse_bits(piece, bits_of(self.batch_size)) ^ meta[place + 1]) * self.seq_size
        shard = shard + (reverse_bits(position, bits_of(self.seq_size)) ^ meta[0])
        source = shard * self.shard_rows + relative % self.shard_rows
        return jnp.where(lax.broadcasted_iota(jnp.int32, shape, 1) == source, 1.0, 0.0).astype(bf16)

    def to_natural(self, meta, place, parts, target):
        if self.by_block:
            for p, part in enumerate(parts):
                for q in range(self.seq_size):
                    target[self.natural(meta, p, q), :] = part[
                        pl.ds(q * self.shard_rows, self.shard_rows), :
                    ]
        else:
            whole = jnp.concatenate([part[...] for part in parts], axis=0)
            target[...] = dot_left_t(self.order(meta, place), whole).astype(bf16)

    def to_relative(self, meta, place, value, scratch, store):
        if self.by_block:
            scratch[...] = value.astype(bf16)
        else:
            moved = dot(self.order(meta, place), value.astype(bf16))
        for p in range(self.batch_size):
            for q in range(self.seq_size):
                if self.by_block:
                    block = scratch[self.natural(meta, p, q), :]
                else:
                    start = (p * self.seq_size + q) * self.shard_rows
                    block = moved[start : start + self.shard_rows].astype(bf16)
                store(p, q, block)


def gate_kernel(pieces, order, meta, *refs):
    active_ref, x_ref, cot_ref, perm_ref, vec_ref, glu_bias_ref = refs[:6]
    weights = refs[6 : 6 + pieces]
    act_ref, resid_ref, gated_ref, norm_ref, norm_t_ref, cot_out, weight_scr = refs[6 + pieces :]
    m = pl.program_id(0)
    _, span, width = x_ref.shape
    micro = pl.num_programs(0)

    @pl.when(m == 0)
    def _():
        order.to_natural(meta, 1 + micro, weights, weight_scr)

    act = jnp.concatenate([active_ref[d] for d in range(active_ref.shape[0])], axis=1)
    act = dot_right_t(act, perm_ref[...]).astype(bf16)
    act_ref[0] = act
    gated = dot(act, weight_scr[...]) + glu_bias_ref[...]
    gated_ref[0] = gated
    residual = x_ref[0].astype(f32) + gated[:, :width] * jax.nn.sigmoid(gated[:, width:])
    resid_ref[0] = residual
    normed, _ = layer_stats(residual)
    norm_two = (normed * vec_ref[0:1, :] + vec_ref[1:2, :]).astype(bf16)
    norm_ref[...] = norm_two
    norm_t_ref[...] = norm_two.T
    rows = meta[1 + micro] + lax.broadcasted_iota(jnp.int32, (span, width), 0)
    cot_out[...] = jnp.where(rows < meta[1 + m], cot_ref[0].astype(f32), 0.0).astype(bf16)


def gate_call(meta, order, active, x, cot, perm, vec, glu_bias, weights):
    parts, _, chan = active.shape
    pieces = len(weights)
    micro, span, width = x.shape
    tokens = micro * span
    tile = lambda cols: pl.BlockSpec((1, span, cols), lambda m, _: (m, 0, 0))
    flat = pl.BlockSpec((span, width), lambda m, _: (m, 0))
    return call(
        functools.partial(gate_kernel, pieces, order),
        (micro,),
        meta,
        [parted(parts, span, chan), tile(width), tile(width)]
        + [full_spec(a.shape) for a in (perm, vec, glu_bias, *weights)],
        (active, x, cot, perm, vec, glu_bias, *weights),
        [
            tile(width),
            tile(width),
            tile(2 * width),
            flat,
            pl.BlockSpec((width, span), lambda m, _: (0, m)),
            flat,
        ],
        [
            jax.ShapeDtypeStruct((micro, span, width), bf16),
            jax.ShapeDtypeStruct((micro, span, width), f32),
            jax.ShapeDtypeStruct((micro, span, 2 * width), f32),
            jax.ShapeDtypeStruct((tokens, width), bf16),
            jax.ShapeDtypeStruct((width, tokens), bf16),
            jax.ShapeDtypeStruct((tokens, width), bf16),
        ],
        [pltpu.VMEM((width, 2 * width), bf16)],
        6 * tokens * width * width,
        "gated_unit",
    )


ff_block = 512


def ffn_kernel(pieces, batch_pieces, sub, order, out_table, place, meta, *refs):
    norm_ref, norm_t_ref, cot_ref, bias_ref = refs[:4]
    w_in = refs[4 : 4 + batch_pieces]
    w_out = refs[4 + batch_pieces : 4 + batch_pieces + pieces]
    rest = refs[4 + batch_pieces + pieces :]
    out_ref, back_ref, grad_bias = rest[:3]
    grad_out = rest[3 : 3 + pieces]
    grad_in = rest[3 + pieces : 3 + pieces + batch_pieces // 2]
    grad_in_send, in_scr, out_scr, grad_in_scr = rest[3 + pieces + batch_pieces // 2 :]
    k = pl.program_id(0)
    s = pl.program_id(1)
    order.to_natural(meta, place, w_in, in_scr)
    subs = ff_block // sub

    def sub_rows(t):
        return pl.ds(pl.multiple_of(meta[out_table + s * subs + t] * sub, sub), sub)

    for piece in range(pieces):

        @pl.when(k == piece)
        def _():
            for t in range(subs):
                out_scr[pl.ds(t * sub, sub), :] = w_out[piece][sub_rows(t), :]

    hidden = dot(norm_ref[...], in_scr[...]) + bias_ref[0]
    spread, slope = gelu_both(hidden)
    spread = spread.astype(bf16)
    grad_hidden = (dot_right_t(cot_ref[...], out_scr[...]) * slope).astype(bf16)
    grad_bias[0] = jnp.sum(grad_hidden.astype(f32), axis=0, keepdims=True)
    part_out = dot(spread, out_scr[...])
    part_back = dot_right_t(grad_hidden, in_scr[...])
    first = jnp.logical_and(k == 0, s == 0)

    @pl.when(first)
    def _():
        out_ref[...] = part_out
        back_ref[...] = part_back

    @pl.when(jnp.logical_not(first))
    def _():
        out_ref[...] += part_out
        back_ref[...] += part_back

    def store(p, q, block):
        if p < batch_pieces // 2:
            grad_in[p][q, 0] = block
        else:
            grad_in_send[p - batch_pieces // 2, q, 0] = block

    part_in = dot(norm_t_ref[...], grad_hidden)
    order.to_relative(meta, place, part_in, grad_in_scr, store)

    part = dot_left_t(spread, cot_ref[...]).astype(bf16)
    for piece in range(pieces):

        @pl.when(k == piece)
        def _():
            for t in range(subs):
                grad_out[piece][sub_rows(t), :] = part[t * sub : (t + 1) * sub, :]


def ffn_call(meta, order, out_table, place, base, column, norm, norm_t, cot, bias, w_in, w_out):
    pieces, batch_pieces = len(w_out), len(w_in)
    tokens, width = norm.shape
    piece_ff = w_out[0].shape[0]
    steps = piece_ff // ff_block
    sub = piece_ff // order.seq_size
    rows = order.piece_rows
    half = batch_pieces // 2
    block = lambda k, s, meta: meta[base + k] + s
    seq_size, low = order.seq_size, order.shard_rows
    kept = pl.BlockSpec(
        (seq_size, 1, low, ff_block), lambda k, s, meta: (0, meta[column + k], 0, s)
    )
    sent = pl.BlockSpec(
        (half, seq_size, 1, low, ff_block), lambda k, s, meta: (0, 0, meta[column + k], 0, s)
    )
    outs = call(
        functools.partial(ffn_kernel, pieces, batch_pieces, sub, order, out_table, place),
        (pieces, steps),
        meta,
        [full_spec(a.shape) for a in (norm, norm_t, cot)]
        + [pl.BlockSpec((1, 1, ff_block), lambda k, s, meta: (block(k, s, meta), 0, 0))]
        + [
            pl.BlockSpec((rows, ff_block), lambda k, s, meta: (0, block(k, s, meta)))
            for _ in w_in
        ]
        + [full_spec(a.shape) for a in w_out],
        (norm, norm_t, cot, bias, *w_in, *w_out),
        [
            full_spec((tokens, width)),
            full_spec((tokens, width)),
            pl.BlockSpec((1, 1, ff_block), lambda k, s, meta: (meta[column + k] * steps + s, 0, 0)),
        ]
        + [full_spec(a.shape) for a in w_out]
        + [kept] * half
        + [sent],
        [
            jax.ShapeDtypeStruct((tokens, width), f32),
            jax.ShapeDtypeStruct((tokens, width), f32),
            jax.ShapeDtypeStruct((pieces * steps, 1, ff_block), f32),
        ]
        + [jax.ShapeDtypeStruct(a.shape, bf16) for a in w_out]
        + [jax.ShapeDtypeStruct((seq_size, pieces, low, piece_ff), bf16)] * half
        + [jax.ShapeDtypeStruct((half, seq_size, pieces, low, piece_ff), bf16)],
        [
            pltpu.VMEM((width, ff_block), bf16),
            pltpu.VMEM((ff_block, width), bf16),
            pltpu.VMEM((width, ff_block), bf16),
        ],
        12 * tokens * width * piece_ff * pieces,
        "feed_forward",
    )
    split = 3 + pieces
    return outs[0], outs[1], outs[2], outs[3:split], outs[split:-1], outs[-1]


def gate_back_kernel(pieces, halves, order, meta, *refs):
    ffn = refs[:halves]
    back = refs[halves : 2 * halves]
    resid_ref, gated_ref, act_ref, cot_ref, perm_ref, vec_ref = refs[2 * halves : 2 * halves + 6]
    weights = refs[2 * halves + 6 : 2 * halves + 6 + pieces]
    rest = refs[2 * halves + 6 + pieces :]
    out_ref, grad_resid_ref, glu_bias_ref, sums_ref, moved_ref = rest[:5]
    grad_keep = rest[5 : 5 + pieces // 2]
    grad_send, weight_scr, gated_scr, act_scr, grad_scr = rest[5 + pieces // 2 :]
    m = pl.program_id(0)
    count = pl.num_programs(0)
    span, width = cot_ref.shape

    @pl.when(m == 0)
    def _():
        glu_bias_ref[...] = jnp.zeros_like(glu_bias_ref)
        sums_ref[...] = jnp.zeros_like(sums_ref)
        order.to_natural(meta, 1 + count, weights, weight_scr)

    residual = resid_ref[0]
    total = ffn[0][...]
    grad_norm = back[0][...]
    for h in range(1, halves):
        total = total + ffn[h][...]
        grad_norm = grad_norm + back[h][...]
    out_ref[0] = (residual + (total + vec_ref[2:3, :])).astype(bf16)
    grad_out = cot_ref[...].astype(f32)
    normed, scale = layer_stats(residual)
    sums_ref[0:1, :] += jnp.sum(grad_out, axis=0, keepdims=True)
    sums_ref[1:2, :] += jnp.sum(grad_norm * normed, axis=0, keepdims=True)
    sums_ref[2:3, :] += jnp.sum(grad_norm, axis=0, keepdims=True)
    grad_resid = grad_out + norm_back(grad_norm * vec_ref[0:1, :], normed, scale)
    grad_resid_ref[0] = grad_resid
    gated = gated_ref[0]
    gate = jax.nn.sigmoid(gated[:, width:])
    grad_left = grad_resid * gate
    grad_right = grad_left * gated[:, :width] * (1.0 - gate)
    grad_gated = jnp.concatenate([grad_left, grad_right], axis=1).astype(bf16)
    glu_bias_ref[0:1, :] += jnp.sum(grad_gated.astype(f32), axis=0, keepdims=True)
    grad_act = dot_right_t(grad_gated, weight_scr[...]).astype(bf16)
    moved = dot(grad_act, perm_ref[...]).astype(bf16)
    chan = moved_ref.shape[-1]
    for d in range(moved_ref.shape[0]):
        moved_ref[d] = moved[:, d * chan : (d + 1) * chan]
    rows = pl.ds(pl.multiple_of(m * span, span), span)
    gated_scr[rows, :] = grad_gated
    act_scr[rows, :] = act_ref[0]

    @pl.when(m == count - 1)
    def _():
        half = width // 2
        for part in range(4):
            cols = pl.ds(part * half, half)
            value = dot_left_t(act_scr[...], gated_scr[:, cols])

            def store(p, q, block):
                if p < pieces // 2:
                    grad_keep[p][q, :, cols] = block
                else:
                    grad_send[p - pieces // 2, q, :, cols] = block

            order.to_relative(meta, 1 + count, value, grad_scr, store)


def gate_back_call(meta, order, parts, ffn, back, resid, gated, act, cot, perm, vec, weights):
    halves, pieces = len(ffn), len(weights)
    micro, span, width = resid.shape
    tokens = micro * span
    chan = width // parts
    tile = lambda cols: pl.BlockSpec((1, span, cols), lambda m, _: (m, 0, 0))
    flat = pl.BlockSpec((span, width), lambda m, _: (m, 0))
    outs = call(
        functools.partial(gate_back_kernel, pieces, halves, order),
        (micro,),
        meta,
        [flat] * (2 * halves)
        + [tile(width), tile(2 * width), tile(width), flat]
        + [full_spec(a.shape) for a in (perm, vec, *weights)],
        (*ffn, *back, resid, gated, act, cot, perm, vec, *weights),
        [
            tile(width),
            tile(width),
            full_spec((8, 2 * width)),
            full_spec((8, width)),
            parted(parts, span, chan),
        ]
        + [full_spec((parts, order.shard_rows, 2 * width))] * (pieces // 2)
        + [full_spec((pieces // 2, parts, order.shard_rows, 2 * width))],
        [
            jax.ShapeDtypeStruct((micro, span, width), bf16),
            jax.ShapeDtypeStruct((micro, span, width), f32),
            jax.ShapeDtypeStruct((8, 2 * width), f32),
            jax.ShapeDtypeStruct((8, width), f32),
            jax.ShapeDtypeStruct((parts, micro * span, chan), bf16),
        ]
        + [jax.ShapeDtypeStruct((parts, order.shard_rows, 2 * width), bf16)] * (pieces // 2)
        + [jax.ShapeDtypeStruct((pieces // 2, parts, order.shard_rows, 2 * width), bf16)],
        [
            pltpu.VMEM((width, 2 * width), bf16),
            pltpu.VMEM((tokens, 2 * width), bf16),
            pltpu.VMEM((tokens, width), bf16),
            pltpu.VMEM((width, width // 2), bf16),
        ],
        10 * tokens * width * width,
        "gated_back",
    )
    return outs[:5], outs[5:-1], outs[-1]


def input_kernel(meta, moved_ref, x_ref, grad_resid_ref, perm_ref, out_ref):
    e = jnp.concatenate([moved_ref[d] for d in range(moved_ref.shape[0])], axis=1)
    e = dot_right_t(e, perm_ref[...])
    normed, scale = layer_stats(x_ref[0].astype(f32))
    out_ref[0] = (grad_resid_ref[0] + norm_back(e, normed, scale)).astype(bf16)


def input_call(meta, moved, x, grad_resid, perm):
    parts, _, chan = moved.shape
    micro, span, width = x.shape
    tile = lambda cols: pl.BlockSpec((1, span, cols), lambda m, _: (m, 0, 0))
    return call(
        input_kernel,
        (micro,),
        meta,
        [parted(parts, span, chan), tile(width), tile(width), full_spec(perm.shape)],
        (moved, x, grad_resid, perm),
        tile(width),
        jax.ShapeDtypeStruct((micro, span, width), bf16),
        [],
        2 * micro * span * width * width,
        "input_grad",
    )


def mode_tables(step_len, mode_count, length):
    order = jnp.arange(mode_count, dtype=f32)[:, None]
    rate = order * step_len

    def power(offsets):
        turns = 0.5 * rate[:, None, :] * offsets[None, :, None]
        angle = 2.0 * math.pi * (turns - jnp.round(turns))
        fading = jnp.exp(-0.5 * step_len[:, None, :] * offsets[None, :, None])
        return fading * jnp.cos(angle), fading * jnp.sin(angle)

    def outer(far, near):
        a, b = far[0][:, :, None], far[1][:, :, None]
        c, d = near[0][:, None], near[1][:, None]
        shape = (mode_count, far[0].shape[1] * near[0].shape[1], step_len.shape[-1])
        return (a * c - b * d).reshape(shape), (a * d + b * c).reshape(shape)

    ramp = jnp.arange(8, dtype=f32)
    near = outer(power(8.0 * ramp), power(ramp))
    far_count = length // near_span
    far = outer(
        power(8.0 * near_span * jnp.arange(far_count // 8, dtype=f32)), power(near_span * ramp)
    )

    def wave(scale):
        turns = scale * rate
        return 2.0 * math.pi * (turns - jnp.round(turns))

    decay = -0.5 * step_len
    turn_rate = math.pi * order
    step_im = jnp.exp(decay) * jnp.sin(wave(0.5))
    minus_one = jnp.expm1(decay) * jnp.cos(wave(0.5)) - 2.0 * jnp.sin(wave(0.25)) ** 2
    denominator = 0.25 + turn_rate**2
    input_mult = (
        (-0.5 * minus_one + step_im * turn_rate) / denominator,
        (-0.5 * step_im - minus_one * turn_rate) / denominator,
    )
    return near, far, input_mult


def cmul(a, b):
    return a[0] * b[0] - a[1] * b[1], a[0] * b[1] + a[1] * b[0]


def per_device(
    inputs,
    lengths,
    cotangent,
    norm1_gain,
    norm1_bias,
    step_size,
    state_out,
    skip_gain,
    glu_weight,
    glu_bias,
    norm2_gain,
    norm2_bias,
    ffn_in_weight,
    ffn_in_bias,
    ffn_out_weight,
    ffn_out_bias,
):
    micro, _, span, width = inputs.shape
    batch_size, seq_size = lax.axis_size("batch"), lax.axis_size("seq")
    batch_bits, seq_bits = bits_of(batch_size), bits_of(seq_size)
    devices = batch_size * seq_size
    shard_rows = width // devices
    chan = width // seq_size
    length = span * seq_size
    mode_count = state_out.shape[2]
    ff = ffn_in_weight.shape[1]
    me_b, me_s = lax.axis_index("batch"), lax.axis_index("seq")
    me = me_b * seq_size + me_s

    natural_piece = reverse_bits(jnp.arange(batch_size, dtype=jnp.int32), batch_bits) ^ me_b
    piece_of = reverse_bits(jnp.arange(batch_size, dtype=jnp.int32) ^ me_b, batch_bits)
    place = jnp.arange(devices, dtype=jnp.int32)
    of_piece = reverse_bits(place // seq_size, batch_bits) ^ me_b
    of_seq = reverse_bits(place % seq_size, seq_bits) ^ me_s
    natural = of_piece * seq_size + of_seq
    ramp = jnp.arange(seq_size, dtype=jnp.int32)
    out_place = reverse_bits(ramp ^ me_s, seq_bits)
    piece_ff = ff // batch_size
    groups = [[p for p in range(batch_size) if p % 2 == half] for half in range(2)]
    of_group = natural_piece[jnp.array(groups[0] + groups[1])]
    place_at = 1 + micro
    in_table = 8
    out_table = in_table + devices
    base_table = out_table + seq_size
    column_table = base_table + batch_size
    meta = jnp.concatenate(
        [
            me_s[None].astype(jnp.int32),
            lengths[:, 0],
            jnp.stack([me_s * span, me_b]).astype(jnp.int32),
            jnp.zeros((8 - 3 - micro,), jnp.int32),
            natural,
            out_place,
            of_group * (piece_ff // ff_block),
            of_group & (batch_size // 2 - 1),
        ]
    )
    order = Rows(width, shard_rows, seq_size, batch_size, in_table)

    x = inputs[:, 0]
    cot = cotangent[:, 0]

    top = batch_bits - 1
    half = batch_size // 2

    def over_low(pieces):
        for bit in reversed(range(top)):
            pieces = pieces + swap_batch(pieces, bit)
        return pieces

    def weave(low, high):
        return [piece for pair in zip(low, high) for piece in pair]

    def join(*parts):
        return jnp.concatenate(parts, axis=0)

    def near_swap(value):
        return swap(value, "seq", 1)

    def middle_swap(value):
        return swap(value, "seq", 2)

    def last_swap(value):
        return swap(value, "seq", seq_size // 2)

    def top_swap(value):
        return swap(value, "batch", 1 << top)

    counts = [2 * shard_rows, shard_rows, shard_rows, shard_rows, 4 * shard_rows]
    starts = [sum(counts[:k]) for k in range(len(counts))]
    small_size = sum(counts)
    small = jnp.concatenate(
        [
            glu_bias,
            norm2_gain,
            norm2_bias,
            ffn_out_bias,
            ffn_in_bias,
            jnp.zeros((16 * chan - small_size,), bf16),
        ]
    )
    glu_1 = gather_direct(glu_weight)
    in_1 = gather_first(ffn_in_weight)
    normed, perm = norm_call(
        me_b[None].astype(jnp.int32),
        x,
        small.reshape(16, chan),
        batch_bits,
        shard_rows,
        seq_size,
    )
    normed, glu_1, in_1, ffn_out_weight, one, coefs = together(
        (
            normed,
            glu_1,
            in_1,
            ffn_out_weight,
            jnp.concatenate([norm1_gain, norm1_bias, skip_gain, step_size]),
            state_out,
        )
    )

    normed = exchange(normed)
    glu_w = gather_more(join(glu_weight[None], *glu_1), 1)
    glu_2 = near_swap(glu_w)
    in_w = gather_more(join(ffn_in_weight[None], in_1), 2)
    in_2 = middle_swap(in_w)
    out_1 = gather_first(ffn_out_weight)
    one, coefs = gather_batch(one), gather_batch(coefs)
    one = jnp.stack(one).reshape(batch_size, 4, shard_rows).astype(f32)
    one = jnp.moveaxis(one, 0, 1).reshape(4, chan)
    vec_one = jnp.concatenate([one[:3], jnp.zeros((5, chan), f32)], axis=0)
    coefs = jnp.concatenate(coefs, axis=1)
    coefs = jnp.swapaxes(coefs, 1, 2).astype(f32)
    near, far, input_mult = mode_tables(one[3:4], mode_count, length)
    joint = cmul(coefs, input_mult)
    lift = cmul((joint[0][:, None], joint[1][:, None]), far)
    fwd_np, inv_np = transform_tables(span)
    fwd, inv = jnp.asarray(fwd_np), jnp.asarray(inv_np)
    spec = kernel_call(meta, lift, near, fwd, seq_size, span)
    normed, glu_2, in_2, out_1, spec = together((normed, glu_2, in_2, out_1, spec))

    glu_w = join(glu_w, glu_2).reshape(-1, 2 * width)
    glu_top = top_swap(glu_w)
    in_w = join(in_w, in_2)
    in_3 = near_swap(in_w)
    out_w = gather_more(join(ffn_out_weight[None], out_1), 2)
    out_2 = middle_swap(out_w)
    drive_spec, mixed, active = conv_call(
        meta, micro, normed, vec_one, after(spec, glu_w, in_w, out_w), fwd, inv
    )
    active, glu_top, in_3, out_2 = together((active, glu_top, in_3, out_2))

    small_seq = after(normed, active)[:, micro * span :, :].reshape(seq_size, -1)[:, :small_size]
    active = exchange(active)
    (small_top,) = swap_batch([small_seq], top)
    in_w = join(in_w, in_3).reshape(-1, ff)
    in_top = top_swap(after(in_w, small_top))
    out_w = join(out_w, out_2)
    out_3 = near_swap(out_w)
    glu_parts = weave(over_low([glu_w]), over_low([glu_top]))
    small_all = jnp.stack(weave(over_low([small_seq]), over_low([small_top])))
    small_all = jnp.take(small_all, piece_of, axis=0).reshape(devices, -1).astype(f32)
    glu_bias_all, gain_two, bias_two, out_bias, in_bias = [
        small_all[:, s : s + c].reshape(-1) for s, c in zip(starts, counts)
    ]
    vec_two = jnp.concatenate(
        [gain_two[None], bias_two[None], out_bias[None], jnp.zeros((5, width), f32)]
    )
    in_low = over_low([after(in_w, vec_two, glu_bias_all, in_bias, glu_parts)])
    active, in_top, out_3, in_low = together((active, in_top, out_3, in_low))

    out_w = join(out_w, out_3).reshape(-1, width)
    out_top = top_swap(out_w)
    out_low = over_low([out_w])
    in_parts = weave(in_low, over_low([in_top]))
    act, resid, gated, norm_two, norm_two_t, cot_out = gate_call(
        meta, order, after(active, out_w), x, cot, perm, vec_two, glu_bias_all[None], glu_parts
    )

    in_bias_blocks = in_bias.reshape(ff // ff_block, 1, ff_block)

    def ffn_half(which, norm_two, weights):
        return ffn_call(
            meta,
            order,
            out_table,
            place_at,
            base_table + which * half,
            column_table + which * half,
            norm_two,
            norm_two_t,
            cot_out,
            in_bias_blocks,
            in_parts,
            weights,
        )

    def low_rest(values):
        for bit in range(1, top):
            keep, send = values[: len(values) // 2], values[len(values) // 2 :]
            came = swap(jnp.stack([Sum(*v).total().astype(bf16) for v in send]), "batch", 1 << bit)
            values = [v + [came[i]] for i, v in enumerate(keep)]
        return values

    def low_sum(keep, came):
        return low_rest([[v, came[i]] for i, v in enumerate(keep)])

    def out_send(parts):
        return parts[half // 2][None] if half == 2 else jnp.stack(parts[half // 2 :])

    def rounded(terms):
        return Sum(*terms).total().astype(bf16)

    out_a, back_a, bias_a, grad_out_a, keep_in_a, send_in_a = ffn_half(0, norm_two, out_low)
    out_top = after(out_top, out_a)
    in_a_came = swap(send_in_a, "batch", 1)
    out_a_came = swap(out_send(grad_out_a), "batch", 1)
    out_b, back_b, bias_b, grad_out_b, keep_in_b, send_in_b = ffn_half(
        1, after(norm_two, out_a), over_low([out_top])
    )
    in_a_came, out_a_came = after((in_a_came, out_a_came), out_b)

    in_b_came = swap(send_in_b, "batch", 1)
    out_b_came = swap(out_send(grad_out_b), "batch", 1)
    in_a_own, in_a_other = low_sum(keep_in_a, in_a_came)
    in_a_other = rounded(in_a_other)
    in_b_top = top_swap(in_a_other)
    (output, grad_resid, grad_glu_bias, sums, moved), keep_glu, send_glu = gate_back_call(
        meta,
        order,
        seq_size,
        [out_a, out_b],
        [back_a, back_b],
        after(resid, in_a_other),
        gated,
        act,
        cot_out,
        perm,
        vec_two,
        glu_parts,
    )
    moved, in_b_came, out_b_came, in_b_top = together((moved, in_b_came, out_b_came, in_b_top))

    grads_in = exchange(moved)
    glu_came = swap(send_glu, "batch", 1)
    (out_b_sum,) = low_sum(grad_out_b[: half // 2], out_b_came)
    out_b_sum = rounded(out_b_sum)
    out_a_top = top_swap(out_b_sum)
    in_b_own, in_b_other = low_sum(keep_in_b, in_b_came)
    in_b_other = rounded([after(in_b_other[0], out_b_sum), *in_b_other[1:]])
    in_a_top = top_swap(in_b_other)
    sum_in_b = Sum(*in_b_own, in_b_top)
    in_b_near = near_swap(sum_in_b.upper())

    lower = (me_b >> top) == 0

    def halves(a, b, axis):
        return jnp.concatenate([jnp.where(lower, a, b), jnp.where(lower, b, a)], axis=axis)

    in_bias_sums = halves(bias_a.reshape(-1), bias_b.reshape(-1), 0)
    small_grads = jnp.concatenate(
        [
            value.reshape(devices, -1)
            for value in (grad_glu_bias[0], sums[1], sums[2], sums[0], in_bias_sums)
        ],
        axis=1,
    )
    small_grads = small_grads.reshape(batch_size, seq_size, -1)
    small_grads = jnp.moveaxis(small_grads, 1, 0).reshape(seq_size, -1)
    high = lax.reduce_precision(small_grads, 8, 7)
    rest = (small_grads - high).astype(bf16)
    extra_rows = -(-2 * small_grads.shape[1] // (16 * chan)) * 16
    blank = jnp.zeros((seq_size, extra_rows * chan - 2 * small_grads.shape[1]), bf16)
    extra = jnp.concatenate([high.astype(bf16), rest, blank], axis=1)
    extra = extra.reshape(seq_size, extra_rows, chan)
    grads_in, glu_came, in_b_near, extra = together((grads_in, glu_came, in_b_near, extra))

    sum_in_b.keep(in_b_near)
    in_b_middle = sum_in_b.upper()
    moved_back, cross, state_sums = back_call(
        meta,
        after(grads_in, in_b_middle),
        normed,
        drive_spec,
        mixed,
        vec_one,
        spec,
        fwd,
        inv,
        extra,
    )
    in_b_middle = middle_swap(in_b_middle)
    moved_back, cross, in_b_middle, out_a_top, in_a_top = together(
        (moved_back, cross, in_b_middle, out_a_top, in_a_top)
    )

    moved_back = exchange(moved_back)
    (out_a_sum,) = low_sum(grad_out_a[: half // 2], out_a_came)
    sum_out = Sum(*[v.reshape(seq_size, -1, width) for v in (*out_a_sum, out_a_top)])
    out_near = sum_out.upper()
    out_near_came = near_swap(out_near)
    glu_own, glu_other = low_sum(keep_glu, glu_came)
    glu_other = rounded([after(glu_other[0], out_near), *glu_other[1:]])
    glu_top_came = top_swap(glu_other)
    sum_in_a = Sum(*in_a_own, after(in_a_top, glu_other))
    in_a_near = near_swap(sum_in_a.upper())
    sum_in_b.keep(in_b_middle)
    sum_in_b.middle()
    in_b_last = last_swap(sum_in_b.upper())
    moved_back, out_near_came, glu_top_came, in_a_near, in_b_last = together(
        (moved_back, out_near_came, glu_top_came, in_a_near, in_b_last)
    )

    sum_out.keep(out_near_came)
    out_middle = sum_out.upper()
    sum_in_a.keep(in_a_near)
    in_a_middle = sum_in_a.upper()
    sum_glu = Sum(*glu_own, glu_top_came)
    glu_near = sum_glu.upper()
    input_grad = input_call(
        meta, after(moved_back, out_middle, in_a_middle, glu_near), x, grad_resid, perm
    )
    out_middle, in_a_middle = middle_swap(out_middle), middle_swap(in_a_middle)
    glu_near = near_swap(glu_near)
    input_grad, out_middle, in_a_middle, glu_near = together(
        (input_grad, out_middle, in_a_middle, glu_near)
    )

    sum_out.keep(out_middle)
    sum_out.middle()
    out_last = sum_out.upper()
    sum_in_a.keep(in_a_middle)
    sum_in_a.middle()
    in_a_last = sum_in_a.upper()
    sum_glu.keep(glu_near)
    glu_middle = sum_glu.upper()
    raw_modes = modes_call(
        meta, after(cross, input_grad, out_last, in_a_last, glu_middle), far, near, inv
    )
    out_last, in_a_last = last_swap(out_last), last_swap(in_a_last)
    glu_middle = middle_swap(glu_middle)
    raw_modes, out_last, in_a_last, glu_middle = together(
        (raw_modes, out_last, in_a_last, glu_middle)
    )
    sum_glu.keep(glu_middle)
    sum_glu.middle()
    glu_last = last_swap(sum_glu.upper())

    def finish(value, came):
        value.keep(came)
        return value.total()[0]

    z = cmul((raw_modes[0], raw_modes[1]), input_mult)
    state_grads = jnp.concatenate([z[0], -z[1], state_sums[:3]], axis=0).T
    state_grads = reduce_batch(state_grads.reshape(batch_size, shard_rows, -1))
    grad_state = jnp.stack([state_grads[:, :mode_count], state_grads[:, mode_count : 2 * mode_count]])
    grad_out_total = finish(sum_out, out_last)
    far_in = halves(finish(sum_in_a, in_a_last), finish(sum_in_b, in_b_last), 0)
    grad_in_total = jnp.concatenate([far_in[b] for b in range(batch_size)], axis=1)
    grad_glu_total = finish(sum_glu, glu_last)

    small_came = moved_back[:, micro * span :, :].reshape(seq_size, -1).astype(f32)
    small_came = jnp.sum(small_came, axis=0)
    size = batch_size * small_size
    small_came = (small_came[:size] + small_came[size : 2 * size]).reshape(batch_size, -1)
    own = reduce_batch(jnp.take(small_came, natural_piece, axis=0))
    grad_glu_bias_own, grad_gain_two, grad_bias_two, grad_out_bias, grad_in_bias_own = [
        own[s : s + c] for s, c in zip(starts, counts)
    ]

    return (
        output[:, None],
        input_grad[:, None],
        state_grads[:, 2 * mode_count + 1],
        state_grads[:, 2 * mode_count + 2],
        grad_state,
        state_grads[:, 2 * mode_count],
        grad_glu_total,
        grad_glu_bias_own,
        grad_gain_two,
        grad_bias_two,
        grad_in_total,
        grad_in_bias_own,
        grad_out_total,
        grad_out_bias,
    )


def solution(mesh):
    both = ("batch", "seq")
    rows = P(None, "batch", "seq", None)
    vector = P(both)
    matrix = P(both, None)
    state = P(None, both, None)
    return jax.shard_map(
        per_device,
        mesh=mesh,
        in_specs=(
            rows,
            P(None, "batch"),
            rows,
            vector,
            vector,
            vector,
            state,
            vector,
            matrix,
            vector,
            vector,
            vector,
            matrix,
            vector,
            matrix,
            vector,
        ),
        out_specs=(
            rows,
            rows,
            vector,
            vector,
            state,
            vector,
            matrix,
            vector,
            vector,
            vector,
            matrix,
            vector,
            matrix,
            vector,
        ),
        check_vma=False,
    )
```

```python
import functools
import math

import jax
import jax.numpy as jnp
import numpy as np
from jax import lax
from jax.experimental import pallas as pl
from jax.experimental.pallas import tpu as pltpu
from jax.sharding import PartitionSpec as P

f32 = jnp.float32
bf16 = jnp.bfloat16
norm_eps = 1e-05
near_span = 64
vmem_limit = 60 * 1024 * 1024
gelu_scale = math.sqrt(2.0 / math.pi)
gelu_cubic = 0.044715


def after(value, *tokens):
    return jax.tree.map(lambda v: lax.optimization_barrier((v, tokens))[0], value)


together = lax.optimization_barrier


def bits_of(size):
    count = size.bit_length() - 1
    if (1 << count) != size:
        raise ValueError("axis size")
    return count


def reverse_bits(value, count):
    result = 0
    for bit in range(count):
        result = result | (((value >> bit) & 1) << (count - 1 - bit))
    return result


def swap(value, axis, bit):
    size = lax.axis_size(axis)
    return lax.ppermute(value, axis, [(i, i ^ bit) for i in range(size)])


def gather_first(shard):
    return swap(shard[None], "seq", lax.axis_size("seq") // 2)


def gather_direct(shard):
    size = lax.axis_size("seq")
    return [swap(shard[None], "seq", bits) for bits in (size // 2, size // 4, size // 2 + size // 4)]


def gather_more(joined, lowest):
    size = lax.axis_size("seq")
    while joined.shape[0] << lowest < size:
        bit = size // joined.shape[0] // 2
        joined = jnp.concatenate([joined, swap(joined, "seq", bit)], axis=0)
    return joined


class Sum:
    def __init__(self, *terms):
        self.terms = list(terms)

    def total(self, start=0, stop=None):
        values = [term[start:stop].astype(f32) for term in self.terms]
        return functools.reduce(lambda a, b: a + b, values)

    def upper(self):
        return self.total(self.terms[0].shape[0] // 2).astype(bf16)

    def keep(self, came):
        half = self.terms[0].shape[0] // 2
        self.terms = [term[:half] for term in self.terms] + [came]

    def add(self, came):
        self.terms.append(came)

    def middle(self):
        for bit in range(2, bits_of(lax.axis_size("seq")) - 1):
            self.keep(swap(self.upper(), "seq", 1 << bit))


def swap_batch(pieces, bit):
    return [swap(piece, "batch", 1 << bit) for piece in pieces]


def gather_batch(part):
    pieces = [part]
    for bit in reversed(range(bits_of(lax.axis_size("batch")))):
        pieces = pieces + swap_batch(pieces, bit)
    return pieces


def reduce_batch(value):
    for bit in range(bits_of(lax.axis_size("batch"))):
        half = value.shape[0] // 2
        value = value[:half] + swap(value[half:], "batch", 1 << bit)
    return value[0]


def exchange(parts):
    return lax.all_to_all(parts, "seq", 0, 0)


def gelu_parts(values):
    square = values * values
    half = 0.5 * jnp.tanh(values * (gelu_scale + gelu_scale * gelu_cubic * square)) + 0.5
    return square, half


def gelu_value(values):
    return values * gelu_parts(values)[1]


def gelu_both(values):
    square, half = gelu_parts(values)
    value = values * half
    inner = 2.0 * gelu_scale + 6.0 * gelu_scale * gelu_cubic * square
    return value, half + value * (1.0 - half) * inner


def gelu_slope(values):
    return gelu_both(values)[1]


def layer_stats(values):
    centered = values - jnp.mean(values, axis=-1, keepdims=True)
    scale_inv = lax.rsqrt(jnp.mean(centered * centered, axis=-1, keepdims=True) + norm_eps)
    return centered * scale_inv, scale_inv


def norm_back(grad_normed, normed, scale_inv):
    first_mean = jnp.mean(grad_normed, axis=-1, keepdims=True)
    second_mean = jnp.mean(grad_normed * normed, axis=-1, keepdims=True)
    return scale_inv * (grad_normed - first_mean - normed * second_mean)


def dot(left, right):
    return jnp.dot(left, right, preferred_element_type=f32)


def dot_left_t(left, right):
    return lax.dot_general(left, right, (((0,), (0,)), ((), ())), preferred_element_type=f32)


def dot_right_t(left, right):
    return lax.dot_general(left, right, (((1,), (1,)), ((), ())), preferred_element_type=f32)


def stack_split(values):
    high = values.astype(bf16)
    low = (values - high.astype(f32)).astype(bf16)
    return jnp.concatenate([high, high, low], axis=0)


def table_split(table):
    high = table.astype(jnp.bfloat16)
    low = (table - high.astype(np.float64)).astype(jnp.bfloat16)
    return np.concatenate([high, low, high], axis=1)


def transform_tables(span):
    freqs = np.arange(span, dtype=np.float64) + 0.5
    phase = 2.0 * math.pi / (2 * span) * freqs[:, None] * np.arange(span, dtype=np.float64)[None]
    forward = np.concatenate([np.cos(phase), -np.sin(phase)], axis=0)
    backward = np.concatenate([np.cos(phase).T, -np.sin(phase).T], axis=1) / span
    return table_split(forward), table_split(backward)


def loop(count, body):
    if count <= 8:
        for index in range(count):
            body(index)
    else:
        lax.fori_loop(0, count, lambda index, carry: (body(index), carry)[1], 0)


def sum_loop(first, last, body, init):
    if isinstance(first, int) and isinstance(last, int):
        for index in range(first, last):
            init = body(index, init)
        return init
    return lax.fori_loop(first, last, body, init)


def full_spec(shape, buffered=True):
    zeros = (0,) * len(shape)
    if buffered:
        return pl.BlockSpec(shape, lambda *_: zeros, pipeline_mode=pl.Buffered(1))
    return pl.BlockSpec(shape, lambda *_: zeros)


def parted(parts, span, chan):
    return pl.BlockSpec((parts, span, chan), lambda m, _: (0, m, 0))


def call(kernel, grid, meta, in_specs, operands, out_specs, out_shape, scratch, flops, name):
    return pl.pallas_call(
        kernel,
        grid_spec=pltpu.PrefetchScalarGridSpec(
            num_scalar_prefetch=1,
            grid=grid,
            in_specs=in_specs,
            out_specs=out_specs,
            scratch_shapes=scratch,
        ),
        out_shape=out_shape,
        compiler_params=pltpu.CompilerParams(
            vmem_limit_bytes=vmem_limit, dimension_semantics=("arbitrary",) * len(grid)
        ),
        cost_estimate=pl.CostEstimate(
            flops=int(flops * 0.02), bytes_accessed=int(flops * 0.02 / 400), transcendentals=0
        ),
        name=name,
    )(meta, *operands)


def norm_kernel(batch_bits, shard_rows, seq_size, meta, x_ref, extra_ref, out_ref, perm_ref):
    width = x_ref.shape[2]
    chan = out_ref.shape[-1]

    @pl.when(pl.program_id(0) == 0)
    def _():
        lane = lax.broadcasted_iota(jnp.int32, (width, width), 1)
        piece = (lane & (chan - 1)) // shard_rows
        source = (
            (reverse_bits(piece, batch_bits) ^ meta[0]) * seq_size + lane // chan
        ) * shard_rows + (lane & (shard_rows - 1))
        row = lax.broadcasted_iota(jnp.int32, (width, width), 0)
        perm_ref[...] = jnp.where(row == source, 1.0, 0.0).astype(bf16)
        for d in range(out_ref.shape[0]):
            out_ref[d, pl.ds(out_ref.shape[1] - 16, 16), :] = extra_ref[...]

    span = x_ref.shape[1]
    rows = pl.ds(pl.multiple_of(pl.program_id(0) * span, span), span)
    normed, _ = layer_stats(x_ref[0].astype(f32))
    spread = dot(normed.astype(bf16), perm_ref[...]).astype(bf16)
    for d in range(out_ref.shape[0]):
        out_ref[d, rows, :] = spread[:, d * chan : (d + 1) * chan]


def norm_call(meta, x, extra, batch_bits, shard_rows, parts):
    micro, span, width = x.shape
    chan = width // parts
    return call(
        functools.partial(norm_kernel, batch_bits, shard_rows, parts),
        (micro,),
        meta,
        [pl.BlockSpec((1, span, width), lambda m, _: (m, 0, 0))]
        + [full_spec(extra.shape)],
        (x, extra),
        [full_spec((parts, micro * span + 16, chan)), full_spec((width, width))],
        [
            jax.ShapeDtypeStruct((parts, micro * span + 16, chan), bf16),
            jax.ShapeDtypeStruct((width, width), bf16),
        ],
        [],
        2 * micro * span * width * width,
        "norm_one",
    )


def kernel_kernel(meta, lift_re, lift_im, near_re, near_im, fwd_ref, out_ref, series, spec):
    modes, span_near, chan = near_re.shape
    far_count = lift_re.shape[1]
    blocks, _, span, _ = out_ref.shape
    group = 2

    def far_group(index, carry):
        def one_mode(n, acc):
            near_r, near_i = near_re[n], near_im[n]
            result = []
            for g in range(group):
                row = index * group + g
                a = lift_re[n, pl.ds(row, 1), :]
                b = lift_im[n, pl.ds(row, 1), :]
                result.append(acc[g] + (a * near_r - b * near_i))
            return tuple(result)

        zero = jnp.zeros((span_near, chan), f32)
        acc = lax.fori_loop(0, modes, one_mode, (zero,) * group, unroll=4)
        for g in range(group):
            start = pl.multiple_of((index * group + g) * span_near, span_near)
            series[pl.ds(start, span_near), :] = acc[g]
        return carry

    lax.fori_loop(0, far_count // group, far_group, 0)

    def one_pair(index):
        first = index * 2 * span
        pair = [series[pl.ds(first + k * span, span), :] for k in range(2)]
        both = dot(fwd_ref[...], stack_split(jnp.concatenate(pair, axis=1)))
        for k in range(2):
            spec[index * 2 + k] = both[:, k * chan : (k + 1) * chan]

    loop(blocks // 2, one_pair)
    rows = lax.broadcasted_iota(jnp.int32, (span, chan), 0)
    sign = 1.0 - 2.0 * (rows & 1).astype(f32)

    def one_block(d):
        real, imag = spec[d, :span], spec[d, span:]
        before = d - 1 if isinstance(d, int) else jnp.maximum(d - 1, 0)
        if isinstance(d, int) and d == 0:
            out_ref[0, 0], out_ref[0, 1] = real, imag
            return
        keep = 1.0 if isinstance(d, int) else jnp.where(d > 0, 1.0, 0.0)
        out_ref[d, 0] = real - keep * (sign * spec[before, span:])
        out_ref[d, 1] = imag + keep * (sign * spec[before, :span])

    loop(blocks, one_block)


def kernel_call(meta, lift, near, fwd, blocks, span):
    chan = near[0].shape[-1]
    operands = (lift[0], lift[1], near[0], near[1], fwd)
    return call(
        kernel_kernel,
        (1,),
        meta,
        [full_spec(a.shape) for a in operands],
        operands,
        full_spec((blocks, 2, span, chan)),
        jax.ShapeDtypeStruct((blocks, 2, span, chan), f32),
        [pltpu.VMEM((blocks * span, chan), f32), pltpu.VMEM((blocks, 2 * span, chan), f32)],
        1.1e10,
        "state_kernel",
    )


def mask_of(meta, m, block, span, chan):
    rows = block * span + lax.broadcasted_iota(jnp.int32, (span, chan), 0)
    return (rows < meta[1 + m]).astype(f32)


freq_tile = 64


def conv_kernel(
    meta,
    normed_ref,
    vec_ref,
    spec_ref,
    fwd_ref,
    inv_ref,
    drive_ref,
    mixed_ref,
    out_ref,
    drive,
    spectrum,
):
    m = pl.program_id(0)
    blocks, span, chan = drive.shape
    gain, bias, skip = vec_ref[0:1, :], vec_ref[1:2, :], vec_ref[2:3, :]

    def drive_pair(pair):
        values = []
        for k in range(2):
            block = 2 * pair + k
            normed = normed_ref[block].astype(f32)
            u = mask_of(meta, m, block, span, chan) * (normed * gain + bias)
            drive[block] = u
            values.append(u)
        both = dot(fwd_ref[...], stack_split(jnp.concatenate(values, axis=1)))
        for k in range(2):
            drive_ref[0, 2 * pair + k] = both[:, k * chan : (k + 1) * chan]

    loop(blocks // 2, drive_pair)

    def one_pair(index):
        for k in range(2):
            i = index * 2 + k

            def one_tile(tile, carry):
                low = pl.ds(pl.multiple_of(tile * freq_tile, freq_tile), freq_tile)
                high = pl.ds(pl.multiple_of(span + tile * freq_tile, freq_tile), freq_tile)

                def one_term(j, acc):
                    xr, xi = drive_ref[0, j, low], drive_ref[0, j, high]
                    gr, gi = spec_ref[i - j, 0, low], spec_ref[i - j, 1, low]
                    return (acc[0] + (xr * gr - xi * gi), acc[1] + (xr * gi + xi * gr))

                zero = jnp.zeros((freq_tile, chan), f32)
                acc = sum_loop(0, i + 1, one_term, (zero, zero))
                spectrum[k, low] = acc[0]
                spectrum[k, high] = acc[1]
                return carry

            lax.fori_loop(0, span // freq_tile, one_tile, 0, unroll=True)
        both = dot(
            inv_ref[...], stack_split(jnp.concatenate([spectrum[0], spectrum[1]], axis=1))
        )
        for k in range(2):
            i = index * 2 + k
            mixed = both[:, k * chan : (k + 1) * chan] + skip * drive[i]
            mixed_ref[0, i] = mixed
            out_ref[i] = gelu_value(mixed).astype(bf16)

    loop(blocks // 2, one_pair)


def conv_call(meta, micro, normed, vec, spec, fwd, inv):
    parts, _, chan = normed.shape
    span = spec.shape[2]
    wide = lambda rows: pl.BlockSpec((1, parts, rows, chan), lambda m, _: (m, 0, 0, 0))
    return call(
        conv_kernel,
        (micro,),
        meta,
        [parted(parts, span, chan)] + [full_spec(a.shape) for a in (vec, spec, fwd, inv)],
        (normed, vec, spec, fwd, inv),
        [wide(2 * span), wide(span), parted(parts, span, chan)],
        [
            jax.ShapeDtypeStruct((micro, parts, 2 * span, chan), f32),
            jax.ShapeDtypeStruct((micro, parts, span, chan), f32),
            jax.ShapeDtypeStruct((parts, micro * span, chan), bf16),
        ],
        [
            pltpu.VMEM((parts, span, chan), f32),
            pltpu.VMEM((2, 2 * span, chan), f32),
        ],
        1.5e10,
        "state_conv",
    )


def back_kernel(
    meta,
    grads_ref,
    normed_ref,
    drive_ref,
    mixed_ref,
    vec_ref,
    spec_ref,
    fwd_ref,
    inv_ref,
    extra_ref,
    out_ref,
    cross_ref,
    sums_ref,
    grad_mixed,
    grad_spec,
    spectrum,
):
    m = pl.program_id(0)
    blocks, span, chan = grad_mixed.shape
    gain, bias, skip = vec_ref[0:1, :], vec_ref[1:2, :], vec_ref[2:3, :]

    @pl.when(m == 0)
    def _():
        cross_ref[...] = jnp.zeros_like(cross_ref)
        sums_ref[...] = jnp.zeros_like(sums_ref)
        extra = extra_ref.shape[1]
        out_ref[:, pl.ds(out_ref.shape[1] - extra, extra), :] = extra_ref[...]

    def grad_pair(pair):
        values = []
        for k in range(2):
            block = 2 * pair + k
            normed = normed_ref[block].astype(f32)
            u = mask_of(meta, m, block, span, chan) * (normed * gain + bias)
            gm = grads_ref[block].astype(f32) * gelu_slope(mixed_ref[0, block])
            sums_ref[0:1, :] += jnp.sum(gm * u, axis=0, keepdims=True)
            grad_mixed[block] = gm
            values.append(gm)
        both = dot(fwd_ref[...], stack_split(jnp.concatenate(values, axis=1)))
        for k in range(2):
            grad_spec[2 * pair + k] = both[:, k * chan : (k + 1) * chan]

    loop(blocks // 2, grad_pair)

    def tiles_of(body):
        def one_tile(tile, carry):
            low = pl.ds(pl.multiple_of(tile * freq_tile, freq_tile), freq_tile)
            high = pl.ds(pl.multiple_of(span + tile * freq_tile, freq_tile), freq_tile)
            body(low, high)
            return carry

        lax.fori_loop(0, span // freq_tile, one_tile, 0, unroll=True)

    zero = jnp.zeros((freq_tile, chan), f32)

    def one_pair(index):
        for k in range(2):
            j = index * 2 + k

            def body(low, high):
                def one_term(i, acc):
                    mr, mi = grad_spec[i, low], grad_spec[i, high]
                    gr, gi = spec_ref[i - j, 0, low], spec_ref[i - j, 1, low]
                    return (acc[0] + (mr * gr + mi * gi), acc[1] + (mi * gr - mr * gi))

                acc = sum_loop(j, blocks, one_term, (zero, zero))
                spectrum[k, low] = acc[0]
                spectrum[k, high] = acc[1]

            tiles_of(body)
        both = dot(
            inv_ref[...], stack_split(jnp.concatenate([spectrum[0], spectrum[1]], axis=1))
        )
        for k in range(2):
            j = index * 2 + k
            grad_mixed[j] = both[:, k * chan : (k + 1) * chan] + skip * grad_mixed[j]

    loop(blocks // 2, one_pair)

    def finish(block):
        g = mask_of(meta, m, block, span, chan) * grad_mixed[block]
        normed = normed_ref[block].astype(f32)
        sums_ref[1:2, :] += jnp.sum(g * normed, axis=0, keepdims=True)
        sums_ref[2:3, :] += jnp.sum(g, axis=0, keepdims=True)
        out_ref[block, pl.ds(pl.multiple_of(m * span, span), span), :] = (g * gain).astype(bf16)

    loop(blocks, finish)

    def one_lag(d):
        def body(low, high):
            def one_term(j, acc):
                mr, mi = grad_spec[j + d, low], grad_spec[j + d, high]
                xr, xi = drive_ref[0, j, low], drive_ref[0, j, high]
                return (acc[0] + (mr * xr + mi * xi), acc[1] + (mi * xr - mr * xi))

            acc = sum_loop(0, blocks - d, one_term, (cross_ref[d, low], cross_ref[d, high]))
            cross_ref[d, low] = acc[0]
            cross_ref[d, high] = acc[1]

        tiles_of(body)

    loop(blocks, one_lag)


def back_call(meta, grads, normed, drive, mixed, vec, spec, fwd, inv, extra):
    parts, _, chan = normed.shape
    micro, _, span, _ = mixed.shape
    total = micro * span + extra.shape[1]
    mode = None if parts <= 8 else pl.Buffered(1)
    wide = lambda rows: pl.BlockSpec(
        (1, parts, rows, chan), lambda m, _: (m, 0, 0, 0), pipeline_mode=mode
    )
    return call(
        back_kernel,
        (micro,),
        meta,
        [parted(parts, span, chan)] * 2
        + [wide(2 * span), wide(span)]
        + [full_spec(a.shape) for a in (vec, spec, fwd, inv, extra)],
        (grads, normed, drive, mixed, vec, spec, fwd, inv, extra),
        [
            full_spec((parts, total, chan)),
            full_spec((parts, 2 * span, chan)),
            full_spec((8, chan)),
        ],
        [
            jax.ShapeDtypeStruct((parts, total, chan), bf16),
            jax.ShapeDtypeStruct((parts, 2 * span, chan), f32),
            jax.ShapeDtypeStruct((8, chan), f32),
        ],
        [
            pltpu.VMEM((parts, span, chan), f32),
            pltpu.VMEM((parts, 2 * span, chan), f32),
            pltpu.VMEM((2, 2 * span, chan), f32),
        ],
        2e10,
        "state_back",
    )


def modes_kernel(meta, cross_ref, far_re, far_im, near_re, near_im, inv_ref, out_ref, series):
    modes, span_near, chan = near_re.shape
    far_count = far_re.shape[1]
    blocks, double, _ = cross_ref.shape
    span = double // 2
    rows = lax.broadcasted_iota(jnp.int32, (span, chan), 0)
    sign = 1.0 - 2.0 * (rows & 1).astype(f32)

    def one_pair(index):
        pair = []
        for k in range(2):
            d = index * 2 + k
            real, imag = cross_ref[d, :span], cross_ref[d, span:]
            if isinstance(d, int):
                keep = 1.0 if d + 1 < blocks else 0.0
                after = min(d + 1, blocks - 1)
            else:
                keep = jnp.where(d + 1 < blocks, 1.0, 0.0)
                after = jnp.minimum(d + 1, blocks - 1)
            real = real + keep * (sign * cross_ref[after, span:])
            imag = imag - keep * (sign * cross_ref[after, :span])
            pair.append(jnp.concatenate([real, imag], axis=0))
        both = dot(inv_ref[...], stack_split(jnp.concatenate(pair, axis=1)))
        for k in range(2):
            series[pl.ds((index * 2 + k) * span, span), :] = both[:, k * chan : (k + 1) * chan]

    loop(blocks // 2, one_pair)
    group = 2

    def mode_group(index, carry):
        def one_far(i, acc):
            values = series[pl.ds(pl.multiple_of(i * span_near, span_near), span_near), :]
            result = []
            for g in range(group):
                n = index * group + g
                a = far_re[n, pl.ds(i, 1), :]
                b = far_im[n, pl.ds(i, 1), :]
                result.append((acc[g][0] + a * values, acc[g][1] + b * values))
            return tuple(result)

        zero = jnp.zeros((span_near, chan), f32)
        acc = lax.fori_loop(0, far_count, one_far, ((zero, zero),) * group, unroll=4)
        for g in range(group):
            n = index * group + g
            near_r, near_i = near_re[n], near_im[n]
            re, im = acc[g]
            out_ref[0, pl.ds(n, 1), :] = jnp.sum(re * near_r - im * near_i, axis=0, keepdims=True)
            out_ref[1, pl.ds(n, 1), :] = jnp.sum(re * near_i + im * near_r, axis=0, keepdims=True)
        return carry

    lax.fori_loop(0, modes // group, mode_group, 0)


def modes_call(meta, cross, far, near, inv):
    modes, _, chan = near[0].shape
    blocks, double, _ = cross.shape
    operands = (cross, far[0], far[1], near[0], near[1], inv)
    return call(
        modes_kernel,
        (1,),
        meta,
        [full_spec(a.shape) for a in operands],
        operands,
        full_spec((2, modes, chan)),
        jax.ShapeDtypeStruct((2, modes, chan), f32),
        [pltpu.VMEM((blocks * double // 2, chan), f32)],
        1.1e10,
        "state_modes",
    )


class Rows:
    def __init__(self, width, shard_rows, seq_size, batch_size, table, by_channel=False):
        self.width = width
        self.shard_rows = shard_rows
        self.seq_size = seq_size
        self.batch_size = batch_size
        self.table = table
        self.piece_rows = shard_rows * seq_size
        self.by_block = shard_rows % 16 == 0
        self.by_channel = by_channel

    def natural(self, meta, p, q):
        start = meta[self.table + p * self.seq_size + q] * self.shard_rows
        return pl.ds(pl.multiple_of(start, self.shard_rows), self.shard_rows)

    def order(self, meta, place):
        shape = (self.width, self.width)
        relative = lax.broadcasted_iota(jnp.int32, shape, 0)
        piece = relative // self.piece_rows
        position = (relative % self.piece_rows) // self.shard_rows
        seq = reverse_bits(position, bits_of(self.seq_size)) ^ meta[0]
        if self.by_channel:
            shard = seq * self.batch_size + piece
        else:
            batch = reverse_bits(piece, bits_of(self.batch_size)) ^ meta[place + 1]
            shard = batch * self.seq_size + seq
        source = shard * self.shard_rows + relative % self.shard_rows
        return jnp.where(lax.broadcasted_iota(jnp.int32, shape, 1) == source, 1.0, 0.0).astype(bf16)

    def to_natural(self, meta, place, parts, target):
        if self.by_block:
            for p, part in enumerate(parts):
                for q in range(self.seq_size):
                    target[self.natural(meta, p, q), :] = part[
                        pl.ds(q * self.shard_rows, self.shard_rows), :
                    ]
        else:
            whole = jnp.concatenate([part[...] for part in parts], axis=0)
            target[...] = dot_left_t(self.order(meta, place), whole).astype(bf16)

    def to_relative(self, meta, place, value, scratch, store):
        if self.by_block:
            scratch[...] = value.astype(bf16)
        else:
            moved = dot(self.order(meta, place), value.astype(bf16))
        for p in range(self.batch_size):
            for q in range(self.seq_size):
                if self.by_block:
                    block = scratch[self.natural(meta, p, q), :]
                else:
                    start = (p * self.seq_size + q) * self.shard_rows
                    block = moved[start : start + self.shard_rows].astype(bf16)
                store(p, q, block)


def gate_kernel(pieces, order, meta, *refs):
    active_ref, x_ref, cot_ref, vec_ref, glu_bias_ref = refs[:5]
    weights = refs[5 : 5 + pieces]
    act_ref, resid_ref, gated_ref, norm_ref, norm_t_ref, cot_out, weight_scr = refs[5 + pieces :]
    m = pl.program_id(0)
    _, span, width = x_ref.shape
    micro = pl.num_programs(0)

    @pl.when(m == 0)
    def _():
        order.to_natural(meta, 1 + micro, weights, weight_scr)

    act = jnp.concatenate([active_ref[d] for d in range(active_ref.shape[0])], axis=1)
    act_ref[...] = act
    gated = dot(act, weight_scr[...]) + glu_bias_ref[...]
    gated_ref[0] = gated
    residual = x_ref[0].astype(f32) + gated[:, :width] * jax.nn.sigmoid(gated[:, width:])
    resid_ref[0] = residual
    normed, _ = layer_stats(residual)
    norm_two = (normed * vec_ref[0:1, :] + vec_ref[1:2, :]).astype(bf16)
    norm_ref[...] = norm_two
    norm_t_ref[...] = norm_two.T
    rows = meta[1 + micro] + lax.broadcasted_iota(jnp.int32, (span, width), 0)
    cot_out[...] = jnp.where(rows < meta[1 + m], cot_ref[0].astype(f32), 0.0).astype(bf16)


def gate_call(meta, order, active, x, cot, vec, glu_bias, weights):
    parts, _, chan = active.shape
    pieces = len(weights)
    micro, span, width = x.shape
    tokens = micro * span
    tile = lambda cols: pl.BlockSpec((1, span, cols), lambda m, _: (m, 0, 0))
    flat = pl.BlockSpec((span, width), lambda m, _: (m, 0))
    return call(
        functools.partial(gate_kernel, pieces, order),
        (micro,),
        meta,
        [parted(parts, span, chan), tile(width), tile(width)]
        + [full_spec(a.shape) for a in (vec, glu_bias, *weights)],
        (active, x, cot, vec, glu_bias, *weights),
        [
            flat,
            tile(width),
            tile(2 * width),
            flat,
            pl.BlockSpec((width, span), lambda m, _: (0, m)),
            flat,
        ],
        [
            jax.ShapeDtypeStruct((tokens, width), bf16),
            jax.ShapeDtypeStruct((micro, span, width), f32),
            jax.ShapeDtypeStruct((micro, span, 2 * width), f32),
            jax.ShapeDtypeStruct((tokens, width), bf16),
            jax.ShapeDtypeStruct((width, tokens), bf16),
            jax.ShapeDtypeStruct((tokens, width), bf16),
        ],
        [pltpu.VMEM((width, 2 * width), bf16)],
        6 * tokens * width * width,
        "gated_unit",
    )


def ff_block_of(piece_ff):
    return min(1024, piece_ff)


def ffn_kernel(pieces, batch_pieces, sub, order, out_table, place, first, second, meta, *refs):
    refs = list(refs)
    take = lambda count: [refs.pop(0) for _ in range(count)]
    half = batch_pieces // 2
    (cot_ref,) = take(1)
    w_out = take(pieces)
    if first:
        norm_ref, bias_ref = take(2)
        w_in = take(batch_pieces)
    else:
        spread_ref, hidden_ref = take(2)
    if second:
        (norm_t_ref,) = take(1)
    if first:
        back_ref, grad_bias = take(2)
        if not second:
            spread_ref, hidden_ref = take(2)
    if second:
        (out_ref,) = take(1)
        grad_out, grad_in = take(pieces), take(half)
        (grad_in_send,) = take(1)
    (out_scr,) = take(1)
    if first:
        (in_scr,) = take(1)
    if second:
        (grad_in_scr,) = take(1)
    k = pl.program_id(0)
    s = pl.program_id(1)
    ff_block = out_scr.shape[0]
    subs = ff_block // sub
    start = jnp.logical_and(k == 0, s == 0)

    def sub_rows(t):
        return pl.ds(pl.multiple_of(meta[out_table + s * subs + t] * sub, sub), sub)

    for piece in range(pieces):

        @pl.when(k == piece)
        def _():
            for t in range(subs):
                out_scr[pl.ds(t * sub, sub), :] = w_out[piece][sub_rows(t), :]

    def accumulate(ref, part):
        @pl.when(start)
        def _():
            ref[...] = part

        @pl.when(jnp.logical_not(start))
        def _():
            ref[...] += part

    if first:
        order.to_natural(meta, place, w_in, in_scr)
        hidden = dot(norm_ref[...], in_scr[...]) + bias_ref[0]
        spread, slope = gelu_both(hidden)
        spread = spread.astype(bf16)
        grad_hidden = (dot_right_t(cot_ref[...], out_scr[...]) * slope).astype(bf16)
        grad_bias[0] = jnp.sum(grad_hidden.astype(f32), axis=0, keepdims=True)
        if not second:
            spread_ref[...] = spread
            hidden_ref[...] = grad_hidden
        accumulate(back_ref, dot_right_t(grad_hidden, in_scr[...]))
    else:
        spread, grad_hidden = spread_ref[...], hidden_ref[...]

    if second:
        accumulate(out_ref, dot(spread, out_scr[...]))

        def store(p, q, block):
            if p < half:
                grad_in[p][q, 0] = block
            else:
                grad_in_send[p - half, q, 0] = block

        order.to_relative(meta, place, dot(norm_t_ref[...], grad_hidden), grad_in_scr, store)
        part = dot_left_t(spread, cot_ref[...]).astype(bf16)
        for piece in range(pieces):

            @pl.when(k == piece)
            def _():
                for t in range(subs):
                    grad_out[piece][sub_rows(t), :] = part[t * sub : (t + 1) * sub, :]


def ffn_call(meta, order, out_table, place, base, column, cot, w_out, norm=None, bias=None, w_in=None, norm_t=None, kept=None):
    first, second = norm is not None, norm_t is not None
    pieces, batch_pieces = len(w_out), order.batch_size
    tokens, width = cot.shape
    piece_ff = w_out[0].shape[0]
    ff_block = ff_block_of(piece_ff)
    steps = piece_ff // ff_block
    sub = piece_ff // order.seq_size
    rows = order.piece_rows
    half = batch_pieces // 2
    seq_size, low = order.seq_size, order.shard_rows
    block = lambda k, s, meta: meta[base + k] + s
    wide = full_spec((tokens, width))
    step_columns = pl.BlockSpec((tokens, ff_block), lambda k, s, meta: (0, k * steps + s))
    activations = jax.ShapeDtypeStruct((tokens, pieces * piece_ff), bf16)
    total = jax.ShapeDtypeStruct((tokens, width), f32)
    operands = [cot, *w_out]
    in_specs = [wide] + [full_spec(a.shape) for a in w_out]
    outs, out_specs, scratch = [], [], [pltpu.VMEM((ff_block, width), bf16)]
    if first:
        operands += [norm, bias, *w_in]
        in_specs += [wide]
        in_specs += [pl.BlockSpec((1, 1, ff_block), lambda k, s, meta: (block(k, s, meta), 0, 0))]
        in_specs += [
            pl.BlockSpec((rows, ff_block), lambda k, s, meta: (0, block(k, s, meta)))
            for _ in w_in
        ]
        outs += [total, jax.ShapeDtypeStruct((pieces * steps, 1, ff_block), f32)]
        out_specs += [wide]
        out_specs += [
            pl.BlockSpec((1, 1, ff_block), lambda k, s, meta: (meta[column + k] * steps + s, 0, 0))
        ]
        scratch += [pltpu.VMEM((width, ff_block), bf16)]
        if not second:
            outs += [activations] * 2
            out_specs += [step_columns] * 2
    else:
        operands += kept
        in_specs += [step_columns] * 2
    if second:
        operands += [norm_t]
        in_specs += [full_spec(norm_t.shape)]
        outs += [total] + [jax.ShapeDtypeStruct(a.shape, bf16) for a in w_out]
        outs += [jax.ShapeDtypeStruct((seq_size, pieces, low, piece_ff), bf16)] * half
        outs += [jax.ShapeDtypeStruct((half, seq_size, pieces, low, piece_ff), bf16)]
        out_specs += [wide] + [full_spec(a.shape) for a in w_out]
        out_specs += [
            pl.BlockSpec((seq_size, 1, low, ff_block), lambda k, s, meta: (0, meta[column + k], 0, s))
        ] * half
        out_specs += [
            pl.BlockSpec(
                (half, seq_size, 1, low, ff_block),
                lambda k, s, meta: (0, 0, meta[column + k], 0, s),
            )
        ]
        scratch += [pltpu.VMEM((width, ff_block), bf16)]
    results = call(
        functools.partial(
            ffn_kernel, pieces, batch_pieces, sub, order, out_table, place, first, second
        ),
        (pieces, steps),
        meta,
        in_specs,
        operands,
        out_specs,
        outs,
        scratch,
        6 * (first + second) * tokens * width * piece_ff * pieces,
        "feed_forward",
    )
    head = results[: 2 * first + 2 * (first and not second)]
    tail = results[len(head) :]
    return head, tail[:1], tail[1 : 1 + pieces], tail[1 + pieces : -1], tail[-1:]


def gate_back_kernel(pieces, halves, order, meta, *refs):
    back = refs[:halves]
    resid_ref, gated_ref, cot_ref, vec_ref = refs[halves : halves + 4]
    weights = refs[halves + 4 : halves + 4 + pieces]
    rest = refs[halves + 4 + pieces :]
    grad_resid_ref, grad_gated_ref, glu_bias_ref, sums_ref, moved_ref, weight_scr = rest
    m = pl.program_id(0)
    count = pl.num_programs(0)
    width = cot_ref.shape[1]

    @pl.when(m == 0)
    def _():
        glu_bias_ref[...] = jnp.zeros_like(glu_bias_ref)
        sums_ref[...] = jnp.zeros_like(sums_ref)
        order.to_natural(meta, 1 + count, weights, weight_scr)

    residual = resid_ref[0]
    grad_norm = back[0][...]
    for h in range(1, halves):
        grad_norm = grad_norm + back[h][...]
    grad_out = cot_ref[...].astype(f32)
    normed, scale = layer_stats(residual)
    sums_ref[0:1, :] += jnp.sum(grad_out, axis=0, keepdims=True)
    sums_ref[1:2, :] += jnp.sum(grad_norm * normed, axis=0, keepdims=True)
    sums_ref[2:3, :] += jnp.sum(grad_norm, axis=0, keepdims=True)
    grad_resid = grad_out + norm_back(grad_norm * vec_ref[0:1, :], normed, scale)
    grad_resid_ref[0] = grad_resid
    gated = gated_ref[0]
    gate = jax.nn.sigmoid(gated[:, width:])
    grad_left = grad_resid * gate
    grad_right = grad_left * gated[:, :width] * (1.0 - gate)
    grad_gated = jnp.concatenate([grad_left, grad_right], axis=1).astype(bf16)
    grad_gated_ref[...] = grad_gated
    glu_bias_ref[0:1, :] += jnp.sum(grad_gated.astype(f32), axis=0, keepdims=True)
    moved = dot_right_t(grad_gated, weight_scr[...]).astype(bf16)
    chan = moved_ref.shape[-1]
    for d in range(moved_ref.shape[0]):
        moved_ref[d] = moved[:, d * chan : (d + 1) * chan]


def gate_back_call(meta, order, parts, back, resid, gated, cot, vec, weights):
    halves, pieces = len(back), len(weights)
    micro, span, width = resid.shape
    tokens = micro * span
    chan = width // parts
    tile = lambda cols: pl.BlockSpec((1, span, cols), lambda m, _: (m, 0, 0))
    flat = lambda cols: pl.BlockSpec((span, cols), lambda m, _: (m, 0))
    return call(
        functools.partial(gate_back_kernel, pieces, halves, order),
        (micro,),
        meta,
        [flat(width)] * halves
        + [tile(width), tile(2 * width), flat(width)]
        + [full_spec(a.shape) for a in (vec, *weights)],
        (*back, resid, gated, cot, vec, *weights),
        [
            tile(width),
            flat(2 * width),
            full_spec((8, 2 * width)),
            full_spec((8, width)),
            parted(parts, span, chan),
        ],
        [
            jax.ShapeDtypeStruct((micro, span, width), f32),
            jax.ShapeDtypeStruct((tokens, 2 * width), bf16),
            jax.ShapeDtypeStruct((8, 2 * width), f32),
            jax.ShapeDtypeStruct((8, width), f32),
            jax.ShapeDtypeStruct((parts, micro * span, chan), bf16),
        ],
        [pltpu.VMEM((width, 2 * width), bf16)],
        4 * tokens * width * width,
        "gated_back",
    )


def gate_weight_kernel(pieces, order, place, meta, act_ref, grad_ref, *refs):
    grad_keep, grad_send, scratch = refs[: pieces // 2], refs[-2], refs[-1]

    def store(p, q, block):
        if p < pieces // 2:
            grad_keep[p][q] = block
        else:
            grad_send[p - pieces // 2, q] = block

    order.to_relative(meta, place, dot_left_t(act_ref[...], grad_ref[...]), scratch, store)


def gate_weight_call(meta, order, place, act, grad_gated):
    tokens, width = act.shape
    pieces, parts, low = order.batch_size, order.seq_size, order.shard_rows
    cols = width // 2
    outs = call(
        functools.partial(gate_weight_kernel, pieces, order, place),
        (4,),
        meta,
        [full_spec(act.shape), pl.BlockSpec((tokens, cols), lambda c, _: (0, c))],
        (act, grad_gated),
        [pl.BlockSpec((parts, low, cols), lambda c, _: (0, 0, c))] * (pieces // 2)
        + [pl.BlockSpec((pieces // 2, parts, low, cols), lambda c, _: (0, 0, 0, c))],
        [jax.ShapeDtypeStruct((parts, low, 2 * width), bf16)] * (pieces // 2)
        + [jax.ShapeDtypeStruct((pieces // 2, parts, low, 2 * width), bf16)],
        [pltpu.VMEM((width, cols), bf16)],
        4 * tokens * width * width,
        "gated_weight",
    )
    return outs[:-1], outs[-1]


def input_kernel(meta, moved_ref, x_ref, grad_resid_ref, perm_ref, out_ref):
    e = jnp.concatenate([moved_ref[d] for d in range(moved_ref.shape[0])], axis=1)
    e = dot_right_t(e, perm_ref[...])
    normed, scale = layer_stats(x_ref[0].astype(f32))
    out_ref[0] = (grad_resid_ref[0] + norm_back(e, normed, scale)).astype(bf16)


def input_call(meta, moved, x, grad_resid, perm):
    parts, _, chan = moved.shape
    micro, span, width = x.shape
    tile = lambda cols: pl.BlockSpec((1, span, cols), lambda m, _: (m, 0, 0))
    return call(
        input_kernel,
        (micro,),
        meta,
        [parted(parts, span, chan), tile(width), tile(width), full_spec(perm.shape)],
        (moved, x, grad_resid, perm),
        tile(width),
        jax.ShapeDtypeStruct((micro, span, width), bf16),
        [],
        2 * micro * span * width * width,
        "input_grad",
    )


def mode_tables(step_len, mode_count, length):
    order = jnp.arange(mode_count, dtype=f32)[:, None]
    rate = order * step_len

    def power(offsets):
        turns = 0.5 * rate[:, None, :] * offsets[None, :, None]
        angle = 2.0 * math.pi * (turns - jnp.round(turns))
        fading = jnp.exp(-0.5 * step_len[:, None, :] * offsets[None, :, None])
        return fading * jnp.cos(angle), fading * jnp.sin(angle)

    def outer(far, near):
        a, b = far[0][:, :, None], far[1][:, :, None]
        c, d = near[0][:, None], near[1][:, None]
        shape = (mode_count, far[0].shape[1] * near[0].shape[1], step_len.shape[-1])
        return (a * c - b * d).reshape(shape), (a * d + b * c).reshape(shape)

    ramp = jnp.arange(8, dtype=f32)
    near = outer(power(8.0 * ramp), power(ramp))
    far_count = length // near_span
    far = outer(
        power(8.0 * near_span * jnp.arange(far_count // 8, dtype=f32)), power(near_span * ramp)
    )

    def wave(scale):
        turns = scale * rate
        return 2.0 * math.pi * (turns - jnp.round(turns))

    decay = -0.5 * step_len
    turn_rate = math.pi * order
    step_im = jnp.exp(decay) * jnp.sin(wave(0.5))
    minus_one = jnp.expm1(decay) * jnp.cos(wave(0.5)) - 2.0 * jnp.sin(wave(0.25)) ** 2
    denominator = 0.25 + turn_rate**2
    input_mult = (
        (-0.5 * minus_one + step_im * turn_rate) / denominator,
        (-0.5 * step_im - minus_one * turn_rate) / denominator,
    )
    return near, far, input_mult


def cmul(a, b):
    return a[0] * b[0] - a[1] * b[1], a[0] * b[1] + a[1] * b[0]


def per_device(
    inputs,
    lengths,
    cotangent,
    norm1_gain,
    norm1_bias,
    step_size,
    state_out,
    skip_gain,
    glu_weight,
    glu_bias,
    norm2_gain,
    norm2_bias,
    ffn_in_weight,
    ffn_in_bias,
    ffn_out_weight,
    ffn_out_bias,
):
    micro, _, span, width = inputs.shape
    batch_size, seq_size = lax.axis_size("batch"), lax.axis_size("seq")
    batch_bits, seq_bits = bits_of(batch_size), bits_of(seq_size)
    devices = batch_size * seq_size
    shard_rows = width // devices
    chan = width // seq_size
    length = span * seq_size
    mode_count = state_out.shape[2]
    ff = ffn_in_weight.shape[1]
    me_b, me_s = lax.axis_index("batch"), lax.axis_index("seq")
    me = me_b * seq_size + me_s

    piece_ff = ff // batch_size
    place_at = 1 + micro
    in_table = 8
    out_table = in_table + devices
    base_table = out_table + seq_size
    column_table = base_table + batch_size
    chan_table = column_table + batch_size
    pieces = np.arange(batch_size)
    natural_piece = reverse_bits(pieces, batch_bits) ^ me_b
    piece_of = reverse_bits(jnp.arange(batch_size, dtype=jnp.int32) ^ me_b, batch_bits)

    def meta_of(parts):
        lengths, me_b, me_s = parts
        place = np.arange(devices)
        of_piece = reverse_bits(place // seq_size, batch_bits) ^ me_b
        of_seq = reverse_bits(place % seq_size, seq_bits) ^ me_s
        halves = np.concatenate([pieces[pieces % 2 == 0], pieces[pieces % 2 == 1]])
        of_group = reverse_bits(halves, batch_bits) ^ me_b
        table = jnp.concatenate(
            [
                of_piece * seq_size + of_seq,
                reverse_bits(np.arange(seq_size) ^ me_s, seq_bits),
                of_group * (piece_ff // ff_block_of(piece_ff)),
                of_group & (batch_size // 2 - 1),
                of_seq * batch_size + place // seq_size,
            ]
        )
        head = jnp.stack([me_s, *lengths[:, 0], me_s * span, me_b])
        blank = jnp.zeros((8 - head.shape[0],), jnp.int32)
        return jnp.concatenate([head, blank, table]).astype(jnp.int32)

    order = Rows(width, shard_rows, seq_size, batch_size, in_table)
    chan_order = Rows(width, shard_rows, seq_size, batch_size, chan_table, by_channel=True)

    x = inputs[:, 0]
    cot = cotangent[:, 0]

    top = batch_bits - 1
    half = batch_size // 2

    def over_low(pieces):
        for bit in reversed(range(top)):
            pieces = pieces + swap_batch(pieces, bit)
        return pieces

    def weave(low, high):
        return [piece for pair in zip(low, high) for piece in pair]

    def join(*parts):
        return jnp.concatenate(parts, axis=0)

    def near_swap(value):
        return swap(value, "seq", 1)

    def middle_swap(value):
        return swap(value, "seq", 2)

    def last_swap(value):
        return swap(value, "seq", seq_size // 2)

    def top_swap(value):
        return swap(value, "batch", 1 << top)

    counts = [2 * shard_rows, shard_rows, shard_rows, shard_rows, 4 * shard_rows]
    starts = [sum(counts[:k]) for k in range(len(counts))]
    small_size = sum(counts)
    in_1 = gather_first(ffn_in_weight)
    vectors = (norm1_gain, norm1_bias, skip_gain, step_size)
    vectors = vectors + (glu_bias, norm2_gain, norm2_bias, ffn_out_bias, ffn_in_bias)
    vectors = jnp.concatenate([v.reshape(-1, shard_rows) for v in vectors], axis=0)
    vectors = jnp.concatenate(gather_batch(vectors), axis=1)
    coefs = gather_batch(state_out)
    normed, perm = norm_call(
        me_b[None].astype(jnp.int32),
        x,
        jnp.pad(vectors[4:], ((0, 20 - vectors.shape[0]), (0, 0))),
        batch_bits,
        shard_rows,
        seq_size,
    )
    normed, in_1, one, coefs = together((normed, in_1, vectors[:4], coefs))
    in_w = gather_more(join(ffn_in_weight[None], in_1), 2)
    in_2 = middle_swap(in_w)
    glu_1 = gather_first(after(glu_weight, in_w))
    meta = meta_of(after((lengths, me_b, me_s), in_w))
    one = one.astype(f32)
    vec_one = jnp.concatenate([one[:3], jnp.zeros((5, chan), f32)], axis=0)
    coefs = jnp.concatenate(coefs, axis=1)
    coefs = jnp.swapaxes(coefs, 1, 2).astype(f32)
    near, far, input_mult = mode_tables(one[3:4], mode_count, length)
    joint = cmul(coefs, input_mult)
    lift = cmul((joint[0][:, None], joint[1][:, None]), far)
    fwd_np, inv_np = transform_tables(span)
    fwd, inv = jnp.asarray(fwd_np), jnp.asarray(inv_np)
    normed, in_2, glu_1, lift, near = together((normed, in_2, glu_1, lift, near))

    normed = exchange(normed)
    in_w = join(in_w, in_2)
    in_3 = near_swap(in_w)
    glu_w = gather_more(join(glu_weight[None], glu_1), 2)
    glu_2 = middle_swap(glu_w)
    spec = kernel_call(meta, after(lift, in_w, glu_w), near, fwd, seq_size, span)
    small_all = normed[:, micro * span :, :].astype(f32)
    small_all = small_all.reshape(seq_size, 16, batch_size, shard_rows)
    small_all = jnp.take(jnp.transpose(small_all, (2, 0, 1, 3)), piece_of, axis=0)
    glu_bias_all, gain_two, bias_two, out_bias, in_bias = [
        small_all[:, :, s : s + c].reshape(-1) for s, c in ((0, 2), (2, 1), (3, 1), (4, 1), (5, 4))
    ]
    vec_two = jnp.concatenate(
        [gain_two[None], bias_two[None], out_bias[None], jnp.zeros((5, width), f32)]
    )
    normed, in_3, glu_2, spec, ffn_out_weight, vec_two, glu_bias_all, in_bias = together(
        (normed, in_3, glu_2, spec, ffn_out_weight, vec_two, glu_bias_all, in_bias)
    )

    in_w = join(in_w, in_3).reshape(-1, ff)
    in_top = top_swap(in_w)
    glu_w = join(glu_w, glu_2)
    glu_3 = near_swap(glu_w)
    out_1 = gather_direct(ffn_out_weight)
    drive_spec, mixed, active_own = conv_call(
        meta, micro, normed, vec_one, after(spec, glu_w, in_w), fwd, inv
    )
    active_own, glu_3, out_1 = together((active_own, glu_3, out_1))

    active = exchange(active_own)
    out_w = gather_more(join(ffn_out_weight[None], *out_1), 1)
    out_3 = near_swap(out_w)
    glu_w = join(glu_w, after(glu_3, out_w)).reshape(-1, 2 * width)
    glu_top = top_swap(after(glu_w, in_top))
    in_parts = weave(over_low([in_w]), over_low([in_top]))
    glu_parts = weave(over_low([glu_w]), over_low([glu_top]))
    active, out_3, glu_parts = together((active, out_3, glu_parts))
    out_w = join(out_w, out_3).reshape(-1, width)
    out_top = top_swap(out_w)
    out_low = over_low([out_w])
    active = after(active, out_w)

    act, resid, gated, norm_two, norm_two_t, cot_out = gate_call(
        meta, chan_order, active, x, cot, vec_two, glu_bias_all[None], glu_parts
    )

    in_bias_blocks = in_bias.reshape(-1, 1, ff_block_of(piece_ff))

    def ffn_half(which, weights, **parts):
        return ffn_call(
            meta,
            order,
            out_table,
            place_at,
            base_table + which * half,
            column_table + which * half,
            cot_out,
            weights,
            **parts,
        )

    def low_rest(values):
        for bit in range(1, top):
            keep, send = values[: len(values) // 2], values[len(values) // 2 :]
            came = swap(jnp.stack([Sum(*v).total().astype(bf16) for v in send]), "batch", 1 << bit)
            values = [v + [came[i]] for i, v in enumerate(keep)]
        return values

    def low_sum(keep, came):
        return low_rest([[v, came[i]] for i, v in enumerate(keep)])

    def out_send(parts):
        return parts[half // 2][None] if half == 2 else jnp.stack(parts[half // 2 :])

    def rounded(terms):
        return Sum(*terms).total().astype(bf16)

    (back_a, bias_a), (out_a,), grad_out_a, keep_in_a, (send_in_a,) = ffn_half(
        0, out_low, norm=norm_two, bias=in_bias_blocks, w_in=in_parts, norm_t=norm_two_t
    )
    out_high = over_low([after(out_top, back_a)])
    in_a_came = swap(send_in_a, "batch", 1)
    out_a_came = swap(out_send(grad_out_a), "batch", 1)
    in_a_own, in_a_other = low_sum(keep_in_a, in_a_came)
    in_a_other = rounded(in_a_other)
    in_b_top = top_swap(in_a_other)
    (back_b, bias_b), (out_b,), grad_out_b, keep_in_b, (send_in_b,) = ffn_half(
        1,
        out_high,
        norm=after(norm_two, back_a, in_a_other),
        bias=in_bias_blocks,
        w_in=in_parts,
        norm_t=norm_two_t,
    )
    back_b, in_b_top, out_a_came = together((back_b, in_b_top, out_a_came))

    grad_resid, grad_gated, grad_glu_bias, sums, moved = gate_back_call(
        meta,
        chan_order,
        seq_size,
        [back_a, back_b],
        resid,
        gated,
        cot_out,
        vec_two,
        glu_parts,
    )
    grad_out_b, send_in_b = after((grad_out_b, send_in_b), moved)
    out_b_came = swap(out_send(grad_out_b), "batch", 1)
    in_b_came = swap(send_in_b, "batch", 1)

    grads_in = exchange(moved)
    (out_b_sum,) = low_sum(grad_out_b[: half // 2], out_b_came)
    out_b_sum = rounded(out_b_sum)
    out_a_top = top_swap(out_b_sum)
    keep_glu, send_glu = gate_weight_call(
        meta, chan_order, place_at, act, after(grad_gated, out_b_sum)
    )
    in_b_own, in_b_other = low_sum(keep_in_b, in_b_came)
    in_b_other = rounded([after(in_b_other[0], send_glu), *in_b_other[1:]])
    in_a_top = top_swap(in_b_other)
    sum_in_b = Sum(*in_b_own, in_b_top)
    in_b_near = sum_in_b.upper()
    in_b_near_came = near_swap(in_b_near)

    lower = (me_b >> top) == 0

    def halves(a, b, axis):
        return jnp.concatenate([jnp.where(lower, a, b), jnp.where(lower, b, a)], axis=axis)

    in_bias_sums = halves(bias_a.reshape(-1), bias_b.reshape(-1), 0)
    small_grads = jnp.concatenate(
        [
            value.reshape(devices, -1)
            for value in (grad_glu_bias[0], sums[1], sums[2], sums[0], in_bias_sums)
        ],
        axis=1,
    )
    small_grads = small_grads.reshape(batch_size, seq_size, -1)
    small_grads = jnp.moveaxis(small_grads, 1, 0).reshape(seq_size, -1)
    high = lax.reduce_precision(small_grads, 8, 7)
    rest = (small_grads - high).astype(bf16)
    extra_rows = -(-2 * small_grads.shape[1] // (16 * chan)) * 16
    blank = jnp.zeros((seq_size, extra_rows * chan - 2 * small_grads.shape[1]), bf16)
    extra = jnp.concatenate([high.astype(bf16), rest, blank], axis=1)
    extra = extra.reshape(seq_size, extra_rows, chan)
    (out_a_sum,) = low_sum(grad_out_a[: half // 2], out_a_came)
    out_a_sum = [v.reshape(seq_size, -1, width) for v in out_a_sum]
    grads_in, extra, out_a_sum, in_a_own, near, far, input_mult = together(
        (grads_in, extra, out_a_sum, in_a_own, near, far, input_mult)
    )

    moved_back, cross, state_sums = back_call(
        meta,
        after(grads_in, in_b_other, in_b_near),
        normed,
        drive_spec,
        mixed,
        vec_one,
        spec,
        fwd,
        inv,
        extra,
    )
    moved_back, cross, in_b_near_came, out_a_top = together(
        (moved_back, cross, in_b_near_came, out_a_top)
    )

    moved_back = exchange(moved_back)
    glu_came = swap(after(send_glu, cross), "batch", 1)
    sum_out = Sum(*out_a_sum, out_a_top.reshape(seq_size, -1, width))
    out_near = sum_out.upper()
    out_near_came = near_swap(out_near)
    sum_in_b.keep(after(in_b_near_came, out_near))
    in_b_middle = sum_in_b.upper()
    in_b_middle_came = middle_swap(in_b_middle)
    glu_own, glu_other = low_sum(keep_glu, after(glu_came, in_b_middle))
    glu_other = rounded(glu_other)
    glu_top_came = top_swap(glu_other)
    sum_in_a = Sum(*in_a_own, after(in_a_top, glu_other))
    in_a_near = sum_in_a.upper()
    in_a_near_came = near_swap(in_a_near)
    raw_modes = modes_call(meta, after(cross, in_a_near), far, near, inv)
    in_b_middle_came, in_a_near_came, out_near_came, glu_top_came = after(
        (in_b_middle_came, in_a_near_came, out_near_came, glu_top_came), raw_modes
    )
    sum_in_b.keep(in_b_middle_came)
    sum_in_b.middle()
    in_b_last = sum_in_b.upper()
    in_b_last_came = last_swap(in_b_last)
    sum_in_a.keep(after(in_a_near_came, in_b_last))
    in_a_middle = sum_in_a.upper()
    in_a_middle_came = middle_swap(in_a_middle)
    sum_glu = Sum(*glu_own, after(glu_top_came, in_a_middle))
    glu_near = sum_glu.upper()
    glu_near_came = near_swap(glu_near)
    sum_out.keep(after(out_near_came, glu_near))
    out_middle = sum_out.upper()
    out_middle_came = middle_swap(out_middle)

    input_grad = input_call(meta, after(moved_back, out_middle), x, grad_resid, perm)
    input_grad, in_a_middle_came, glu_near_came, out_middle_came = together(
        (input_grad, in_a_middle_came, glu_near_came, out_middle_came)
    )
    sum_glu.keep(glu_near_came)
    glu_middle = sum_glu.upper()
    glu_middle_came = middle_swap(glu_middle)
    sum_in_a.keep(after(in_a_middle_came, glu_middle))
    sum_in_a.middle()
    in_a_last = sum_in_a.upper()
    in_a_last_came = last_swap(in_a_last)
    sum_out.keep(after(out_middle_came, in_a_last))
    sum_out.middle()
    out_last = sum_out.upper()
    out_last_came = last_swap(out_last)
    sum_glu.keep(after(glu_middle_came, out_last))
    sum_glu.middle()
    glu_last = sum_glu.upper()
    glu_last_came = last_swap(glu_last)
    out_a, out_b, resid = after((out_a, out_b, resid), glu_last)
    output = resid + (out_a + out_b + vec_two[2:3]).reshape(resid.shape)
    output = output.astype(bf16)
    in_a_last_came, out_last_came, in_b_last_came = after(
        (in_a_last_came, out_last_came, in_b_last_came), output
    )
    raw_modes, state_sums = after((raw_modes, state_sums), input_grad)

    def finish(value, came):
        value.keep(came)
        return value.total()[0]

    z = cmul((raw_modes[0], raw_modes[1]), input_mult)
    state_grads = jnp.concatenate([z[0], -z[1], state_sums[:3]], axis=0).T
    state_grads = reduce_batch(state_grads.reshape(batch_size, shard_rows, -1))
    grad_state = jnp.stack([state_grads[:, :mode_count], state_grads[:, mode_count : 2 * mode_count]])
    grad_out_total = finish(sum_out, out_last_came)
    far_in = halves(finish(sum_in_a, in_a_last_came), finish(sum_in_b, in_b_last_came), 0)
    grad_in_total = jnp.concatenate([far_in[b] for b in range(batch_size)], axis=1)
    grad_glu_total = finish(sum_glu, glu_last_came)

    small_came = moved_back[:, micro * span :, :].reshape(seq_size, -1).astype(f32)
    small_came = jnp.sum(small_came, axis=0)
    size = batch_size * small_size
    small_came = (small_came[:size] + small_came[size : 2 * size]).reshape(batch_size, -1)
    own = reduce_batch(jnp.take(small_came, natural_piece, axis=0))
    grad_glu_bias_own, grad_gain_two, grad_bias_two, grad_out_bias, grad_in_bias_own = [
        own[s : s + c] for s, c in zip(starts, counts)
    ]

    return (
        output[:, None],
        input_grad[:, None],
        state_grads[:, 2 * mode_count + 1],
        state_grads[:, 2 * mode_count + 2],
        grad_state,
        state_grads[:, 2 * mode_count],
        grad_glu_total,
        grad_glu_bias_own,
        grad_gain_two,
        grad_bias_two,
        grad_in_total,
        grad_in_bias_own,
        grad_out_total,
        grad_out_bias,
    )


def solution(mesh):
    both = ("batch", "seq")
    rows = P(None, "batch", "seq", None)
    vector = P(both)
    matrix = P(both, None)
    state = P(None, both, None)
    return jax.shard_map(
        per_device,
        mesh=mesh,
        in_specs=(
            rows,
            P(None, "batch"),
            rows,
            vector,
            vector,
            vector,
            state,
            vector,
            matrix,
            vector,
            vector,
            vector,
            matrix,
            vector,
            matrix,
            vector,
        ),
        out_specs=(
            rows,
            rows,
            vector,
            vector,
            state,
            vector,
            matrix,
            vector,
            vector,
            vector,
            matrix,
            vector,
            matrix,
            vector,
        ),
        check_vma=False,
    )
```

```python
import functools
import math

import jax
import jax.numpy as jnp
import numpy as np
from jax import lax
from jax.experimental import pallas as pl
from jax.experimental.pallas import tpu as pltpu
from jax.sharding import PartitionSpec as P

f32 = jnp.float32
bf16 = jnp.bfloat16
norm_eps = 1e-05
near_span = 64
vmem_limit = 60 * 1024 * 1024
gelu_scale = math.sqrt(2.0 / math.pi)
gelu_cubic = 0.044715


def after(value, *tokens):
    return jax.tree.map(lambda v: lax.optimization_barrier((v, tokens))[0], value)


together = lax.optimization_barrier


def bits_of(size):
    count = size.bit_length() - 1
    if (1 << count) != size:
        raise ValueError("axis size")
    return count


def reverse_bits(value, count):
    result = 0
    for bit in range(count):
        result = result | (((value >> bit) & 1) << (count - 1 - bit))
    return result


def swap(value, axis, bit):
    size = lax.axis_size(axis)
    return lax.ppermute(value, axis, [(i, i ^ bit) for i in range(size)])


def gather_first(shard):
    return swap(shard[None], "seq", lax.axis_size("seq") // 2)


def gather_direct(shard):
    size = lax.axis_size("seq")
    return [swap(shard[None], "seq", bits) for bits in (size // 2, size // 4, size // 2 + size // 4)]


def gather_more(joined, lowest):
    size = lax.axis_size("seq")
    while joined.shape[0] << lowest < size:
        bit = size // joined.shape[0] // 2
        joined = jnp.concatenate([joined, swap(joined, "seq", bit)], axis=0)
    return joined


class Sum:
    def __init__(self, *terms):
        self.terms = list(terms)

    def total(self, start=0, stop=None):
        values = [term[start:stop].astype(f32) for term in self.terms]
        return functools.reduce(lambda a, b: a + b, values)

    def upper(self):
        return self.total(self.terms[0].shape[0] // 2).astype(bf16)

    def keep(self, came):
        half = self.terms[0].shape[0] // 2
        self.terms = [term[:half] for term in self.terms] + [came]

    def add(self, came):
        self.terms.append(came)

    def middle(self):
        for bit in range(2, bits_of(lax.axis_size("seq")) - 1):
            self.keep(swap(self.upper(), "seq", 1 << bit))


def swap_batch(pieces, bit):
    return [swap(piece, "batch", 1 << bit) for piece in pieces]


def gather_batch(part):
    pieces = [part]
    for bit in reversed(range(bits_of(lax.axis_size("batch")))):
        pieces = pieces + swap_batch(pieces, bit)
    return pieces


def reduce_batch(value):
    for bit in range(bits_of(lax.axis_size("batch"))):
        half = value.shape[0] // 2
        value = value[:half] + swap(value[half:], "batch", 1 << bit)
    return value[0]


def exchange(parts):
    return lax.all_to_all(parts, "seq", 0, 0)


def gelu_parts(values):
    square = values * values
    half = 0.5 * jnp.tanh(values * (gelu_scale + gelu_scale * gelu_cubic * square)) + 0.5
    return square, half


def gelu_value(values):
    return values * gelu_parts(values)[1]


def gelu_both(values):
    square, half = gelu_parts(values)
    value = values * half
    inner = 2.0 * gelu_scale + 6.0 * gelu_scale * gelu_cubic * square
    return value, half + value * (1.0 - half) * inner


def gelu_slope(values):
    return gelu_both(values)[1]


def layer_stats(values):
    centered = values - jnp.mean(values, axis=-1, keepdims=True)
    scale_inv = lax.rsqrt(jnp.mean(centered * centered, axis=-1, keepdims=True) + norm_eps)
    return centered * scale_inv, scale_inv


def norm_back(grad_normed, normed, scale_inv):
    first_mean = jnp.mean(grad_normed, axis=-1, keepdims=True)
    second_mean = jnp.mean(grad_normed * normed, axis=-1, keepdims=True)
    return scale_inv * (grad_normed - first_mean - normed * second_mean)


def dot(left, right):
    return jnp.dot(left, right, preferred_element_type=f32)


def dot_left_t(left, right):
    return lax.dot_general(left, right, (((0,), (0,)), ((), ())), preferred_element_type=f32)


def dot_right_t(left, right):
    return lax.dot_general(left, right, (((1,), (1,)), ((), ())), preferred_element_type=f32)


def stack_split(values):
    high = values.astype(bf16)
    low = (values - high.astype(f32)).astype(bf16)
    return jnp.concatenate([high, high, low], axis=0)


def table_split(table):
    high = table.astype(jnp.bfloat16)
    low = (table - high.astype(np.float64)).astype(jnp.bfloat16)
    return np.concatenate([high, low, high], axis=1)


def transform_tables(span):
    freqs = np.arange(span, dtype=np.float64) + 0.5
    phase = 2.0 * math.pi / (2 * span) * freqs[:, None] * np.arange(span, dtype=np.float64)[None]
    forward = np.concatenate([np.cos(phase), -np.sin(phase)], axis=0)
    backward = np.concatenate([np.cos(phase).T, -np.sin(phase).T], axis=1) / span
    return table_split(forward), table_split(backward)


def loop(count, body):
    if count <= 8:
        for index in range(count):
            body(index)
    else:
        lax.fori_loop(0, count, lambda index, carry: (body(index), carry)[1], 0)


def sum_loop(first, last, body, init):
    if isinstance(first, int) and isinstance(last, int):
        for index in range(first, last):
            init = body(index, init)
        return init
    return lax.fori_loop(first, last, body, init)


def full_spec(shape, buffered=True):
    zeros = (0,) * len(shape)
    if buffered:
        return pl.BlockSpec(shape, lambda *_: zeros, pipeline_mode=pl.Buffered(1))
    return pl.BlockSpec(shape, lambda *_: zeros)


def parted(parts, span, chan):
    return pl.BlockSpec((parts, span, chan), lambda m, _: (0, m, 0))


def call(kernel, grid, meta, in_specs, operands, out_specs, out_shape, scratch, flops, name):
    return pl.pallas_call(
        kernel,
        grid_spec=pltpu.PrefetchScalarGridSpec(
            num_scalar_prefetch=1,
            grid=grid,
            in_specs=in_specs,
            out_specs=out_specs,
            scratch_shapes=scratch,
        ),
        out_shape=out_shape,
        compiler_params=pltpu.CompilerParams(
            vmem_limit_bytes=vmem_limit, dimension_semantics=("arbitrary",) * len(grid)
        ),
        cost_estimate=pl.CostEstimate(
            flops=int(flops * 0.02), bytes_accessed=int(flops * 0.02 / 400), transcendentals=0
        ),
        name=name,
    )(meta, *operands)


def norm_kernel(batch_bits, shard_rows, seq_size, meta, x_ref, extra_ref, out_ref, perm_ref):
    width = x_ref.shape[2]
    chan = out_ref.shape[-1]

    @pl.when(pl.program_id(0) == 0)
    def _():
        lane = lax.broadcasted_iota(jnp.int32, (width, width), 1)
        piece = (lane & (chan - 1)) // shard_rows
        source = (
            (reverse_bits(piece, batch_bits) ^ meta[0]) * seq_size + lane // chan
        ) * shard_rows + (lane & (shard_rows - 1))
        row = lax.broadcasted_iota(jnp.int32, (width, width), 0)
        perm_ref[...] = jnp.where(row == source, 1.0, 0.0).astype(bf16)
        for d in range(out_ref.shape[0]):
            out_ref[d, pl.ds(out_ref.shape[1] - 16, 16), :] = extra_ref[...]

    span = x_ref.shape[1]
    rows = pl.ds(pl.multiple_of(pl.program_id(0) * span, span), span)
    normed, _ = layer_stats(x_ref[0].astype(f32))
    spread = dot(normed.astype(bf16), perm_ref[...]).astype(bf16)
    for d in range(out_ref.shape[0]):
        out_ref[d, rows, :] = spread[:, d * chan : (d + 1) * chan]


def norm_call(meta, x, extra, batch_bits, shard_rows, parts):
    micro, span, width = x.shape
    chan = width // parts
    return call(
        functools.partial(norm_kernel, batch_bits, shard_rows, parts),
        (micro,),
        meta,
        [pl.BlockSpec((1, span, width), lambda m, _: (m, 0, 0))]
        + [full_spec(extra.shape)],
        (x, extra),
        [full_spec((parts, micro * span + 16, chan)), full_spec((width, width))],
        [
            jax.ShapeDtypeStruct((parts, micro * span + 16, chan), bf16),
            jax.ShapeDtypeStruct((width, width), bf16),
        ],
        [],
        2 * micro * span * width * width,
        "norm_one",
    )


def kernel_kernel(meta, lift_re, lift_im, near_re, near_im, fwd_ref, out_ref, series, spec):
    modes, span_near, chan = near_re.shape
    far_count = lift_re.shape[1]
    blocks, _, span, _ = out_ref.shape
    group = 2

    def far_group(index, carry):
        def one_mode(n, acc):
            near_r, near_i = near_re[n], near_im[n]
            result = []
            for g in range(group):
                row = index * group + g
                a = lift_re[n, pl.ds(row, 1), :]
                b = lift_im[n, pl.ds(row, 1), :]
                result.append(acc[g] + (a * near_r - b * near_i))
            return tuple(result)

        zero = jnp.zeros((span_near, chan), f32)
        acc = lax.fori_loop(0, modes, one_mode, (zero,) * group, unroll=4)
        for g in range(group):
            start = pl.multiple_of((index * group + g) * span_near, span_near)
            series[pl.ds(start, span_near), :] = acc[g]
        return carry

    lax.fori_loop(0, far_count // group, far_group, 0)

    def one_pair(index):
        first = index * 2 * span
        pair = [series[pl.ds(first + k * span, span), :] for k in range(2)]
        both = dot(fwd_ref[...], stack_split(jnp.concatenate(pair, axis=1)))
        for k in range(2):
            spec[index * 2 + k] = both[:, k * chan : (k + 1) * chan]

    loop(blocks // 2, one_pair)
    rows = lax.broadcasted_iota(jnp.int32, (span, chan), 0)
    sign = 1.0 - 2.0 * (rows & 1).astype(f32)

    def one_block(d):
        real, imag = spec[d, :span], spec[d, span:]
        before = d - 1 if isinstance(d, int) else jnp.maximum(d - 1, 0)
        if isinstance(d, int) and d == 0:
            out_ref[0, 0], out_ref[0, 1] = real, imag
            return
        keep = 1.0 if isinstance(d, int) else jnp.where(d > 0, 1.0, 0.0)
        out_ref[d, 0] = real - keep * (sign * spec[before, span:])
        out_ref[d, 1] = imag + keep * (sign * spec[before, :span])

    loop(blocks, one_block)


def kernel_call(meta, lift, near, fwd, blocks, span):
    chan = near[0].shape[-1]
    operands = (lift[0], lift[1], near[0], near[1], fwd)
    return call(
        kernel_kernel,
        (1,),
        meta,
        [full_spec(a.shape) for a in operands],
        operands,
        full_spec((blocks, 2, span, chan)),
        jax.ShapeDtypeStruct((blocks, 2, span, chan), f32),
        [pltpu.VMEM((blocks * span, chan), f32), pltpu.VMEM((blocks, 2 * span, chan), f32)],
        1.1e10,
        "state_kernel",
    )


def mask_of(meta, m, block, span, chan):
    rows = block * span + lax.broadcasted_iota(jnp.int32, (span, chan), 0)
    return (rows < meta[1 + m]).astype(f32)


freq_tile = 64


def conv_kernel(
    meta,
    normed_ref,
    vec_ref,
    spec_ref,
    fwd_ref,
    inv_ref,
    drive_ref,
    mixed_ref,
    out_ref,
    drive,
    spectrum,
):
    m = pl.program_id(0)
    blocks, span, chan = drive.shape
    gain, bias, skip = vec_ref[0:1, :], vec_ref[1:2, :], vec_ref[2:3, :]

    def drive_pair(pair):
        values = []
        for k in range(2):
            block = 2 * pair + k
            normed = normed_ref[block].astype(f32)
            u = mask_of(meta, m, block, span, chan) * (normed * gain + bias)
            drive[block] = u
            values.append(u)
        both = dot(fwd_ref[...], stack_split(jnp.concatenate(values, axis=1)))
        for k in range(2):
            drive_ref[0, 2 * pair + k] = both[:, k * chan : (k + 1) * chan]

    loop(blocks // 2, drive_pair)

    def one_pair(index):
        for k in range(2):
            i = index * 2 + k

            def one_tile(tile, carry):
                low = pl.ds(pl.multiple_of(tile * freq_tile, freq_tile), freq_tile)
                high = pl.ds(pl.multiple_of(span + tile * freq_tile, freq_tile), freq_tile)

                def one_term(j, acc):
                    xr, xi = drive_ref[0, j, low], drive_ref[0, j, high]
                    gr, gi = spec_ref[i - j, 0, low], spec_ref[i - j, 1, low]
                    return (acc[0] + (xr * gr - xi * gi), acc[1] + (xr * gi + xi * gr))

                zero = jnp.zeros((freq_tile, chan), f32)
                acc = sum_loop(0, i + 1, one_term, (zero, zero))
                spectrum[k, low] = acc[0]
                spectrum[k, high] = acc[1]
                return carry

            lax.fori_loop(0, span // freq_tile, one_tile, 0, unroll=True)
        both = dot(
            inv_ref[...], stack_split(jnp.concatenate([spectrum[0], spectrum[1]], axis=1))
        )
        for k in range(2):
            i = index * 2 + k
            mixed = both[:, k * chan : (k + 1) * chan] + skip * drive[i]
            mixed_ref[0, i] = mixed
            out_ref[i] = gelu_value(mixed).astype(bf16)

    loop(blocks // 2, one_pair)


def conv_call(meta, micro, normed, vec, spec, fwd, inv):
    parts, _, chan = normed.shape
    span = spec.shape[2]
    wide = lambda rows: pl.BlockSpec((1, parts, rows, chan), lambda m, _: (m, 0, 0, 0))
    return call(
        conv_kernel,
        (micro,),
        meta,
        [parted(parts, span, chan)] + [full_spec(a.shape) for a in (vec, spec, fwd, inv)],
        (normed, vec, spec, fwd, inv),
        [wide(2 * span), wide(span), parted(parts, span, chan)],
        [
            jax.ShapeDtypeStruct((micro, parts, 2 * span, chan), f32),
            jax.ShapeDtypeStruct((micro, parts, span, chan), f32),
            jax.ShapeDtypeStruct((parts, micro * span, chan), bf16),
        ],
        [
            pltpu.VMEM((parts, span, chan), f32),
            pltpu.VMEM((2, 2 * span, chan), f32),
        ],
        1.5e10,
        "state_conv",
    )


def back_kernel(
    meta,
    grads_ref,
    normed_ref,
    drive_ref,
    mixed_ref,
    vec_ref,
    spec_ref,
    fwd_ref,
    inv_ref,
    extra_ref,
    out_ref,
    cross_ref,
    sums_ref,
    grad_mixed,
    grad_spec,
    spectrum,
):
    m = pl.program_id(0)
    blocks, span, chan = grad_mixed.shape
    gain, bias, skip = vec_ref[0:1, :], vec_ref[1:2, :], vec_ref[2:3, :]

    @pl.when(m == 0)
    def _():
        cross_ref[...] = jnp.zeros_like(cross_ref)
        sums_ref[...] = jnp.zeros_like(sums_ref)
        extra = extra_ref.shape[1]
        out_ref[:, pl.ds(out_ref.shape[1] - extra, extra), :] = extra_ref[...]

    def grad_pair(pair):
        values = []
        for k in range(2):
            block = 2 * pair + k
            normed = normed_ref[block].astype(f32)
            u = mask_of(meta, m, block, span, chan) * (normed * gain + bias)
            gm = grads_ref[block].astype(f32) * gelu_slope(mixed_ref[0, block])
            sums_ref[0:1, :] += jnp.sum(gm * u, axis=0, keepdims=True)
            grad_mixed[block] = gm
            values.append(gm)
        both = dot(fwd_ref[...], stack_split(jnp.concatenate(values, axis=1)))
        for k in range(2):
            grad_spec[2 * pair + k] = both[:, k * chan : (k + 1) * chan]

    loop(blocks // 2, grad_pair)

    def tiles_of(body):
        def one_tile(tile, carry):
            low = pl.ds(pl.multiple_of(tile * freq_tile, freq_tile), freq_tile)
            high = pl.ds(pl.multiple_of(span + tile * freq_tile, freq_tile), freq_tile)
            body(low, high)
            return carry

        lax.fori_loop(0, span // freq_tile, one_tile, 0, unroll=True)

    zero = jnp.zeros((freq_tile, chan), f32)

    def one_pair(index):
        for k in range(2):
            j = index * 2 + k

            def body(low, high):
                def one_term(i, acc):
                    mr, mi = grad_spec[i, low], grad_spec[i, high]
                    gr, gi = spec_ref[i - j, 0, low], spec_ref[i - j, 1, low]
                    return (acc[0] + (mr * gr + mi * gi), acc[1] + (mi * gr - mr * gi))

                acc = sum_loop(j, blocks, one_term, (zero, zero))
                spectrum[k, low] = acc[0]
                spectrum[k, high] = acc[1]

            tiles_of(body)
        both = dot(
            inv_ref[...], stack_split(jnp.concatenate([spectrum[0], spectrum[1]], axis=1))
        )
        for k in range(2):
            j = index * 2 + k
            grad_mixed[j] = both[:, k * chan : (k + 1) * chan] + skip * grad_mixed[j]

    loop(blocks // 2, one_pair)

    def finish(block):
        g = mask_of(meta, m, block, span, chan) * grad_mixed[block]
        normed = normed_ref[block].astype(f32)
        sums_ref[1:2, :] += jnp.sum(g * normed, axis=0, keepdims=True)
        sums_ref[2:3, :] += jnp.sum(g, axis=0, keepdims=True)
        out_ref[block, pl.ds(pl.multiple_of(m * span, span), span), :] = (g * gain).astype(bf16)

    loop(blocks, finish)

    def one_lag(d):
        def body(low, high):
            def one_term(j, acc):
                mr, mi = grad_spec[j + d, low], grad_spec[j + d, high]
                xr, xi = drive_ref[0, j, low], drive_ref[0, j, high]
                return (acc[0] + (mr * xr + mi * xi), acc[1] + (mi * xr - mr * xi))

            acc = sum_loop(0, blocks - d, one_term, (cross_ref[d, low], cross_ref[d, high]))
            cross_ref[d, low] = acc[0]
            cross_ref[d, high] = acc[1]

        tiles_of(body)

    loop(blocks, one_lag)


def back_call(meta, grads, normed, drive, mixed, vec, spec, fwd, inv, extra):
    parts, _, chan = normed.shape
    micro, _, span, _ = mixed.shape
    total = micro * span + extra.shape[1]
    mode = None if parts <= 8 else pl.Buffered(1)
    wide = lambda rows: pl.BlockSpec(
        (1, parts, rows, chan), lambda m, _: (m, 0, 0, 0), pipeline_mode=mode
    )
    return call(
        back_kernel,
        (micro,),
        meta,
        [parted(parts, span, chan)] * 2
        + [wide(2 * span), wide(span)]
        + [full_spec(a.shape) for a in (vec, spec, fwd, inv, extra)],
        (grads, normed, drive, mixed, vec, spec, fwd, inv, extra),
        [
            full_spec((parts, total, chan)),
            full_spec((parts, 2 * span, chan)),
            full_spec((8, chan)),
        ],
        [
            jax.ShapeDtypeStruct((parts, total, chan), bf16),
            jax.ShapeDtypeStruct((parts, 2 * span, chan), f32),
            jax.ShapeDtypeStruct((8, chan), f32),
        ],
        [
            pltpu.VMEM((parts, span, chan), f32),
            pltpu.VMEM((parts, 2 * span, chan), f32),
            pltpu.VMEM((2, 2 * span, chan), f32),
        ],
        2e10,
        "state_back",
    )


def modes_kernel(meta, cross_ref, far_re, far_im, near_re, near_im, inv_ref, out_ref, series):
    modes, span_near, chan = near_re.shape
    far_count = far_re.shape[1]
    blocks, double, _ = cross_ref.shape
    span = double // 2
    rows = lax.broadcasted_iota(jnp.int32, (span, chan), 0)
    sign = 1.0 - 2.0 * (rows & 1).astype(f32)

    def one_pair(index):
        pair = []
        for k in range(2):
            d = index * 2 + k
            real, imag = cross_ref[d, :span], cross_ref[d, span:]
            if isinstance(d, int):
                keep = 1.0 if d + 1 < blocks else 0.0
                after = min(d + 1, blocks - 1)
            else:
                keep = jnp.where(d + 1 < blocks, 1.0, 0.0)
                after = jnp.minimum(d + 1, blocks - 1)
            real = real + keep * (sign * cross_ref[after, span:])
            imag = imag - keep * (sign * cross_ref[after, :span])
            pair.append(jnp.concatenate([real, imag], axis=0))
        both = dot(inv_ref[...], stack_split(jnp.concatenate(pair, axis=1)))
        for k in range(2):
            series[pl.ds((index * 2 + k) * span, span), :] = both[:, k * chan : (k + 1) * chan]

    loop(blocks // 2, one_pair)
    group = 2

    def mode_group(index, carry):
        def one_far(i, acc):
            values = series[pl.ds(pl.multiple_of(i * span_near, span_near), span_near), :]
            result = []
            for g in range(group):
                n = index * group + g
                a = far_re[n, pl.ds(i, 1), :]
                b = far_im[n, pl.ds(i, 1), :]
                result.append((acc[g][0] + a * values, acc[g][1] + b * values))
            return tuple(result)

        zero = jnp.zeros((span_near, chan), f32)
        acc = lax.fori_loop(0, far_count, one_far, ((zero, zero),) * group, unroll=4)
        for g in range(group):
            n = index * group + g
            near_r, near_i = near_re[n], near_im[n]
            re, im = acc[g]
            out_ref[0, pl.ds(n, 1), :] = jnp.sum(re * near_r - im * near_i, axis=0, keepdims=True)
            out_ref[1, pl.ds(n, 1), :] = jnp.sum(re * near_i + im * near_r, axis=0, keepdims=True)
        return carry

    lax.fori_loop(0, modes // group, mode_group, 0)


def modes_call(meta, cross, far, near, inv):
    modes, _, chan = near[0].shape
    blocks, double, _ = cross.shape
    operands = (cross, far[0], far[1], near[0], near[1], inv)
    return call(
        modes_kernel,
        (1,),
        meta,
        [full_spec(a.shape) for a in operands],
        operands,
        full_spec((2, modes, chan)),
        jax.ShapeDtypeStruct((2, modes, chan), f32),
        [pltpu.VMEM((blocks * double // 2, chan), f32)],
        1.1e10,
        "state_modes",
    )


class Rows:
    def __init__(self, width, shard_rows, seq_size, batch_size, table, by_channel=False):
        self.width = width
        self.shard_rows = shard_rows
        self.seq_size = seq_size
        self.batch_size = batch_size
        self.table = table
        self.piece_rows = shard_rows * seq_size
        self.by_block = shard_rows % 16 == 0
        self.by_channel = by_channel

    def natural(self, meta, p, q):
        start = meta[self.table + p * self.seq_size + q] * self.shard_rows
        return pl.ds(pl.multiple_of(start, self.shard_rows), self.shard_rows)

    def order(self, meta, place):
        shape = (self.width, self.width)
        relative = lax.broadcasted_iota(jnp.int32, shape, 0)
        piece = relative // self.piece_rows
        position = (relative % self.piece_rows) // self.shard_rows
        seq = reverse_bits(position, bits_of(self.seq_size)) ^ meta[0]
        if self.by_channel:
            shard = seq * self.batch_size + piece
        else:
            batch = reverse_bits(piece, bits_of(self.batch_size)) ^ meta[place + 1]
            shard = batch * self.seq_size + seq
        source = shard * self.shard_rows + relative % self.shard_rows
        return jnp.where(lax.broadcasted_iota(jnp.int32, shape, 1) == source, 1.0, 0.0).astype(bf16)

    def to_natural(self, meta, place, parts, target):
        if self.by_block:
            for p, part in enumerate(parts):
                for q in range(self.seq_size):
                    target[self.natural(meta, p, q), :] = part[
                        pl.ds(q * self.shard_rows, self.shard_rows), :
                    ]
        else:
            whole = jnp.concatenate([part[...] for part in parts], axis=0)
            target[...] = dot_left_t(self.order(meta, place), whole).astype(bf16)

    def to_relative(self, meta, place, value, scratch, store):
        if self.by_block:
            scratch[...] = value.astype(bf16)
        else:
            moved = dot(self.order(meta, place), value.astype(bf16))
        for p in range(self.batch_size):
            for q in range(self.seq_size):
                if self.by_block:
                    block = scratch[self.natural(meta, p, q), :]
                else:
                    start = (p * self.seq_size + q) * self.shard_rows
                    block = moved[start : start + self.shard_rows].astype(bf16)
                store(p, q, block)


def gate_kernel(pieces, order, meta, *refs):
    active_ref, x_ref, cot_ref, vec_ref, glu_bias_ref = refs[:5]
    weights = refs[5 : 5 + pieces]
    act_ref, resid_ref, gated_ref, norm_ref, norm_t_ref, cot_out, weight_scr = refs[5 + pieces :]
    m = pl.program_id(0)
    _, span, width = x_ref.shape
    micro = pl.num_programs(0)

    @pl.when(m == 0)
    def _():
        order.to_natural(meta, 1 + micro, weights, weight_scr)

    act = jnp.concatenate([active_ref[d] for d in range(active_ref.shape[0])], axis=1)
    act_ref[...] = act
    gated = dot(act, weight_scr[...]) + glu_bias_ref[...]
    gated_ref[0] = gated
    residual = x_ref[0].astype(f32) + gated[:, :width] * jax.nn.sigmoid(gated[:, width:])
    resid_ref[0] = residual
    normed, _ = layer_stats(residual)
    norm_two = (normed * vec_ref[0:1, :] + vec_ref[1:2, :]).astype(bf16)
    norm_ref[...] = norm_two
    norm_t_ref[...] = norm_two.T
    rows = meta[1 + micro] + lax.broadcasted_iota(jnp.int32, (span, width), 0)
    cot_out[...] = jnp.where(rows < meta[1 + m], cot_ref[0].astype(f32), 0.0).astype(bf16)


def gate_call(meta, order, active, x, cot, vec, glu_bias, weights):
    parts, _, chan = active.shape
    pieces = len(weights)
    micro, span, width = x.shape
    tokens = micro * span
    tile = lambda cols: pl.BlockSpec((1, span, cols), lambda m, _: (m, 0, 0))
    flat = pl.BlockSpec((span, width), lambda m, _: (m, 0))
    return call(
        functools.partial(gate_kernel, pieces, order),
        (micro,),
        meta,
        [parted(parts, span, chan), tile(width), tile(width)]
        + [full_spec(a.shape) for a in (vec, glu_bias, *weights)],
        (active, x, cot, vec, glu_bias, *weights),
        [
            flat,
            tile(width),
            tile(2 * width),
            flat,
            pl.BlockSpec((width, span), lambda m, _: (0, m)),
            flat,
        ],
        [
            jax.ShapeDtypeStruct((tokens, width), bf16),
            jax.ShapeDtypeStruct((micro, span, width), f32),
            jax.ShapeDtypeStruct((micro, span, 2 * width), f32),
            jax.ShapeDtypeStruct((tokens, width), bf16),
            jax.ShapeDtypeStruct((width, tokens), bf16),
            jax.ShapeDtypeStruct((tokens, width), bf16),
        ],
        [pltpu.VMEM((width, 2 * width), bf16)],
        6 * tokens * width * width,
        "gated_unit",
    )


def ff_block_of(piece_ff):
    return min(1024, piece_ff)


def ffn_kernel(pieces, batch_pieces, sub, order, out_table, place, first, second, meta, *refs):
    refs = list(refs)
    take = lambda count: [refs.pop(0) for _ in range(count)]
    half = batch_pieces // 2
    (cot_ref,) = take(1)
    w_out = take(pieces)
    if first:
        norm_ref, bias_ref = take(2)
        w_in = take(batch_pieces)
    else:
        spread_ref, hidden_ref = take(2)
    if second:
        (norm_t_ref,) = take(1)
    if first:
        back_ref, grad_bias = take(2)
        if not second:
            spread_ref, hidden_ref = take(2)
    if second:
        (out_ref,) = take(1)
        grad_out, grad_in = take(pieces), take(half)
        (grad_in_send,) = take(1)
    (out_scr,) = take(1)
    if first:
        (in_scr,) = take(1)
    if second:
        (grad_in_scr,) = take(1)
    k = pl.program_id(0)
    s = pl.program_id(1)
    ff_block = out_scr.shape[0]
    subs = ff_block // sub
    start = jnp.logical_and(k == 0, s == 0)

    def sub_rows(t):
        return pl.ds(pl.multiple_of(meta[out_table + s * subs + t] * sub, sub), sub)

    for piece in range(pieces):

        @pl.when(k == piece)
        def _():
            for t in range(subs):
                out_scr[pl.ds(t * sub, sub), :] = w_out[piece][sub_rows(t), :]

    def accumulate(ref, part):
        @pl.when(start)
        def _():
            ref[...] = part

        @pl.when(jnp.logical_not(start))
        def _():
            ref[...] += part

    if first:
        order.to_natural(meta, place, w_in, in_scr)
        hidden = dot(norm_ref[...], in_scr[...]) + bias_ref[0]
        spread, slope = gelu_both(hidden)
        spread = spread.astype(bf16)
        grad_hidden = (dot_right_t(cot_ref[...], out_scr[...]) * slope).astype(bf16)
        grad_bias[0] = jnp.sum(grad_hidden.astype(f32), axis=0, keepdims=True)
        if not second:
            spread_ref[...] = spread
            hidden_ref[...] = grad_hidden
        accumulate(back_ref, dot_right_t(grad_hidden, in_scr[...]))
    else:
        spread, grad_hidden = spread_ref[...], hidden_ref[...]

    if second:
        accumulate(out_ref, dot(spread, out_scr[...]))

        def store(p, q, block):
            if p < half:
                grad_in[p][q, 0] = block
            else:
                grad_in_send[p - half, q, 0] = block

        order.to_relative(meta, place, dot(norm_t_ref[...], grad_hidden), grad_in_scr, store)
        part = dot_left_t(spread, cot_ref[...]).astype(bf16)
        for piece in range(pieces):

            @pl.when(k == piece)
            def _():
                for t in range(subs):
                    grad_out[piece][sub_rows(t), :] = part[t * sub : (t + 1) * sub, :]


def ffn_call(meta, order, out_table, place, base, column, cot, w_out, norm=None, bias=None, w_in=None, norm_t=None, kept=None):
    first, second = norm is not None, norm_t is not None
    pieces, batch_pieces = len(w_out), order.batch_size
    tokens, width = cot.shape
    piece_ff = w_out[0].shape[0]
    ff_block = ff_block_of(piece_ff)
    steps = piece_ff // ff_block
    sub = piece_ff // order.seq_size
    rows = order.piece_rows
    half = batch_pieces // 2
    seq_size, low = order.seq_size, order.shard_rows
    block = lambda k, s, meta: meta[base + k] + s
    wide = full_spec((tokens, width))
    step_columns = pl.BlockSpec((tokens, ff_block), lambda k, s, meta: (0, k * steps + s))
    activations = jax.ShapeDtypeStruct((tokens, pieces * piece_ff), bf16)
    total = jax.ShapeDtypeStruct((tokens, width), f32)
    operands = [cot, *w_out]
    in_specs = [wide] + [full_spec(a.shape) for a in w_out]
    outs, out_specs, scratch = [], [], [pltpu.VMEM((ff_block, width), bf16)]
    if first:
        operands += [norm, bias, *w_in]
        in_specs += [wide]
        in_specs += [pl.BlockSpec((1, 1, ff_block), lambda k, s, meta: (block(k, s, meta), 0, 0))]
        in_specs += [
            pl.BlockSpec((rows, ff_block), lambda k, s, meta: (0, block(k, s, meta)))
            for _ in w_in
        ]
        outs += [total, jax.ShapeDtypeStruct((pieces * steps, 1, ff_block), f32)]
        out_specs += [wide]
        out_specs += [
            pl.BlockSpec((1, 1, ff_block), lambda k, s, meta: (meta[column + k] * steps + s, 0, 0))
        ]
        scratch += [pltpu.VMEM((width, ff_block), bf16)]
        if not second:
            outs += [activations] * 2
            out_specs += [step_columns] * 2
    else:
        operands += kept
        in_specs += [step_columns] * 2
    if second:
        operands += [norm_t]
        in_specs += [full_spec(norm_t.shape)]
        outs += [total] + [jax.ShapeDtypeStruct(a.shape, bf16) for a in w_out]
        outs += [jax.ShapeDtypeStruct((seq_size, pieces, low, piece_ff), bf16)] * half
        outs += [jax.ShapeDtypeStruct((half, seq_size, pieces, low, piece_ff), bf16)]
        out_specs += [wide] + [full_spec(a.shape) for a in w_out]
        out_specs += [
            pl.BlockSpec((seq_size, 1, low, ff_block), lambda k, s, meta: (0, meta[column + k], 0, s))
        ] * half
        out_specs += [
            pl.BlockSpec(
                (half, seq_size, 1, low, ff_block),
                lambda k, s, meta: (0, 0, meta[column + k], 0, s),
            )
        ]
        scratch += [pltpu.VMEM((width, ff_block), bf16)]
    results = call(
        functools.partial(
            ffn_kernel, pieces, batch_pieces, sub, order, out_table, place, first, second
        ),
        (pieces, steps),
        meta,
        in_specs,
        operands,
        out_specs,
        outs,
        scratch,
        6 * (first + second) * tokens * width * piece_ff * pieces,
        "feed_forward",
    )
    head = results[: 2 * first + 2 * (first and not second)]
    tail = results[len(head) :]
    return head, tail[:1], tail[1 : 1 + pieces], tail[1 + pieces : -1], tail[-1:]


def gate_back_kernel(pieces, halves, order, meta, *refs):
    back = refs[:halves]
    resid_ref, gated_ref, cot_ref, vec_ref = refs[halves : halves + 4]
    weights = refs[halves + 4 : halves + 4 + pieces]
    rest = refs[halves + 4 + pieces :]
    grad_resid_ref, grad_gated_ref, glu_bias_ref, sums_ref, moved_ref, weight_scr = rest
    m = pl.program_id(0)
    count = pl.num_programs(0)
    width = cot_ref.shape[1]

    @pl.when(m == 0)
    def _():
        glu_bias_ref[...] = jnp.zeros_like(glu_bias_ref)
        sums_ref[...] = jnp.zeros_like(sums_ref)
        order.to_natural(meta, 1 + count, weights, weight_scr)

    residual = resid_ref[0]
    grad_norm = back[0][...]
    for h in range(1, halves):
        grad_norm = grad_norm + back[h][...]
    grad_out = cot_ref[...].astype(f32)
    normed, scale = layer_stats(residual)
    sums_ref[0:1, :] += jnp.sum(grad_out, axis=0, keepdims=True)
    sums_ref[1:2, :] += jnp.sum(grad_norm * normed, axis=0, keepdims=True)
    sums_ref[2:3, :] += jnp.sum(grad_norm, axis=0, keepdims=True)
    grad_resid = grad_out + norm_back(grad_norm * vec_ref[0:1, :], normed, scale)
    grad_resid_ref[0] = grad_resid
    gated = gated_ref[0]
    gate = jax.nn.sigmoid(gated[:, width:])
    grad_left = grad_resid * gate
    grad_right = grad_left * gated[:, :width] * (1.0 - gate)
    grad_gated = jnp.concatenate([grad_left, grad_right], axis=1).astype(bf16)
    grad_gated_ref[...] = grad_gated
    glu_bias_ref[0:1, :] += jnp.sum(grad_gated.astype(f32), axis=0, keepdims=True)
    moved = dot_right_t(grad_gated, weight_scr[...]).astype(bf16)
    chan = moved_ref.shape[-1]
    for d in range(moved_ref.shape[0]):
        moved_ref[d] = moved[:, d * chan : (d + 1) * chan]


def gate_back_call(meta, order, parts, back, resid, gated, cot, vec, weights):
    halves, pieces = len(back), len(weights)
    micro, span, width = resid.shape
    tokens = micro * span
    chan = width // parts
    tile = lambda cols: pl.BlockSpec((1, span, cols), lambda m, _: (m, 0, 0))
    flat = lambda cols: pl.BlockSpec((span, cols), lambda m, _: (m, 0))
    return call(
        functools.partial(gate_back_kernel, pieces, halves, order),
        (micro,),
        meta,
        [flat(width)] * halves
        + [tile(width), tile(2 * width), flat(width)]
        + [full_spec(a.shape) for a in (vec, *weights)],
        (*back, resid, gated, cot, vec, *weights),
        [
            tile(width),
            flat(2 * width),
            full_spec((8, 2 * width)),
            full_spec((8, width)),
            parted(parts, span, chan),
        ],
        [
            jax.ShapeDtypeStruct((micro, span, width), f32),
            jax.ShapeDtypeStruct((tokens, 2 * width), bf16),
            jax.ShapeDtypeStruct((8, 2 * width), f32),
            jax.ShapeDtypeStruct((8, width), f32),
            jax.ShapeDtypeStruct((parts, micro * span, chan), bf16),
        ],
        [pltpu.VMEM((width, 2 * width), bf16)],
        4 * tokens * width * width,
        "gated_back",
    )


def gate_weight_kernel(pieces, order, place, meta, act_ref, grad_ref, *refs):
    grad_keep, grad_send, scratch = refs[: pieces // 2], refs[-2], refs[-1]

    def store(p, q, block):
        if p < pieces // 2:
            grad_keep[p][q] = block
        else:
            grad_send[p - pieces // 2, q] = block

    order.to_relative(meta, place, dot_left_t(act_ref[...], grad_ref[...]), scratch, store)


def gate_weight_call(meta, order, place, act, grad_gated):
    tokens, width = act.shape
    pieces, parts, low = order.batch_size, order.seq_size, order.shard_rows
    cols = width // 2
    outs = call(
        functools.partial(gate_weight_kernel, pieces, order, place),
        (4,),
        meta,
        [full_spec(act.shape), pl.BlockSpec((tokens, cols), lambda c, _: (0, c))],
        (act, grad_gated),
        [pl.BlockSpec((parts, low, cols), lambda c, _: (0, 0, c))] * (pieces // 2)
        + [pl.BlockSpec((pieces // 2, parts, low, cols), lambda c, _: (0, 0, 0, c))],
        [jax.ShapeDtypeStruct((parts, low, 2 * width), bf16)] * (pieces // 2)
        + [jax.ShapeDtypeStruct((pieces // 2, parts, low, 2 * width), bf16)],
        [pltpu.VMEM((width, cols), bf16)],
        4 * tokens * width * width,
        "gated_weight",
    )
    return outs[:-1], outs[-1]


def input_kernel(meta, moved_ref, x_ref, grad_resid_ref, perm_ref, out_ref):
    e = jnp.concatenate([moved_ref[d] for d in range(moved_ref.shape[0])], axis=1)
    e = dot_right_t(e, perm_ref[...])
    normed, scale = layer_stats(x_ref[0].astype(f32))
    out_ref[0] = (grad_resid_ref[0] + norm_back(e, normed, scale)).astype(bf16)


def input_call(meta, moved, x, grad_resid, perm):
    parts, _, chan = moved.shape
    micro, span, width = x.shape
    tile = lambda cols: pl.BlockSpec((1, span, cols), lambda m, _: (m, 0, 0))
    return call(
        input_kernel,
        (micro,),
        meta,
        [parted(parts, span, chan), tile(width), tile(width), full_spec(perm.shape)],
        (moved, x, grad_resid, perm),
        tile(width),
        jax.ShapeDtypeStruct((micro, span, width), bf16),
        [],
        2 * micro * span * width * width,
        "input_grad",
    )


def mode_tables(step_len, mode_count, length):
    order = jnp.arange(mode_count, dtype=f32)[:, None]
    rate = order * step_len

    def power(offsets):
        turns = 0.5 * rate[:, None, :] * offsets[None, :, None]
        angle = 2.0 * math.pi * (turns - jnp.round(turns))
        fading = jnp.exp(-0.5 * step_len[:, None, :] * offsets[None, :, None])
        return fading * jnp.cos(angle), fading * jnp.sin(angle)

    def outer(far, near):
        a, b = far[0][:, :, None], far[1][:, :, None]
        c, d = near[0][:, None], near[1][:, None]
        shape = (mode_count, far[0].shape[1] * near[0].shape[1], step_len.shape[-1])
        return (a * c - b * d).reshape(shape), (a * d + b * c).reshape(shape)

    ramp = jnp.arange(8, dtype=f32)
    near = outer(power(8.0 * ramp), power(ramp))
    far_count = length // near_span
    far = outer(
        power(8.0 * near_span * jnp.arange(far_count // 8, dtype=f32)), power(near_span * ramp)
    )

    def wave(scale):
        turns = scale * rate
        return 2.0 * math.pi * (turns - jnp.round(turns))

    decay = -0.5 * step_len
    turn_rate = math.pi * order
    step_im = jnp.exp(decay) * jnp.sin(wave(0.5))
    minus_one = jnp.expm1(decay) * jnp.cos(wave(0.5)) - 2.0 * jnp.sin(wave(0.25)) ** 2
    denominator = 0.25 + turn_rate**2
    input_mult = (
        (-0.5 * minus_one + step_im * turn_rate) / denominator,
        (-0.5 * step_im - minus_one * turn_rate) / denominator,
    )
    return near, far, input_mult


def cmul(a, b):
    return a[0] * b[0] - a[1] * b[1], a[0] * b[1] + a[1] * b[0]


def per_device(
    inputs,
    lengths,
    cotangent,
    norm1_gain,
    norm1_bias,
    step_size,
    state_out,
    skip_gain,
    glu_weight,
    glu_bias,
    norm2_gain,
    norm2_bias,
    ffn_in_weight,
    ffn_in_bias,
    ffn_out_weight,
    ffn_out_bias,
):
    micro, _, span, width = inputs.shape
    batch_size, seq_size = lax.axis_size("batch"), lax.axis_size("seq")
    batch_bits, seq_bits = bits_of(batch_size), bits_of(seq_size)
    devices = batch_size * seq_size
    shard_rows = width // devices
    chan = width // seq_size
    length = span * seq_size
    mode_count = state_out.shape[2]
    ff = ffn_in_weight.shape[1]
    me_b, me_s = lax.axis_index("batch"), lax.axis_index("seq")
    me = me_b * seq_size + me_s

    piece_ff = ff // batch_size
    place_at = 1 + micro
    in_table = 8
    out_table = in_table + devices
    base_table = out_table + seq_size
    column_table = base_table + batch_size
    chan_table = column_table + batch_size
    pieces = np.arange(batch_size)
    natural_piece = reverse_bits(pieces, batch_bits) ^ me_b
    piece_of = reverse_bits(jnp.arange(batch_size, dtype=jnp.int32) ^ me_b, batch_bits)

    def meta_of(parts):
        lengths, me_b, me_s = parts
        place = np.arange(devices)
        of_piece = reverse_bits(place // seq_size, batch_bits) ^ me_b
        of_seq = reverse_bits(place % seq_size, seq_bits) ^ me_s
        halves = np.concatenate([pieces[pieces % 2 == 0], pieces[pieces % 2 == 1]])
        of_group = reverse_bits(halves, batch_bits) ^ me_b
        table = jnp.concatenate(
            [
                of_piece * seq_size + of_seq,
                reverse_bits(np.arange(seq_size) ^ me_s, seq_bits),
                of_group * (piece_ff // ff_block_of(piece_ff)),
                of_group & (batch_size // 2 - 1),
                of_seq * batch_size + place // seq_size,
            ]
        )
        head = jnp.stack([me_s, *lengths[:, 0], me_s * span, me_b])
        blank = jnp.zeros((8 - head.shape[0],), jnp.int32)
        return jnp.concatenate([head, blank, table]).astype(jnp.int32)

    order = Rows(width, shard_rows, seq_size, batch_size, in_table)
    chan_order = Rows(width, shard_rows, seq_size, batch_size, chan_table, by_channel=True)

    x = inputs[:, 0]
    cot = cotangent[:, 0]

    top = batch_bits - 1
    half = batch_size // 2

    def over_low(pieces):
        for bit in reversed(range(top)):
            pieces = pieces + swap_batch(pieces, bit)
        return pieces

    def weave(low, high):
        return [piece for pair in zip(low, high) for piece in pair]

    def join(*parts):
        return jnp.concatenate(parts, axis=0)

    def near_swap(value):
        return swap(value, "seq", 1)

    def middle_swap(value):
        return swap(value, "seq", 2)

    def last_swap(value):
        return swap(value, "seq", seq_size // 2)

    def top_swap(value):
        return swap(value, "batch", 1 << top)

    counts = [2 * shard_rows, shard_rows, shard_rows, shard_rows, 4 * shard_rows]
    starts = [sum(counts[:k]) for k in range(len(counts))]
    small_size = sum(counts)
    in_1 = gather_first(ffn_in_weight)
    vectors = (norm1_gain, norm1_bias, skip_gain, step_size)
    vectors = vectors + (glu_bias, norm2_gain, norm2_bias, ffn_out_bias, ffn_in_bias)
    vectors = jnp.concatenate([v.reshape(-1, shard_rows) for v in vectors], axis=0)
    vectors = jnp.concatenate(gather_batch(vectors), axis=1)
    coefs = gather_batch(state_out)
    normed, perm = norm_call(
        me_b[None].astype(jnp.int32),
        x,
        jnp.pad(vectors[4:], ((0, 20 - vectors.shape[0]), (0, 0))),
        batch_bits,
        shard_rows,
        seq_size,
    )
    normed, in_1, one, coefs = together((normed, in_1, vectors[:4], coefs))
    in_w = gather_more(join(ffn_in_weight[None], in_1), 2)
    in_2 = middle_swap(in_w)
    glu_1 = gather_first(after(glu_weight, in_w))
    meta = meta_of(after((lengths, me_b, me_s), in_w))
    one = one.astype(f32)
    vec_one = jnp.concatenate([one[:3], jnp.zeros((5, chan), f32)], axis=0)
    coefs = jnp.concatenate(coefs, axis=1)
    coefs = jnp.swapaxes(coefs, 1, 2).astype(f32)
    near, far, input_mult = mode_tables(one[3:4], mode_count, length)
    joint = cmul(coefs, input_mult)
    lift = cmul((joint[0][:, None], joint[1][:, None]), far)
    fwd_np, inv_np = transform_tables(span)
    fwd, inv = jnp.asarray(fwd_np), jnp.asarray(inv_np)
    in_2, glu_1, lift, near = together((in_2, glu_1, lift, near))

    normed = exchange(normed)
    in_w = join(in_w, in_2)
    in_3 = near_swap(in_w)
    glu_w = gather_more(join(glu_weight[None], glu_1), 2)
    glu_2 = middle_swap(glu_w)
    spec = kernel_call(meta, after(lift, in_w, glu_w), near, fwd, seq_size, span)
    small_all = normed[:, micro * span :, :].astype(f32)
    small_all = small_all.reshape(seq_size, 16, batch_size, shard_rows)
    small_all = jnp.take(jnp.transpose(small_all, (2, 0, 1, 3)), piece_of, axis=0)
    glu_bias_all, gain_two, bias_two, out_bias, in_bias = [
        small_all[:, :, s : s + c].reshape(-1) for s, c in ((0, 2), (2, 1), (3, 1), (4, 1), (5, 4))
    ]
    vec_two = jnp.concatenate(
        [gain_two[None], bias_two[None], out_bias[None], jnp.zeros((5, width), f32)]
    )
    normed, in_3, glu_2, spec, ffn_out_weight, vec_two, glu_bias_all, in_bias = together(
        (normed, in_3, glu_2, spec, ffn_out_weight, vec_two, glu_bias_all, in_bias)
    )

    in_w = join(in_w, in_3).reshape(-1, ff)
    in_top = top_swap(in_w)
    glu_w = join(glu_w, glu_2)
    glu_3 = near_swap(glu_w)
    out_1 = gather_direct(ffn_out_weight)
    drive_spec, mixed, active_own = conv_call(
        meta, micro, normed, vec_one, after(spec, glu_w, in_w), fwd, inv
    )
    active_own, glu_3, out_1 = together((active_own, glu_3, out_1))

    active = exchange(active_own)
    out_w = gather_more(join(ffn_out_weight[None], *out_1), 1)
    out_3 = near_swap(out_w)
    glu_w = join(glu_w, after(glu_3, out_w)).reshape(-1, 2 * width)
    glu_top = top_swap(after(glu_w, in_top))
    in_parts = weave(over_low([in_w]), over_low([in_top]))
    glu_parts = weave(over_low([glu_w]), over_low([glu_top]))
    active, out_3, glu_parts = together((active, out_3, glu_parts))
    out_w = join(out_w, out_3).reshape(-1, width)
    out_top = top_swap(out_w)
    out_low = over_low([out_w])
    active = after(active, out_w)

    act, resid, gated, norm_two, norm_two_t, cot_out = gate_call(
        meta, chan_order, active, x, cot, vec_two, glu_bias_all[None], glu_parts
    )

    in_bias_blocks = in_bias.reshape(-1, 1, ff_block_of(piece_ff))

    def ffn_half(which, weights, **parts):
        return ffn_call(
            meta,
            order,
            out_table,
            place_at,
            base_table + which * half,
            column_table + which * half,
            cot_out,
            weights,
            **parts,
        )

    def low_rest(values):
        for bit in range(1, top):
            keep, send = values[: len(values) // 2], values[len(values) // 2 :]
            came = swap(jnp.stack([Sum(*v).total().astype(bf16) for v in send]), "batch", 1 << bit)
            values = [v + [came[i]] for i, v in enumerate(keep)]
        return values

    def low_sum(keep, came):
        return low_rest([[v, came[i]] for i, v in enumerate(keep)])

    def out_send(parts):
        return parts[half // 2][None] if half == 2 else jnp.stack(parts[half // 2 :])

    def rounded(terms):
        return Sum(*terms).total().astype(bf16)

    (back_a, bias_a), (out_a,), grad_out_a, keep_in_a, (send_in_a,) = ffn_half(
        0, out_low, norm=norm_two, bias=in_bias_blocks, w_in=in_parts, norm_t=norm_two_t
    )
    out_high = over_low([after(out_top, back_a)])
    in_a_came = swap(send_in_a, "batch", 1)
    out_a_came = swap(out_send(grad_out_a), "batch", 1)
    in_a_own, in_a_other = low_sum(keep_in_a, in_a_came)
    in_a_other = rounded(in_a_other)
    in_b_top = top_swap(in_a_other)
    (back_b, bias_b), (out_b,), grad_out_b, keep_in_b, (send_in_b,) = ffn_half(
        1,
        out_high,
        norm=after(norm_two, back_a, in_a_other),
        bias=in_bias_blocks,
        w_in=in_parts,
        norm_t=norm_two_t,
    )
    back_b, in_b_top, out_a_came = together((back_b, in_b_top, out_a_came))

    grad_resid, grad_gated, grad_glu_bias, sums, moved = gate_back_call(
        meta,
        chan_order,
        seq_size,
        [back_a, back_b],
        resid,
        gated,
        cot_out,
        vec_two,
        glu_parts,
    )
    grad_out_b, send_in_b = after((grad_out_b, send_in_b), moved)
    out_b_came = swap(out_send(grad_out_b), "batch", 1)
    in_b_came = swap(send_in_b, "batch", 1)

    grads_in = exchange(moved)
    (out_b_sum,) = low_sum(grad_out_b[: half // 2], out_b_came)
    out_b_sum = rounded(out_b_sum)
    out_a_top = top_swap(out_b_sum)
    keep_glu, send_glu = gate_weight_call(
        meta, chan_order, place_at, act, after(grad_gated, out_b_sum)
    )
    in_b_own, in_b_other = low_sum(keep_in_b, in_b_came)
    in_b_other = rounded([after(in_b_other[0], send_glu), *in_b_other[1:]])
    in_a_top = top_swap(in_b_other)
    sum_in_b = Sum(*in_b_own, in_b_top)
    in_b_near = sum_in_b.upper()
    in_b_near_came = near_swap(in_b_near)

    lower = (me_b >> top) == 0

    def halves(a, b, axis):
        return jnp.concatenate([jnp.where(lower, a, b), jnp.where(lower, b, a)], axis=axis)

    in_bias_sums = halves(bias_a.reshape(-1), bias_b.reshape(-1), 0)
    small_grads = jnp.concatenate(
        [
            value.reshape(devices, -1)
            for value in (grad_glu_bias[0], sums[1], sums[2], sums[0], in_bias_sums)
        ],
        axis=1,
    )
    small_grads = small_grads.reshape(batch_size, seq_size, -1)
    small_grads = jnp.moveaxis(small_grads, 1, 0).reshape(seq_size, -1)
    high = lax.reduce_precision(small_grads, 8, 7)
    rest = (small_grads - high).astype(bf16)
    extra_rows = -(-2 * small_grads.shape[1] // (16 * chan)) * 16
    blank = jnp.zeros((seq_size, extra_rows * chan - 2 * small_grads.shape[1]), bf16)
    extra = jnp.concatenate([high.astype(bf16), rest, blank], axis=1)
    extra = extra.reshape(seq_size, extra_rows, chan)
    (out_a_sum,) = low_sum(grad_out_a[: half // 2], out_a_came)
    out_a_sum = [v.reshape(seq_size, -1, width) for v in out_a_sum]
    grads_in, extra, out_a_sum, in_a_own, near, far, input_mult = together(
        (grads_in, extra, out_a_sum, in_a_own, near, far, input_mult)
    )

    moved_back, cross, state_sums = back_call(
        meta,
        after(grads_in, in_b_other, in_b_near),
        normed,
        drive_spec,
        mixed,
        vec_one,
        spec,
        fwd,
        inv,
        extra,
    )
    moved_back, cross, in_b_near_came, out_a_top = together(
        (moved_back, cross, in_b_near_came, out_a_top)
    )

    moved_back = exchange(moved_back)
    glu_came = swap(after(send_glu, cross), "batch", 1)
    sum_out = Sum(*out_a_sum, out_a_top.reshape(seq_size, -1, width))
    out_near = sum_out.upper()
    out_near_came = near_swap(out_near)
    sum_in_b.keep(after(in_b_near_came, out_near))
    in_b_middle = sum_in_b.upper()
    in_b_middle_came = middle_swap(in_b_middle)
    glu_own, glu_other = low_sum(keep_glu, after(glu_came, in_b_middle))
    glu_other = rounded(glu_other)
    glu_top_came = top_swap(glu_other)
    sum_in_a = Sum(*in_a_own, after(in_a_top, glu_other))
    in_a_near = sum_in_a.upper()
    in_a_near_came = near_swap(in_a_near)
    raw_modes = modes_call(meta, after(cross, in_a_near), far, near, inv)
    in_b_middle_came, in_a_near_came, out_near_came, glu_top_came = after(
        (in_b_middle_came, in_a_near_came, out_near_came, glu_top_came), raw_modes
    )
    sum_in_b.keep(in_b_middle_came)
    sum_in_b.middle()
    in_b_last = sum_in_b.upper()
    in_b_last_came = last_swap(in_b_last)
    sum_in_a.keep(after(in_a_near_came, in_b_last))
    in_a_middle = sum_in_a.upper()
    in_a_middle_came = middle_swap(in_a_middle)
    sum_glu = Sum(*glu_own, after(glu_top_came, in_a_middle))
    glu_near = sum_glu.upper()
    glu_near_came = near_swap(glu_near)
    sum_out.keep(after(out_near_came, glu_near))
    out_middle = sum_out.upper()
    out_middle_came = middle_swap(out_middle)

    input_grad = input_call(meta, after(moved_back, out_middle), x, grad_resid, perm)
    input_grad, in_a_middle_came, glu_near_came, out_middle_came = together(
        (input_grad, in_a_middle_came, glu_near_came, out_middle_came)
    )
    sum_out.keep(out_middle_came)
    sum_out.middle()
    out_last = sum_out.upper()
    out_last_came = last_swap(out_last)
    sum_glu.keep(after(glu_near_came, out_last))
    glu_middle = sum_glu.upper()
    glu_middle_came = middle_swap(glu_middle)
    sum_in_a.keep(after(in_a_middle_came, glu_middle))
    sum_in_a.middle()
    in_a_last = sum_in_a.upper()
    in_a_last_came = last_swap(in_a_last)
    sum_glu.keep(after(glu_middle_came, in_a_last))
    sum_glu.middle()
    glu_last = sum_glu.upper()
    glu_last_came = last_swap(glu_last)
    out_a, out_b, resid = after((out_a, out_b, resid), glu_last)
    output = resid + (out_a + out_b + vec_two[2:3]).reshape(resid.shape)
    output = output.astype(bf16)
    in_a_last_came, out_last_came, in_b_last_came = after(
        (in_a_last_came, out_last_came, in_b_last_came), output
    )
    raw_modes, state_sums = after((raw_modes, state_sums), input_grad)

    def finish(value, came):
        value.keep(came)
        return value.total()[0]

    z = cmul((raw_modes[0], raw_modes[1]), input_mult)
    state_grads = jnp.concatenate([z[0], -z[1], state_sums[:3]], axis=0).T
    state_grads = reduce_batch(state_grads.reshape(batch_size, shard_rows, -1))
    grad_state = jnp.stack([state_grads[:, :mode_count], state_grads[:, mode_count : 2 * mode_count]])
    grad_out_total = finish(sum_out, out_last_came)
    far_in = halves(finish(sum_in_a, in_a_last_came), finish(sum_in_b, in_b_last_came), 0)
    grad_in_total = jnp.concatenate([far_in[b] for b in range(batch_size)], axis=1)
    grad_glu_total = finish(sum_glu, glu_last_came)

    small_came = moved_back[:, micro * span :, :].reshape(seq_size, -1).astype(f32)
    small_came = jnp.sum(small_came, axis=0)
    size = batch_size * small_size
    small_came = (small_came[:size] + small_came[size : 2 * size]).reshape(batch_size, -1)
    own = reduce_batch(jnp.take(small_came, natural_piece, axis=0))
    grad_glu_bias_own, grad_gain_two, grad_bias_two, grad_out_bias, grad_in_bias_own = [
        own[s : s + c] for s, c in zip(starts, counts)
    ]

    return (
        output[:, None],
        input_grad[:, None],
        state_grads[:, 2 * mode_count + 1],
        state_grads[:, 2 * mode_count + 2],
        grad_state,
        state_grads[:, 2 * mode_count],
        grad_glu_total,
        grad_glu_bias_own,
        grad_gain_two,
        grad_bias_two,
        grad_in_total,
        grad_in_bias_own,
        grad_out_total,
        grad_out_bias,
    )


def solution(mesh):
    both = ("batch", "seq")
    rows = P(None, "batch", "seq", None)
    vector = P(both)
    matrix = P(both, None)
    state = P(None, both, None)
    return jax.shard_map(
        per_device,
        mesh=mesh,
        in_specs=(
            rows,
            P(None, "batch"),
            rows,
            vector,
            vector,
            vector,
            state,
            vector,
            matrix,
            vector,
            vector,
            vector,
            matrix,
            vector,
            matrix,
            vector,
        ),
        out_specs=(
            rows,
            rows,
            vector,
            vector,
            state,
            vector,
            matrix,
            vector,
            vector,
            vector,
            matrix,
            vector,
            matrix,
            vector,
        ),
        check_vma=False,
    )
```

```python
import functools
import math

import jax
import jax.numpy as jnp
import numpy as np
from jax import lax
from jax.experimental import pallas as pl
from jax.experimental.pallas import tpu as pltpu
from jax.sharding import PartitionSpec as P

f32 = jnp.float32
bf16 = jnp.bfloat16
norm_eps = 1e-05
near_span = 64
vmem_limit = 60 * 1024 * 1024
gelu_scale = math.sqrt(2.0 / math.pi)
gelu_cubic = 0.044715


def after(value, *tokens):
    return jax.tree.map(lambda v: lax.optimization_barrier((v, tokens))[0], value)


together = lax.optimization_barrier


def bits_of(size):
    count = size.bit_length() - 1
    if (1 << count) != size:
        raise ValueError("axis size")
    return count


def reverse_bits(value, count):
    result = 0
    for bit in range(count):
        result = result | (((value >> bit) & 1) << (count - 1 - bit))
    return result


def swap(value, axis, bit):
    size = lax.axis_size(axis)
    return lax.ppermute(value, axis, [(i, i ^ bit) for i in range(size)])


def gather_first(shard):
    return swap(shard[None], "seq", lax.axis_size("seq") // 2)


def gather_direct(shard):
    size = lax.axis_size("seq")
    return [swap(shard[None], "seq", bits) for bits in (size // 2, size // 4, size // 2 + size // 4)]


def gather_more(joined, lowest):
    size = lax.axis_size("seq")
    while joined.shape[0] << lowest < size:
        bit = size // joined.shape[0] // 2
        joined = jnp.concatenate([joined, swap(joined, "seq", bit)], axis=0)
    return joined


class Sum:
    def __init__(self, *terms):
        self.terms = list(terms)

    def total(self, start=0, stop=None):
        values = [term[start:stop].astype(f32) for term in self.terms]
        return functools.reduce(lambda a, b: a + b, values)

    def upper(self):
        return self.total(self.terms[0].shape[0] // 2).astype(bf16)

    def keep(self, came):
        half = self.terms[0].shape[0] // 2
        self.terms = [term[:half] for term in self.terms] + [came]

    def add(self, came):
        self.terms.append(came)

    def middle(self):
        for bit in range(2, bits_of(lax.axis_size("seq")) - 1):
            self.keep(swap(self.upper(), "seq", 1 << bit))


def swap_batch(pieces, bit):
    return [swap(piece, "batch", 1 << bit) for piece in pieces]


def gather_batch(part):
    pieces = [part]
    for bit in reversed(range(bits_of(lax.axis_size("batch")))):
        pieces = pieces + swap_batch(pieces, bit)
    return pieces


def reduce_batch(value):
    for bit in range(bits_of(lax.axis_size("batch"))):
        half = value.shape[0] // 2
        value = value[:half] + swap(value[half:], "batch", 1 << bit)
    return value[0]


def exchange(parts):
    return lax.all_to_all(parts, "seq", 0, 0)


def gelu_parts(values):
    square = values * values
    half = 0.5 * jnp.tanh(values * (gelu_scale + gelu_scale * gelu_cubic * square)) + 0.5
    return square, half


def gelu_value(values):
    return values * gelu_parts(values)[1]


def gelu_both(values):
    square, half = gelu_parts(values)
    value = values * half
    inner = 2.0 * gelu_scale + 6.0 * gelu_scale * gelu_cubic * square
    return value, half + value * (1.0 - half) * inner


def gelu_slope(values):
    return gelu_both(values)[1]


def layer_stats(values):
    centered = values - jnp.mean(values, axis=-1, keepdims=True)
    scale_inv = lax.rsqrt(jnp.mean(centered * centered, axis=-1, keepdims=True) + norm_eps)
    return centered * scale_inv, scale_inv


def norm_back(grad_normed, normed, scale_inv):
    first_mean = jnp.mean(grad_normed, axis=-1, keepdims=True)
    second_mean = jnp.mean(grad_normed * normed, axis=-1, keepdims=True)
    return scale_inv * (grad_normed - first_mean - normed * second_mean)


def dot(left, right):
    return jnp.dot(left, right, preferred_element_type=f32)


def dot_left_t(left, right):
    return lax.dot_general(left, right, (((0,), (0,)), ((), ())), preferred_element_type=f32)


def dot_right_t(left, right):
    return lax.dot_general(left, right, (((1,), (1,)), ((), ())), preferred_element_type=f32)


def stack_split(values):
    high = values.astype(bf16)
    low = (values - high.astype(f32)).astype(bf16)
    return jnp.concatenate([high, high, low], axis=0)


def table_split(table):
    high = table.astype(jnp.bfloat16)
    low = (table - high.astype(np.float64)).astype(jnp.bfloat16)
    return np.concatenate([high, low, high], axis=1)


def transform_tables(span):
    freqs = np.arange(span, dtype=np.float64) + 0.5
    phase = 2.0 * math.pi / (2 * span) * freqs[:, None] * np.arange(span, dtype=np.float64)[None]
    forward = np.concatenate([np.cos(phase), -np.sin(phase)], axis=0)
    backward = np.concatenate([np.cos(phase).T, -np.sin(phase).T], axis=1) / span
    return table_split(forward), table_split(backward)


def loop(count, body):
    if count <= 8:
        for index in range(count):
            body(index)
    else:
        lax.fori_loop(0, count, lambda index, carry: (body(index), carry)[1], 0)


def sum_loop(first, last, body, init):
    if isinstance(first, int) and isinstance(last, int):
        for index in range(first, last):
            init = body(index, init)
        return init
    return lax.fori_loop(first, last, body, init)


def full_spec(shape, buffered=True):
    zeros = (0,) * len(shape)
    if buffered:
        return pl.BlockSpec(shape, lambda *_: zeros, pipeline_mode=pl.Buffered(1))
    return pl.BlockSpec(shape, lambda *_: zeros)


def parted(parts, span, chan):
    return pl.BlockSpec((parts, span, chan), lambda m, _: (0, m, 0))


def call(kernel, grid, meta, in_specs, operands, out_specs, out_shape, scratch, flops, name):
    return pl.pallas_call(
        kernel,
        grid_spec=pltpu.PrefetchScalarGridSpec(
            num_scalar_prefetch=1,
            grid=grid,
            in_specs=in_specs,
            out_specs=out_specs,
            scratch_shapes=scratch,
        ),
        out_shape=out_shape,
        compiler_params=pltpu.CompilerParams(
            vmem_limit_bytes=vmem_limit, dimension_semantics=("arbitrary",) * len(grid)
        ),
        cost_estimate=pl.CostEstimate(
            flops=int(flops * 0.02), bytes_accessed=int(flops * 0.02 / 400), transcendentals=0
        ),
        name=name,
    )(meta, *operands)


def norm_kernel(batch_bits, shard_rows, seq_size, meta, x_ref, extra_ref, out_ref, perm_ref):
    width = x_ref.shape[2]
    chan = out_ref.shape[-1]

    @pl.when(pl.program_id(0) == 0)
    def _():
        lane = lax.broadcasted_iota(jnp.int32, (width, width), 1)
        piece = (lane & (chan - 1)) // shard_rows
        source = (
            (reverse_bits(piece, batch_bits) ^ meta[0]) * seq_size + lane // chan
        ) * shard_rows + (lane & (shard_rows - 1))
        row = lax.broadcasted_iota(jnp.int32, (width, width), 0)
        perm_ref[...] = jnp.where(row == source, 1.0, 0.0).astype(bf16)
        for d in range(out_ref.shape[0]):
            out_ref[d, pl.ds(out_ref.shape[1] - 16, 16), :] = extra_ref[...]

    span = x_ref.shape[1]
    rows = pl.ds(pl.multiple_of(pl.program_id(0) * span, span), span)
    normed, _ = layer_stats(x_ref[0].astype(f32))
    spread = dot(normed.astype(bf16), perm_ref[...]).astype(bf16)
    for d in range(out_ref.shape[0]):
        out_ref[d, rows, :] = spread[:, d * chan : (d + 1) * chan]


def norm_call(meta, x, extra, batch_bits, shard_rows, parts):
    micro, span, width = x.shape
    chan = width // parts
    return call(
        functools.partial(norm_kernel, batch_bits, shard_rows, parts),
        (micro,),
        meta,
        [pl.BlockSpec((1, span, width), lambda m, _: (m, 0, 0))]
        + [full_spec(extra.shape)],
        (x, extra),
        [full_spec((parts, micro * span + 16, chan)), full_spec((width, width))],
        [
            jax.ShapeDtypeStruct((parts, micro * span + 16, chan), bf16),
            jax.ShapeDtypeStruct((width, width), bf16),
        ],
        [],
        2 * micro * span * width * width,
        "norm_one",
    )


def kernel_kernel(meta, lift_re, lift_im, near_re, near_im, fwd_ref, out_ref, series, spec):
    modes, span_near, chan = near_re.shape
    far_count = lift_re.shape[1]
    blocks, _, span, _ = out_ref.shape
    group = 2

    def far_group(index, carry):
        def one_mode(n, acc):
            near_r, near_i = near_re[n], near_im[n]
            result = []
            for g in range(group):
                row = index * group + g
                a = lift_re[n, pl.ds(row, 1), :]
                b = lift_im[n, pl.ds(row, 1), :]
                result.append(acc[g] + (a * near_r - b * near_i))
            return tuple(result)

        zero = jnp.zeros((span_near, chan), f32)
        acc = lax.fori_loop(0, modes, one_mode, (zero,) * group, unroll=4)
        for g in range(group):
            start = pl.multiple_of((index * group + g) * span_near, span_near)
            series[pl.ds(start, span_near), :] = acc[g]
        return carry

    lax.fori_loop(0, far_count // group, far_group, 0)

    def one_pair(index):
        first = index * 2 * span
        pair = [series[pl.ds(first + k * span, span), :] for k in range(2)]
        both = dot(fwd_ref[...], stack_split(jnp.concatenate(pair, axis=1)))
        for k in range(2):
            spec[index * 2 + k] = both[:, k * chan : (k + 1) * chan]

    loop(blocks // 2, one_pair)
    rows = lax.broadcasted_iota(jnp.int32, (span, chan), 0)
    sign = 1.0 - 2.0 * (rows & 1).astype(f32)

    def one_block(d):
        real, imag = spec[d, :span], spec[d, span:]
        before = d - 1 if isinstance(d, int) else jnp.maximum(d - 1, 0)
        if isinstance(d, int) and d == 0:
            out_ref[0, 0], out_ref[0, 1] = real, imag
            return
        keep = 1.0 if isinstance(d, int) else jnp.where(d > 0, 1.0, 0.0)
        out_ref[d, 0] = real - keep * (sign * spec[before, span:])
        out_ref[d, 1] = imag + keep * (sign * spec[before, :span])

    loop(blocks, one_block)


def kernel_call(meta, lift, near, fwd, blocks, span):
    chan = near[0].shape[-1]
    operands = (lift[0], lift[1], near[0], near[1], fwd)
    return call(
        kernel_kernel,
        (1,),
        meta,
        [full_spec(a.shape) for a in operands],
        operands,
        full_spec((blocks, 2, span, chan)),
        jax.ShapeDtypeStruct((blocks, 2, span, chan), f32),
        [pltpu.VMEM((blocks * span, chan), f32), pltpu.VMEM((blocks, 2 * span, chan), f32)],
        1.1e10,
        "state_kernel",
    )


def mask_of(meta, m, block, span, chan):
    rows = block * span + lax.broadcasted_iota(jnp.int32, (span, chan), 0)
    return (rows < meta[1 + m]).astype(f32)


freq_tile = 64


def conv_kernel(
    meta,
    normed_ref,
    vec_ref,
    spec_ref,
    fwd_ref,
    inv_ref,
    drive_ref,
    mixed_ref,
    out_ref,
    drive,
    spectrum,
):
    m = pl.program_id(0)
    blocks, span, chan = drive.shape
    gain, bias, skip = vec_ref[0:1, :], vec_ref[1:2, :], vec_ref[2:3, :]

    def drive_pair(pair):
        values = []
        for k in range(2):
            block = 2 * pair + k
            normed = normed_ref[block].astype(f32)
            u = mask_of(meta, m, block, span, chan) * (normed * gain + bias)
            drive[block] = u
            values.append(u)
        both = dot(fwd_ref[...], stack_split(jnp.concatenate(values, axis=1)))
        for k in range(2):
            drive_ref[0, 2 * pair + k] = both[:, k * chan : (k + 1) * chan]

    loop(blocks // 2, drive_pair)

    def one_pair(index):
        for k in range(2):
            i = index * 2 + k

            def one_tile(tile, carry):
                low = pl.ds(pl.multiple_of(tile * freq_tile, freq_tile), freq_tile)
                high = pl.ds(pl.multiple_of(span + tile * freq_tile, freq_tile), freq_tile)

                def one_term(j, acc):
                    xr, xi = drive_ref[0, j, low], drive_ref[0, j, high]
                    gr, gi = spec_ref[i - j, 0, low], spec_ref[i - j, 1, low]
                    return (acc[0] + (xr * gr - xi * gi), acc[1] + (xr * gi + xi * gr))

                zero = jnp.zeros((freq_tile, chan), f32)
                acc = sum_loop(0, i + 1, one_term, (zero, zero))
                spectrum[k, low] = acc[0]
                spectrum[k, high] = acc[1]
                return carry

            lax.fori_loop(0, span // freq_tile, one_tile, 0, unroll=True)
        both = dot(
            inv_ref[...], stack_split(jnp.concatenate([spectrum[0], spectrum[1]], axis=1))
        )
        for k in range(2):
            i = index * 2 + k
            mixed = both[:, k * chan : (k + 1) * chan] + skip * drive[i]
            mixed_ref[0, i] = mixed
            out_ref[i] = gelu_value(mixed).astype(bf16)

    loop(blocks // 2, one_pair)


def conv_call(meta, micro, normed, vec, spec, fwd, inv):
    parts, _, chan = normed.shape
    span = spec.shape[2]
    wide = lambda rows: pl.BlockSpec((1, parts, rows, chan), lambda m, _: (m, 0, 0, 0))
    return call(
        conv_kernel,
        (micro,),
        meta,
        [parted(parts, span, chan)] + [full_spec(a.shape) for a in (vec, spec, fwd, inv)],
        (normed, vec, spec, fwd, inv),
        [wide(2 * span), wide(span), parted(parts, span, chan)],
        [
            jax.ShapeDtypeStruct((micro, parts, 2 * span, chan), f32),
            jax.ShapeDtypeStruct((micro, parts, span, chan), f32),
            jax.ShapeDtypeStruct((parts, micro * span, chan), bf16),
        ],
        [
            pltpu.VMEM((parts, span, chan), f32),
            pltpu.VMEM((2, 2 * span, chan), f32),
        ],
        1.5e10,
        "state_conv",
    )


def back_kernel(
    meta,
    grads_ref,
    normed_ref,
    drive_ref,
    mixed_ref,
    vec_ref,
    spec_ref,
    fwd_ref,
    inv_ref,
    extra_ref,
    out_ref,
    cross_ref,
    sums_ref,
    grad_mixed,
    grad_spec,
    spectrum,
):
    m = pl.program_id(0)
    blocks, span, chan = grad_mixed.shape
    gain, bias, skip = vec_ref[0:1, :], vec_ref[1:2, :], vec_ref[2:3, :]

    @pl.when(m == 0)
    def _():
        cross_ref[...] = jnp.zeros_like(cross_ref)
        sums_ref[...] = jnp.zeros_like(sums_ref)
        extra = extra_ref.shape[1]
        out_ref[:, pl.ds(out_ref.shape[1] - extra, extra), :] = extra_ref[...]

    def grad_pair(pair):
        values = []
        for k in range(2):
            block = 2 * pair + k
            normed = normed_ref[block].astype(f32)
            u = mask_of(meta, m, block, span, chan) * (normed * gain + bias)
            gm = grads_ref[block].astype(f32) * gelu_slope(mixed_ref[0, block])
            sums_ref[0:1, :] += jnp.sum(gm * u, axis=0, keepdims=True)
            grad_mixed[block] = gm
            values.append(gm)
        both = dot(fwd_ref[...], stack_split(jnp.concatenate(values, axis=1)))
        for k in range(2):
            grad_spec[2 * pair + k] = both[:, k * chan : (k + 1) * chan]

    loop(blocks // 2, grad_pair)

    def tiles_of(body):
        def one_tile(tile, carry):
            low = pl.ds(pl.multiple_of(tile * freq_tile, freq_tile), freq_tile)
            high = pl.ds(pl.multiple_of(span + tile * freq_tile, freq_tile), freq_tile)
            body(low, high)
            return carry

        lax.fori_loop(0, span // freq_tile, one_tile, 0, unroll=True)

    zero = jnp.zeros((freq_tile, chan), f32)

    def one_pair(index):
        for k in range(2):
            j = index * 2 + k

            def body(low, high):
                def one_term(i, acc):
                    mr, mi = grad_spec[i, low], grad_spec[i, high]
                    gr, gi = spec_ref[i - j, 0, low], spec_ref[i - j, 1, low]
                    return (acc[0] + (mr * gr + mi * gi), acc[1] + (mi * gr - mr * gi))

                acc = sum_loop(j, blocks, one_term, (zero, zero))
                spectrum[k, low] = acc[0]
                spectrum[k, high] = acc[1]

            tiles_of(body)
        both = dot(
            inv_ref[...], stack_split(jnp.concatenate([spectrum[0], spectrum[1]], axis=1))
        )
        for k in range(2):
            j = index * 2 + k
            grad_mixed[j] = both[:, k * chan : (k + 1) * chan] + skip * grad_mixed[j]

    loop(blocks // 2, one_pair)

    def finish(block):
        g = mask_of(meta, m, block, span, chan) * grad_mixed[block]
        normed = normed_ref[block].astype(f32)
        sums_ref[1:2, :] += jnp.sum(g * normed, axis=0, keepdims=True)
        sums_ref[2:3, :] += jnp.sum(g, axis=0, keepdims=True)
        out_ref[block, pl.ds(pl.multiple_of(m * span, span), span), :] = (g * gain).astype(bf16)

    loop(blocks, finish)

    def one_lag(d):
        def body(low, high):
            def one_term(j, acc):
                mr, mi = grad_spec[j + d, low], grad_spec[j + d, high]
                xr, xi = drive_ref[0, j, low], drive_ref[0, j, high]
                return (acc[0] + (mr * xr + mi * xi), acc[1] + (mi * xr - mr * xi))

            acc = sum_loop(0, blocks - d, one_term, (cross_ref[d, low], cross_ref[d, high]))
            cross_ref[d, low] = acc[0]
            cross_ref[d, high] = acc[1]

        tiles_of(body)

    loop(blocks, one_lag)


def back_call(meta, grads, normed, drive, mixed, vec, spec, fwd, inv, extra):
    parts, _, chan = normed.shape
    micro, _, span, _ = mixed.shape
    total = micro * span + extra.shape[1]
    mode = None if parts <= 8 else pl.Buffered(1)
    wide = lambda rows: pl.BlockSpec(
        (1, parts, rows, chan), lambda m, _: (m, 0, 0, 0), pipeline_mode=mode
    )
    return call(
        back_kernel,
        (micro,),
        meta,
        [parted(parts, span, chan)] * 2
        + [wide(2 * span), wide(span)]
        + [full_spec(a.shape) for a in (vec, spec, fwd, inv, extra)],
        (grads, normed, drive, mixed, vec, spec, fwd, inv, extra),
        [
            full_spec((parts, total, chan)),
            full_spec((parts, 2 * span, chan)),
            full_spec((8, chan)),
        ],
        [
            jax.ShapeDtypeStruct((parts, total, chan), bf16),
            jax.ShapeDtypeStruct((parts, 2 * span, chan), f32),
            jax.ShapeDtypeStruct((8, chan), f32),
        ],
        [
            pltpu.VMEM((parts, span, chan), f32),
            pltpu.VMEM((parts, 2 * span, chan), f32),
            pltpu.VMEM((2, 2 * span, chan), f32),
        ],
        2e10,
        "state_back",
    )


def modes_kernel(meta, cross_ref, far_re, far_im, near_re, near_im, inv_ref, out_ref, series):
    modes, span_near, chan = near_re.shape
    far_count = far_re.shape[1]
    blocks, double, _ = cross_ref.shape
    span = double // 2
    rows = lax.broadcasted_iota(jnp.int32, (span, chan), 0)
    sign = 1.0 - 2.0 * (rows & 1).astype(f32)

    def one_pair(index):
        pair = []
        for k in range(2):
            d = index * 2 + k
            real, imag = cross_ref[d, :span], cross_ref[d, span:]
            if isinstance(d, int):
                keep = 1.0 if d + 1 < blocks else 0.0
                after = min(d + 1, blocks - 1)
            else:
                keep = jnp.where(d + 1 < blocks, 1.0, 0.0)
                after = jnp.minimum(d + 1, blocks - 1)
            real = real + keep * (sign * cross_ref[after, span:])
            imag = imag - keep * (sign * cross_ref[after, :span])
            pair.append(jnp.concatenate([real, imag], axis=0))
        both = dot(inv_ref[...], stack_split(jnp.concatenate(pair, axis=1)))
        for k in range(2):
            series[pl.ds((index * 2 + k) * span, span), :] = both[:, k * chan : (k + 1) * chan]

    loop(blocks // 2, one_pair)
    group = 2

    def mode_group(index, carry):
        def one_far(i, acc):
            values = series[pl.ds(pl.multiple_of(i * span_near, span_near), span_near), :]
            result = []
            for g in range(group):
                n = index * group + g
                a = far_re[n, pl.ds(i, 1), :]
                b = far_im[n, pl.ds(i, 1), :]
                result.append((acc[g][0] + a * values, acc[g][1] + b * values))
            return tuple(result)

        zero = jnp.zeros((span_near, chan), f32)
        acc = lax.fori_loop(0, far_count, one_far, ((zero, zero),) * group, unroll=4)
        for g in range(group):
            n = index * group + g
            near_r, near_i = near_re[n], near_im[n]
            re, im = acc[g]
            out_ref[0, pl.ds(n, 1), :] = jnp.sum(re * near_r - im * near_i, axis=0, keepdims=True)
            out_ref[1, pl.ds(n, 1), :] = jnp.sum(re * near_i + im * near_r, axis=0, keepdims=True)
        return carry

    lax.fori_loop(0, modes // group, mode_group, 0)


def modes_call(meta, cross, far, near, inv):
    modes, _, chan = near[0].shape
    blocks, double, _ = cross.shape
    operands = (cross, far[0], far[1], near[0], near[1], inv)
    return call(
        modes_kernel,
        (1,),
        meta,
        [full_spec(a.shape) for a in operands],
        operands,
        full_spec((2, modes, chan)),
        jax.ShapeDtypeStruct((2, modes, chan), f32),
        [pltpu.VMEM((blocks * double // 2, chan), f32)],
        1.1e10,
        "state_modes",
    )


class Rows:
    def __init__(self, width, shard_rows, seq_size, batch_size, table, by_channel=False):
        self.width = width
        self.shard_rows = shard_rows
        self.seq_size = seq_size
        self.batch_size = batch_size
        self.table = table
        self.piece_rows = shard_rows * seq_size
        self.by_block = shard_rows % 16 == 0
        self.by_channel = by_channel

    def natural(self, meta, p, q):
        start = meta[self.table + p * self.seq_size + q] * self.shard_rows
        return pl.ds(pl.multiple_of(start, self.shard_rows), self.shard_rows)

    def order(self, meta, place):
        shape = (self.width, self.width)
        relative = lax.broadcasted_iota(jnp.int32, shape, 0)
        piece = relative // self.piece_rows
        position = (relative % self.piece_rows) // self.shard_rows
        seq = reverse_bits(position, bits_of(self.seq_size)) ^ meta[0]
        if self.by_channel:
            shard = seq * self.batch_size + piece
        else:
            batch = reverse_bits(piece, bits_of(self.batch_size)) ^ meta[place + 1]
            shard = batch * self.seq_size + seq
        source = shard * self.shard_rows + relative % self.shard_rows
        return jnp.where(lax.broadcasted_iota(jnp.int32, shape, 1) == source, 1.0, 0.0).astype(bf16)

    def to_natural(self, meta, place, parts, target):
        if self.by_block:
            for p, part in enumerate(parts):
                for q in range(self.seq_size):
                    target[self.natural(meta, p, q), :] = part[
                        pl.ds(q * self.shard_rows, self.shard_rows), :
                    ]
        else:
            whole = jnp.concatenate([part[...] for part in parts], axis=0)
            target[...] = dot_left_t(self.order(meta, place), whole).astype(bf16)

    def to_relative(self, meta, place, value, scratch, store):
        if self.by_block:
            scratch[...] = value.astype(bf16)
        else:
            moved = dot(self.order(meta, place), value.astype(bf16))
        for p in range(self.batch_size):
            for q in range(self.seq_size):
                if self.by_block:
                    block = scratch[self.natural(meta, p, q), :]
                else:
                    start = (p * self.seq_size + q) * self.shard_rows
                    block = moved[start : start + self.shard_rows].astype(bf16)
                store(p, q, block)


def gate_kernel(pieces, order, meta, *refs):
    active_ref, x_ref, cot_ref, vec_ref, glu_bias_ref = refs[:5]
    weights = refs[5 : 5 + pieces]
    act_ref, resid_ref, gated_ref, norm_ref, norm_t_ref, cot_out, weight_scr = refs[5 + pieces :]
    m = pl.program_id(0)
    _, span, width = x_ref.shape
    micro = pl.num_programs(0)

    @pl.when(m == 0)
    def _():
        order.to_natural(meta, 1 + micro, weights, weight_scr)

    act = jnp.concatenate([active_ref[d] for d in range(active_ref.shape[0])], axis=1)
    act_ref[...] = act
    gated = dot(act, weight_scr[...]) + glu_bias_ref[...]
    gated_ref[0] = gated
    residual = x_ref[0].astype(f32) + gated[:, :width] * jax.nn.sigmoid(gated[:, width:])
    resid_ref[0] = residual
    normed, _ = layer_stats(residual)
    norm_two = (normed * vec_ref[0:1, :] + vec_ref[1:2, :]).astype(bf16)
    norm_ref[...] = norm_two
    norm_t_ref[...] = norm_two.T
    rows = meta[1 + micro] + lax.broadcasted_iota(jnp.int32, (span, width), 0)
    cot_out[...] = jnp.where(rows < meta[1 + m], cot_ref[0].astype(f32), 0.0).astype(bf16)


def gate_call(meta, order, active, x, cot, vec, glu_bias, weights):
    parts, _, chan = active.shape
    pieces = len(weights)
    micro, span, width = x.shape
    tokens = micro * span
    tile = lambda cols: pl.BlockSpec((1, span, cols), lambda m, _: (m, 0, 0))
    flat = pl.BlockSpec((span, width), lambda m, _: (m, 0))
    return call(
        functools.partial(gate_kernel, pieces, order),
        (micro,),
        meta,
        [parted(parts, span, chan), tile(width), tile(width)]
        + [full_spec(a.shape) for a in (vec, glu_bias, *weights)],
        (active, x, cot, vec, glu_bias, *weights),
        [
            flat,
            tile(width),
            tile(2 * width),
            flat,
            pl.BlockSpec((width, span), lambda m, _: (0, m)),
            flat,
        ],
        [
            jax.ShapeDtypeStruct((tokens, width), bf16),
            jax.ShapeDtypeStruct((micro, span, width), f32),
            jax.ShapeDtypeStruct((micro, span, 2 * width), f32),
            jax.ShapeDtypeStruct((tokens, width), bf16),
            jax.ShapeDtypeStruct((width, tokens), bf16),
            jax.ShapeDtypeStruct((tokens, width), bf16),
        ],
        [pltpu.VMEM((width, 2 * width), bf16)],
        6 * tokens * width * width,
        "gated_unit",
    )


def ff_block_of(piece_ff):
    return min(1024, piece_ff)


def ffn_kernel(pieces, batch_pieces, sub, order, out_table, place, first, second, meta, *refs):
    refs = list(refs)
    take = lambda count: [refs.pop(0) for _ in range(count)]
    half = batch_pieces // 2
    (cot_ref,) = take(1)
    w_out = take(pieces)
    if first:
        norm_ref, bias_ref = take(2)
        w_in = take(batch_pieces)
    else:
        spread_ref, hidden_ref = take(2)
    if second:
        (norm_t_ref,) = take(1)
    if first:
        back_ref, grad_bias = take(2)
        if not second:
            spread_ref, hidden_ref = take(2)
    if second:
        (out_ref,) = take(1)
        grad_out, grad_in = take(pieces), take(half)
        (grad_in_send,) = take(1)
    (out_scr,) = take(1)
    if first:
        (in_scr,) = take(1)
    if second:
        (grad_in_scr,) = take(1)
    k = pl.program_id(0)
    s = pl.program_id(1)
    ff_block = out_scr.shape[0]
    subs = ff_block // sub
    start = jnp.logical_and(k == 0, s == 0)

    def sub_rows(t):
        return pl.ds(pl.multiple_of(meta[out_table + s * subs + t] * sub, sub), sub)

    for piece in range(pieces):

        @pl.when(k == piece)
        def _():
            for t in range(subs):
                out_scr[pl.ds(t * sub, sub), :] = w_out[piece][sub_rows(t), :]

    def accumulate(ref, part):
        @pl.when(start)
        def _():
            ref[...] = part

        @pl.when(jnp.logical_not(start))
        def _():
            ref[...] += part

    if first:
        order.to_natural(meta, place, w_in, in_scr)
        hidden = dot(norm_ref[...], in_scr[...]) + bias_ref[0]
        spread, slope = gelu_both(hidden)
        spread = spread.astype(bf16)
        grad_hidden = (dot_right_t(cot_ref[...], out_scr[...]) * slope).astype(bf16)
        grad_bias[0] = jnp.sum(grad_hidden.astype(f32), axis=0, keepdims=True)
        if not second:
            spread_ref[...] = spread
            hidden_ref[...] = grad_hidden
        accumulate(back_ref, dot_right_t(grad_hidden, in_scr[...]))
    else:
        spread, grad_hidden = spread_ref[...], hidden_ref[...]

    if second:
        accumulate(out_ref, dot(spread, out_scr[...]))

        def store(p, q, block):
            if p < half:
                grad_in[p][q, 0] = block
            else:
                grad_in_send[p - half, q, 0] = block

        order.to_relative(meta, place, dot(norm_t_ref[...], grad_hidden), grad_in_scr, store)
        part = dot_left_t(spread, cot_ref[...]).astype(bf16)
        for piece in range(pieces):

            @pl.when(k == piece)
            def _():
                for t in range(subs):
                    grad_out[piece][sub_rows(t), :] = part[t * sub : (t + 1) * sub, :]


def ffn_call(meta, order, out_table, place, base, column, cot, w_out, norm=None, bias=None, w_in=None, norm_t=None, kept=None):
    first, second = norm is not None, norm_t is not None
    pieces, batch_pieces = len(w_out), order.batch_size
    tokens, width = cot.shape
    piece_ff = w_out[0].shape[0]
    ff_block = ff_block_of(piece_ff)
    steps = piece_ff // ff_block
    sub = piece_ff // order.seq_size
    rows = order.piece_rows
    half = batch_pieces // 2
    seq_size, low = order.seq_size, order.shard_rows
    block = lambda k, s, meta: meta[base + k] + s
    wide = full_spec((tokens, width))
    step_columns = pl.BlockSpec((tokens, ff_block), lambda k, s, meta: (0, k * steps + s))
    activations = jax.ShapeDtypeStruct((tokens, pieces * piece_ff), bf16)
    total = jax.ShapeDtypeStruct((tokens, width), f32)
    operands = [cot, *w_out]
    in_specs = [wide] + [full_spec(a.shape) for a in w_out]
    outs, out_specs, scratch = [], [], [pltpu.VMEM((ff_block, width), bf16)]
    if first:
        operands += [norm, bias, *w_in]
        in_specs += [wide]
        in_specs += [pl.BlockSpec((1, 1, ff_block), lambda k, s, meta: (block(k, s, meta), 0, 0))]
        in_specs += [
            pl.BlockSpec((rows, ff_block), lambda k, s, meta: (0, block(k, s, meta)))
            for _ in w_in
        ]
        outs += [total, jax.ShapeDtypeStruct((pieces * steps, 1, ff_block), f32)]
        out_specs += [wide]
        out_specs += [
            pl.BlockSpec((1, 1, ff_block), lambda k, s, meta: (meta[column + k] * steps + s, 0, 0))
        ]
        scratch += [pltpu.VMEM((width, ff_block), bf16)]
        if not second:
            outs += [activations] * 2
            out_specs += [step_columns] * 2
    else:
        operands += kept
        in_specs += [step_columns] * 2
    if second:
        operands += [norm_t]
        in_specs += [full_spec(norm_t.shape)]
        outs += [total] + [jax.ShapeDtypeStruct(a.shape, bf16) for a in w_out]
        outs += [jax.ShapeDtypeStruct((seq_size, pieces, low, piece_ff), bf16)] * half
        outs += [jax.ShapeDtypeStruct((half, seq_size, pieces, low, piece_ff), bf16)]
        out_specs += [wide] + [full_spec(a.shape) for a in w_out]
        out_specs += [
            pl.BlockSpec((seq_size, 1, low, ff_block), lambda k, s, meta: (0, meta[column + k], 0, s))
        ] * half
        out_specs += [
            pl.BlockSpec(
                (half, seq_size, 1, low, ff_block),
                lambda k, s, meta: (0, 0, meta[column + k], 0, s),
            )
        ]
        scratch += [pltpu.VMEM((width, ff_block), bf16)]
    results = call(
        functools.partial(
            ffn_kernel, pieces, batch_pieces, sub, order, out_table, place, first, second
        ),
        (pieces, steps),
        meta,
        in_specs,
        operands,
        out_specs,
        outs,
        scratch,
        6 * (first + second) * tokens * width * piece_ff * pieces,
        "feed_forward",
    )
    head = results[: 2 * first + 2 * (first and not second)]
    tail = results[len(head) :]
    return head, tail[:1], tail[1 : 1 + pieces], tail[1 + pieces : -1], tail[-1:]


def gate_back_kernel(pieces, halves, order, meta, *refs):
    back = refs[:halves]
    resid_ref, gated_ref, cot_ref, vec_ref = refs[halves : halves + 4]
    weights = refs[halves + 4 : halves + 4 + pieces]
    rest = refs[halves + 4 + pieces :]
    grad_resid_ref, grad_gated_ref, glu_bias_ref, sums_ref, moved_ref, weight_scr = rest
    m = pl.program_id(0)
    count = pl.num_programs(0)
    width = cot_ref.shape[1]

    @pl.when(m == 0)
    def _():
        glu_bias_ref[...] = jnp.zeros_like(glu_bias_ref)
        sums_ref[...] = jnp.zeros_like(sums_ref)
        order.to_natural(meta, 1 + count, weights, weight_scr)

    residual = resid_ref[0]
    grad_norm = back[0][...]
    for h in range(1, halves):
        grad_norm = grad_norm + back[h][...]
    grad_out = cot_ref[...].astype(f32)
    normed, scale = layer_stats(residual)
    sums_ref[0:1, :] += jnp.sum(grad_out, axis=0, keepdims=True)
    sums_ref[1:2, :] += jnp.sum(grad_norm * normed, axis=0, keepdims=True)
    sums_ref[2:3, :] += jnp.sum(grad_norm, axis=0, keepdims=True)
    grad_resid = grad_out + norm_back(grad_norm * vec_ref[0:1, :], normed, scale)
    grad_resid_ref[0] = grad_resid
    gated = gated_ref[0]
    gate = jax.nn.sigmoid(gated[:, width:])
    grad_left = grad_resid * gate
    grad_right = grad_left * gated[:, :width] * (1.0 - gate)
    grad_gated = jnp.concatenate([grad_left, grad_right], axis=1).astype(bf16)
    grad_gated_ref[...] = grad_gated
    glu_bias_ref[0:1, :] += jnp.sum(grad_gated.astype(f32), axis=0, keepdims=True)
    moved = dot_right_t(grad_gated, weight_scr[...]).astype(bf16)
    chan = moved_ref.shape[-1]
    for d in range(moved_ref.shape[0]):
        moved_ref[d] = moved[:, d * chan : (d + 1) * chan]


def gate_back_call(meta, order, parts, back, resid, gated, cot, vec, weights):
    halves, pieces = len(back), len(weights)
    micro, span, width = resid.shape
    tokens = micro * span
    chan = width // parts
    tile = lambda cols: pl.BlockSpec((1, span, cols), lambda m, _: (m, 0, 0))
    flat = lambda cols: pl.BlockSpec((span, cols), lambda m, _: (m, 0))
    return call(
        functools.partial(gate_back_kernel, pieces, halves, order),
        (micro,),
        meta,
        [flat(width)] * halves
        + [tile(width), tile(2 * width), flat(width)]
        + [full_spec(a.shape) for a in (vec, *weights)],
        (*back, resid, gated, cot, vec, *weights),
        [
            tile(width),
            flat(2 * width),
            full_spec((8, 2 * width)),
            full_spec((8, width)),
            parted(parts, span, chan),
        ],
        [
            jax.ShapeDtypeStruct((micro, span, width), f32),
            jax.ShapeDtypeStruct((tokens, 2 * width), bf16),
            jax.ShapeDtypeStruct((8, 2 * width), f32),
            jax.ShapeDtypeStruct((8, width), f32),
            jax.ShapeDtypeStruct((parts, micro * span, chan), bf16),
        ],
        [pltpu.VMEM((width, 2 * width), bf16)],
        4 * tokens * width * width,
        "gated_back",
    )


def gate_weight_kernel(pieces, order, place, meta, act_ref, grad_ref, *refs):
    grad_keep, grad_send, scratch = refs[: pieces // 2], refs[-2], refs[-1]

    def store(p, q, block):
        if p < pieces // 2:
            grad_keep[p][q] = block
        else:
            grad_send[p - pieces // 2, q] = block

    order.to_relative(meta, place, dot_left_t(act_ref[...], grad_ref[...]), scratch, store)


def gate_weight_call(meta, order, place, act, grad_gated):
    tokens, width = act.shape
    pieces, parts, low = order.batch_size, order.seq_size, order.shard_rows
    cols = width // 2
    outs = call(
        functools.partial(gate_weight_kernel, pieces, order, place),
        (4,),
        meta,
        [full_spec(act.shape), pl.BlockSpec((tokens, cols), lambda c, _: (0, c))],
        (act, grad_gated),
        [pl.BlockSpec((parts, low, cols), lambda c, _: (0, 0, c))] * (pieces // 2)
        + [pl.BlockSpec((pieces // 2, parts, low, cols), lambda c, _: (0, 0, 0, c))],
        [jax.ShapeDtypeStruct((parts, low, 2 * width), bf16)] * (pieces // 2)
        + [jax.ShapeDtypeStruct((pieces // 2, parts, low, 2 * width), bf16)],
        [pltpu.VMEM((width, cols), bf16)],
        4 * tokens * width * width,
        "gated_weight",
    )
    return outs[:-1], outs[-1]


def input_kernel(meta, moved_ref, x_ref, grad_resid_ref, perm_ref, out_ref):
    e = jnp.concatenate([moved_ref[d] for d in range(moved_ref.shape[0])], axis=1)
    e = dot_right_t(e, perm_ref[...])
    normed, scale = layer_stats(x_ref[0].astype(f32))
    out_ref[0] = (grad_resid_ref[0] + norm_back(e, normed, scale)).astype(bf16)


def input_call(meta, moved, x, grad_resid, perm):
    parts, _, chan = moved.shape
    micro, span, width = x.shape
    tile = lambda cols: pl.BlockSpec((1, span, cols), lambda m, _: (m, 0, 0))
    return call(
        input_kernel,
        (micro,),
        meta,
        [parted(parts, span, chan), tile(width), tile(width), full_spec(perm.shape)],
        (moved, x, grad_resid, perm),
        tile(width),
        jax.ShapeDtypeStruct((micro, span, width), bf16),
        [],
        2 * micro * span * width * width,
        "input_grad",
    )


def mode_tables(step_len, mode_count, length):
    order = jnp.arange(mode_count, dtype=f32)[:, None]
    rate = order * step_len

    def power(offsets):
        turns = 0.5 * rate[:, None, :] * offsets[None, :, None]
        angle = 2.0 * math.pi * (turns - jnp.round(turns))
        fading = jnp.exp(-0.5 * step_len[:, None, :] * offsets[None, :, None])
        return fading * jnp.cos(angle), fading * jnp.sin(angle)

    def outer(far, near):
        a, b = far[0][:, :, None], far[1][:, :, None]
        c, d = near[0][:, None], near[1][:, None]
        shape = (mode_count, far[0].shape[1] * near[0].shape[1], step_len.shape[-1])
        return (a * c - b * d).reshape(shape), (a * d + b * c).reshape(shape)

    ramp = jnp.arange(8, dtype=f32)
    near = outer(power(8.0 * ramp), power(ramp))
    far_count = length // near_span
    far = outer(
        power(8.0 * near_span * jnp.arange(far_count // 8, dtype=f32)), power(near_span * ramp)
    )

    def wave(scale):
        turns = scale * rate
        return 2.0 * math.pi * (turns - jnp.round(turns))

    decay = -0.5 * step_len
    turn_rate = math.pi * order
    step_im = jnp.exp(decay) * jnp.sin(wave(0.5))
    minus_one = jnp.expm1(decay) * jnp.cos(wave(0.5)) - 2.0 * jnp.sin(wave(0.25)) ** 2
    denominator = 0.25 + turn_rate**2
    input_mult = (
        (-0.5 * minus_one + step_im * turn_rate) / denominator,
        (-0.5 * step_im - minus_one * turn_rate) / denominator,
    )
    return near, far, input_mult


def cmul(a, b):
    return a[0] * b[0] - a[1] * b[1], a[0] * b[1] + a[1] * b[0]


def per_device(
    inputs,
    lengths,
    cotangent,
    norm1_gain,
    norm1_bias,
    step_size,
    state_out,
    skip_gain,
    glu_weight,
    glu_bias,
    norm2_gain,
    norm2_bias,
    ffn_in_weight,
    ffn_in_bias,
    ffn_out_weight,
    ffn_out_bias,
):
    micro, _, span, width = inputs.shape
    batch_size, seq_size = lax.axis_size("batch"), lax.axis_size("seq")
    batch_bits, seq_bits = bits_of(batch_size), bits_of(seq_size)
    devices = batch_size * seq_size
    shard_rows = width // devices
    chan = width // seq_size
    length = span * seq_size
    mode_count = state_out.shape[2]
    ff = ffn_in_weight.shape[1]
    me_b, me_s = lax.axis_index("batch"), lax.axis_index("seq")
    me = me_b * seq_size + me_s

    piece_ff = ff // batch_size
    place_at = 1 + micro
    in_table = 8
    out_table = in_table + devices
    base_table = out_table + seq_size
    column_table = base_table + batch_size
    chan_table = column_table + batch_size
    pieces = np.arange(batch_size)
    natural_piece = reverse_bits(pieces, batch_bits) ^ me_b
    piece_of = reverse_bits(jnp.arange(batch_size, dtype=jnp.int32) ^ me_b, batch_bits)

    def meta_of(parts):
        lengths, me_b, me_s = parts
        place = np.arange(devices)
        of_piece = reverse_bits(place // seq_size, batch_bits) ^ me_b
        of_seq = reverse_bits(place % seq_size, seq_bits) ^ me_s
        halves = np.concatenate([pieces[pieces % 2 == 0], pieces[pieces % 2 == 1]])
        of_group = reverse_bits(halves, batch_bits) ^ me_b
        table = jnp.concatenate(
            [
                of_piece * seq_size + of_seq,
                reverse_bits(np.arange(seq_size) ^ me_s, seq_bits),
                of_group * (piece_ff // ff_block_of(piece_ff)),
                of_group & (batch_size // 2 - 1),
                of_seq * batch_size + place // seq_size,
            ]
        )
        head = jnp.stack([me_s, *lengths[:, 0], me_s * span, me_b])
        blank = jnp.zeros((8 - head.shape[0],), jnp.int32)
        return jnp.concatenate([head, blank, table]).astype(jnp.int32)

    order = Rows(width, shard_rows, seq_size, batch_size, in_table)
    chan_order = Rows(width, shard_rows, seq_size, batch_size, chan_table, by_channel=True)

    x = inputs[:, 0]
    cot = cotangent[:, 0]

    top = batch_bits - 1
    half = batch_size // 2

    def over_low(pieces):
        for bit in reversed(range(top)):
            pieces = pieces + swap_batch(pieces, bit)
        return pieces

    def weave(low, high):
        return [piece for pair in zip(low, high) for piece in pair]

    def join(*parts):
        return jnp.concatenate(parts, axis=0)

    def near_swap(value):
        return swap(value, "seq", 1)

    def middle_swap(value):
        return swap(value, "seq", 2)

    def last_swap(value):
        return swap(value, "seq", seq_size // 2)

    def top_swap(value):
        return swap(value, "batch", 1 << top)

    counts = [2 * shard_rows, shard_rows, shard_rows, shard_rows, 4 * shard_rows]
    starts = [sum(counts[:k]) for k in range(len(counts))]
    small_size = sum(counts)
    in_1 = gather_first(ffn_in_weight)
    vectors = (norm1_gain, norm1_bias, skip_gain, step_size)
    vectors = vectors + (glu_bias, norm2_gain, norm2_bias, ffn_out_bias, ffn_in_bias)
    vectors = jnp.concatenate([v.reshape(-1, shard_rows) for v in vectors], axis=0)
    vectors = jnp.concatenate(gather_batch(vectors), axis=1)
    coefs = gather_batch(state_out)
    normed, perm = norm_call(
        me_b[None].astype(jnp.int32),
        x,
        jnp.pad(vectors[4:], ((0, 20 - vectors.shape[0]), (0, 0))),
        batch_bits,
        shard_rows,
        seq_size,
    )
    normed, in_1, one, coefs = together((normed, in_1, vectors[:4], coefs))
    in_w = gather_more(join(ffn_in_weight[None], in_1), 2)
    in_2 = middle_swap(in_w)
    glu_1 = gather_first(after(glu_weight, in_w))
    meta = meta_of(after((lengths, me_b, me_s), in_w))
    one = one.astype(f32)
    vec_one = jnp.concatenate([one[:3], jnp.zeros((5, chan), f32)], axis=0)
    coefs = jnp.concatenate(coefs, axis=1)
    coefs = jnp.swapaxes(coefs, 1, 2).astype(f32)
    near, far, input_mult = mode_tables(one[3:4], mode_count, length)
    joint = cmul(coefs, input_mult)
    lift = cmul((joint[0][:, None], joint[1][:, None]), far)
    fwd_np, inv_np = transform_tables(span)
    fwd, inv = jnp.asarray(fwd_np), jnp.asarray(inv_np)
    in_2, glu_1, lift, near = together((in_2, glu_1, lift, near))

    normed = exchange(normed)
    in_w = join(in_w, in_2)
    in_3 = near_swap(in_w)
    glu_w = gather_more(join(glu_weight[None], glu_1), 2)
    glu_2 = middle_swap(glu_w)
    spec = kernel_call(meta, after(lift, in_w, glu_w), near, fwd, seq_size, span)
    small_all = normed[:, micro * span :, :].astype(f32)
    small_all = small_all.reshape(seq_size, 16, batch_size, shard_rows)
    small_all = jnp.take(jnp.transpose(small_all, (2, 0, 1, 3)), piece_of, axis=0)
    glu_bias_all, gain_two, bias_two, out_bias, in_bias = [
        small_all[:, :, s : s + c].reshape(-1) for s, c in ((0, 2), (2, 1), (3, 1), (4, 1), (5, 4))
    ]
    vec_two = jnp.concatenate(
        [gain_two[None], bias_two[None], out_bias[None], jnp.zeros((5, width), f32)]
    )
    normed, in_3, glu_2, spec, ffn_out_weight, vec_two, glu_bias_all, in_bias = together(
        (normed, in_3, glu_2, spec, ffn_out_weight, vec_two, glu_bias_all, in_bias)
    )

    in_w = join(in_w, in_3).reshape(-1, ff)
    in_top = top_swap(in_w)
    glu_w = join(glu_w, glu_2)
    glu_3 = near_swap(glu_w)
    out_1 = gather_direct(ffn_out_weight)
    drive_spec, mixed, active_own = conv_call(
        meta, micro, normed, vec_one, after(spec, glu_w, in_w), fwd, inv
    )
    active_own, glu_3, out_1 = together((active_own, glu_3, out_1))

    active = exchange(active_own)
    out_w = gather_more(join(ffn_out_weight[None], *out_1), 1)
    out_3 = near_swap(out_w)
    glu_w = join(glu_w, after(glu_3, out_w)).reshape(-1, 2 * width)
    glu_top = top_swap(after(glu_w, in_top))
    in_parts = weave(over_low([in_w]), over_low([in_top]))
    glu_parts = weave(over_low([glu_w]), over_low([glu_top]))
    active, out_3, glu_parts = together((active, out_3, glu_parts))
    out_w = join(out_w, out_3).reshape(-1, width)
    out_top = top_swap(out_w)
    out_low = over_low([out_w])
    active = after(active, out_w)

    act, resid, gated, norm_two, norm_two_t, cot_out = gate_call(
        meta, chan_order, active, x, cot, vec_two, glu_bias_all[None], glu_parts
    )

    in_bias_blocks = in_bias.reshape(-1, 1, ff_block_of(piece_ff))

    def ffn_half(which, weights, **parts):
        return ffn_call(
            meta,
            order,
            out_table,
            place_at,
            base_table + which * half,
            column_table + which * half,
            cot_out,
            weights,
            **parts,
        )

    def low_rest(values):
        for bit in range(1, top):
            keep, send = values[: len(values) // 2], values[len(values) // 2 :]
            came = swap(jnp.stack([Sum(*v).total().astype(bf16) for v in send]), "batch", 1 << bit)
            values = [v + [came[i]] for i, v in enumerate(keep)]
        return values

    def low_sum(keep, came):
        return low_rest([[v, came[i]] for i, v in enumerate(keep)])

    def out_send(parts):
        return parts[half // 2][None] if half == 2 else jnp.stack(parts[half // 2 :])

    def rounded(terms):
        return Sum(*terms).total().astype(bf16)

    (back_a, bias_a), (out_a,), grad_out_a, keep_in_a, (send_in_a,) = ffn_half(
        0, out_low, norm=norm_two, bias=in_bias_blocks, w_in=in_parts, norm_t=norm_two_t
    )
    out_high = over_low([after(out_top, back_a)])
    in_a_came = swap(send_in_a, "batch", 1)
    out_a_came = swap(out_send(grad_out_a), "batch", 1)
    in_a_own, in_a_other = low_sum(keep_in_a, in_a_came)
    in_a_other = rounded(in_a_other)
    in_b_top = top_swap(in_a_other)
    (back_b, bias_b), (out_b,), grad_out_b, keep_in_b, (send_in_b,) = ffn_half(
        1,
        out_high,
        norm=after(norm_two, back_a, in_a_other),
        bias=in_bias_blocks,
        w_in=in_parts,
        norm_t=norm_two_t,
    )
    back_b, in_b_top, out_a_came = together((back_b, in_b_top, out_a_came))

    grad_resid, grad_gated, grad_glu_bias, sums, moved = gate_back_call(
        meta,
        chan_order,
        seq_size,
        [back_a, back_b],
        resid,
        gated,
        cot_out,
        vec_two,
        glu_parts,
    )
    grad_out_b, send_in_b = after((grad_out_b, send_in_b), moved)
    out_b_came = swap(out_send(grad_out_b), "batch", 1)
    in_b_came = swap(send_in_b, "batch", 1)

    grads_in = exchange(moved)
    (out_b_sum,) = low_sum(grad_out_b[: half // 2], out_b_came)
    out_b_sum = rounded(out_b_sum)
    out_a_top = top_swap(out_b_sum)
    keep_glu, send_glu = gate_weight_call(
        meta, chan_order, place_at, act, after(grad_gated, out_b_sum)
    )
    in_b_own, in_b_other = low_sum(keep_in_b, in_b_came)
    in_b_other = rounded([after(in_b_other[0], send_glu), *in_b_other[1:]])
    in_a_top = top_swap(in_b_other)
    sum_in_b = Sum(*in_b_own, in_b_top)
    in_b_near = sum_in_b.upper()
    in_b_near_came = near_swap(in_b_near)

    lower = (me_b >> top) == 0

    def halves(a, b, axis):
        return jnp.concatenate([jnp.where(lower, a, b), jnp.where(lower, b, a)], axis=axis)

    in_bias_sums = halves(bias_a.reshape(-1), bias_b.reshape(-1), 0)
    small_grads = jnp.concatenate(
        [
            value.reshape(devices, -1)
            for value in (grad_glu_bias[0], sums[1], sums[2], sums[0], in_bias_sums)
        ],
        axis=1,
    )
    small_grads = small_grads.reshape(batch_size, seq_size, -1)
    small_grads = jnp.moveaxis(small_grads, 1, 0).reshape(seq_size, -1)
    high = lax.reduce_precision(small_grads, 8, 7)
    rest = (small_grads - high).astype(bf16)
    extra_rows = -(-2 * small_grads.shape[1] // (16 * chan)) * 16
    blank = jnp.zeros((seq_size, extra_rows * chan - 2 * small_grads.shape[1]), bf16)
    extra = jnp.concatenate([high.astype(bf16), rest, blank], axis=1)
    extra = extra.reshape(seq_size, extra_rows, chan)
    out_a, out_b, resid = after((out_a, out_b, resid), in_b_other)
    output = resid + (out_a + out_b + vec_two[2:3]).reshape(resid.shape)
    output = output.astype(bf16)
    (out_a_sum,) = low_sum(grad_out_a[: half // 2], out_a_came)
    out_a_sum = [v.reshape(seq_size, -1, width) for v in out_a_sum]
    grads_in, extra, out_a_sum, in_a_own, near, far, input_mult = together(
        (grads_in, extra, out_a_sum, in_a_own, near, far, input_mult)
    )

    moved_back, cross, state_sums = back_call(
        meta,
        after(grads_in, in_b_other, in_b_near, output),
        normed,
        drive_spec,
        mixed,
        vec_one,
        spec,
        fwd,
        inv,
        extra,
    )
    moved_back, cross, in_b_near_came, out_a_top = together(
        (moved_back, cross, in_b_near_came, out_a_top)
    )

    moved_back = exchange(moved_back)
    glu_came = swap(after(send_glu, cross), "batch", 1)
    sum_out = Sum(*out_a_sum, out_a_top.reshape(seq_size, -1, width))
    out_near = sum_out.upper()
    out_near_came = near_swap(out_near)
    sum_in_b.keep(after(in_b_near_came, out_near))
    in_b_middle = sum_in_b.upper()
    in_b_middle_came = middle_swap(in_b_middle)
    glu_own, glu_other = low_sum(keep_glu, after(glu_came, in_b_middle))
    glu_other = rounded(glu_other)
    glu_top_came = top_swap(glu_other)
    sum_in_a = Sum(*in_a_own, after(in_a_top, glu_other))
    in_a_near = sum_in_a.upper()
    in_a_near_came = near_swap(in_a_near)
    raw_modes = modes_call(meta, after(cross, in_a_near), far, near, inv)
    in_b_middle_came, in_a_near_came, out_near_came, glu_top_came = after(
        (in_b_middle_came, in_a_near_came, out_near_came, glu_top_came), raw_modes
    )
    sum_in_b.keep(in_b_middle_came)
    sum_in_b.middle()
    in_b_last = sum_in_b.upper()
    in_b_last_came = last_swap(in_b_last)
    sum_in_a.keep(after(in_a_near_came, in_b_last))
    in_a_middle = sum_in_a.upper()
    in_a_middle_came = middle_swap(in_a_middle)
    sum_glu = Sum(*glu_own, after(glu_top_came, in_a_middle))
    glu_near = sum_glu.upper()
    glu_near_came = near_swap(glu_near)
    sum_out.keep(after(out_near_came, glu_near))
    out_middle = sum_out.upper()
    out_middle_came = middle_swap(out_middle)

    input_grad = input_call(meta, after(moved_back, out_middle), x, grad_resid, perm)
    input_grad, in_a_middle_came, glu_near_came, out_middle_came = together(
        (input_grad, in_a_middle_came, glu_near_came, out_middle_came)
    )
    sum_out.keep(out_middle_came)
    sum_out.middle()
    out_last = sum_out.upper()
    out_last_came = last_swap(out_last)
    sum_glu.keep(after(glu_near_came, out_last))
    glu_middle = sum_glu.upper()
    glu_middle_came = middle_swap(glu_middle)
    sum_in_a.keep(after(in_a_middle_came, glu_middle))
    sum_in_a.middle()
    in_a_last = sum_in_a.upper()
    in_a_last_came = last_swap(in_a_last)
    sum_glu.keep(after(glu_middle_came, in_a_last))
    sum_glu.middle()
    glu_last = sum_glu.upper()
    glu_last_came = last_swap(glu_last)
    in_a_last_came, out_last_came, in_b_last_came = after(
        (in_a_last_came, out_last_came, in_b_last_came), glu_last
    )
    raw_modes, state_sums = after((raw_modes, state_sums), input_grad)

    def finish(value, came):
        value.keep(came)
        return value.total()[0]

    z = cmul((raw_modes[0], raw_modes[1]), input_mult)
    state_grads = jnp.concatenate([z[0], -z[1], state_sums[:3]], axis=0).T
    state_grads = reduce_batch(state_grads.reshape(batch_size, shard_rows, -1))
    grad_state = jnp.stack([state_grads[:, :mode_count], state_grads[:, mode_count : 2 * mode_count]])
    grad_out_total = finish(sum_out, out_last_came)
    far_in = halves(finish(sum_in_a, in_a_last_came), finish(sum_in_b, in_b_last_came), 0)
    grad_in_total = jnp.concatenate([far_in[b] for b in range(batch_size)], axis=1)
    grad_glu_total = finish(sum_glu, glu_last_came)

    small_came = moved_back[:, micro * span :, :].reshape(seq_size, -1).astype(f32)
    small_came = jnp.sum(small_came, axis=0)
    size = batch_size * small_size
    small_came = (small_came[:size] + small_came[size : 2 * size]).reshape(batch_size, -1)
    own = reduce_batch(jnp.take(small_came, natural_piece, axis=0))
    grad_glu_bias_own, grad_gain_two, grad_bias_two, grad_out_bias, grad_in_bias_own = [
        own[s : s + c] for s, c in zip(starts, counts)
    ]

    return (
        output[:, None],
        input_grad[:, None],
        state_grads[:, 2 * mode_count + 1],
        state_grads[:, 2 * mode_count + 2],
        grad_state,
        state_grads[:, 2 * mode_count],
        grad_glu_total,
        grad_glu_bias_own,
        grad_gain_two,
        grad_bias_two,
        grad_in_total,
        grad_in_bias_own,
        grad_out_total,
        grad_out_bias,
    )


def solution(mesh):
    both = ("batch", "seq")
    rows = P(None, "batch", "seq", None)
    vector = P(both)
    matrix = P(both, None)
    state = P(None, both, None)
    return jax.shard_map(
        per_device,
        mesh=mesh,
        in_specs=(
            rows,
            P(None, "batch"),
            rows,
            vector,
            vector,
            vector,
            state,
            vector,
            matrix,
            vector,
            vector,
            vector,
            matrix,
            vector,
            matrix,
            vector,
        ),
        out_specs=(
            rows,
            rows,
            vector,
            vector,
            state,
            vector,
            matrix,
            vector,
            vector,
            vector,
            matrix,
            vector,
            matrix,
            vector,
        ),
        check_vma=False,
    )
```

```python
import functools
import math

import jax
import jax.numpy as jnp
import numpy as np
from jax import lax
from jax.experimental import pallas as pl
from jax.experimental.pallas import tpu as pltpu
from jax.sharding import PartitionSpec as P

f32 = jnp.float32
bf16 = jnp.bfloat16
norm_eps = 1e-05
near_span = 64
vmem_limit = 60 * 1024 * 1024
gelu_scale = math.sqrt(2.0 / math.pi)
gelu_cubic = 0.044715


def after(value, *tokens):
    return jax.tree.map(lambda v: lax.optimization_barrier((v, tokens))[0], value)


together = lax.optimization_barrier


def bits_of(size):
    count = size.bit_length() - 1
    if (1 << count) != size:
        raise ValueError("axis size")
    return count


def reverse_bits(value, count):
    result = 0
    for bit in range(count):
        result = result | (((value >> bit) & 1) << (count - 1 - bit))
    return result


def swap(value, axis, bit):
    size = lax.axis_size(axis)
    return lax.ppermute(value, axis, [(i, i ^ bit) for i in range(size)])


def gather_first(shard):
    return swap(shard[None], "seq", lax.axis_size("seq") // 2)


def gather_direct(shard):
    size = lax.axis_size("seq")
    return [swap(shard[None], "seq", bits) for bits in (size // 2, size // 4, size // 2 + size // 4)]


def gather_more(joined, lowest):
    size = lax.axis_size("seq")
    while joined.shape[0] << lowest < size:
        bit = size // joined.shape[0] // 2
        joined = jnp.concatenate([joined, swap(joined, "seq", bit)], axis=0)
    return joined


class Sum:
    def __init__(self, *terms):
        self.terms = list(terms)

    def total(self, start=0, stop=None):
        values = [term[start:stop].astype(f32) for term in self.terms]
        return functools.reduce(lambda a, b: a + b, values)

    def upper(self):
        return self.total(self.terms[0].shape[0] // 2).astype(bf16)

    def keep(self, came):
        half = self.terms[0].shape[0] // 2
        self.terms = [term[:half] for term in self.terms] + [came]

    def add(self, came):
        self.terms.append(came)

    def middle(self):
        for bit in range(2, bits_of(lax.axis_size("seq")) - 1):
            self.keep(swap(self.upper(), "seq", 1 << bit))


def swap_batch(pieces, bit):
    return [swap(piece, "batch", 1 << bit) for piece in pieces]


def gather_batch(part):
    pieces = [part]
    for bit in reversed(range(bits_of(lax.axis_size("batch")))):
        pieces = pieces + swap_batch(pieces, bit)
    return pieces


def reduce_batch(value):
    for bit in range(bits_of(lax.axis_size("batch"))):
        half = value.shape[0] // 2
        value = value[:half] + swap(value[half:], "batch", 1 << bit)
    return value[0]


def exchange(parts):
    return lax.all_to_all(parts, "seq", 0, 0)


def gelu_parts(values):
    square = values * values
    half = 0.5 * jnp.tanh(values * (gelu_scale + gelu_scale * gelu_cubic * square)) + 0.5
    return square, half


def gelu_value(values):
    return values * gelu_parts(values)[1]


def gelu_both(values):
    square, half = gelu_parts(values)
    value = values * half
    inner = 2.0 * gelu_scale + 6.0 * gelu_scale * gelu_cubic * square
    return value, half + value * (1.0 - half) * inner


def gelu_slope(values):
    return gelu_both(values)[1]


def layer_stats(values):
    centered = values - jnp.mean(values, axis=-1, keepdims=True)
    scale_inv = lax.rsqrt(jnp.mean(centered * centered, axis=-1, keepdims=True) + norm_eps)
    return centered * scale_inv, scale_inv


def norm_back(grad_normed, normed, scale_inv):
    first_mean = jnp.mean(grad_normed, axis=-1, keepdims=True)
    second_mean = jnp.mean(grad_normed * normed, axis=-1, keepdims=True)
    return scale_inv * (grad_normed - first_mean - normed * second_mean)


def dot(left, right):
    return jnp.dot(left, right, preferred_element_type=f32)


def dot_left_t(left, right):
    return lax.dot_general(left, right, (((0,), (0,)), ((), ())), preferred_element_type=f32)


def dot_right_t(left, right):
    return lax.dot_general(left, right, (((1,), (1,)), ((), ())), preferred_element_type=f32)


def stack_split(values):
    high = values.astype(bf16)
    low = (values - high.astype(f32)).astype(bf16)
    return jnp.concatenate([high, high, low], axis=0)


def table_split(table):
    high = table.astype(jnp.bfloat16)
    low = (table - high.astype(np.float64)).astype(jnp.bfloat16)
    return np.concatenate([high, low, high], axis=1)


def transform_tables(span):
    freqs = np.arange(span, dtype=np.float64) + 0.5
    phase = 2.0 * math.pi / (2 * span) * freqs[:, None] * np.arange(span, dtype=np.float64)[None]
    forward = np.concatenate([np.cos(phase), -np.sin(phase)], axis=0)
    backward = np.concatenate([np.cos(phase).T, -np.sin(phase).T], axis=1) / span
    return table_split(forward), table_split(backward)


def loop(count, body):
    if count <= 8:
        for index in range(count):
            body(index)
    else:
        lax.fori_loop(0, count, lambda index, carry: (body(index), carry)[1], 0)


def sum_loop(first, last, body, init):
    if isinstance(first, int) and isinstance(last, int):
        for index in range(first, last):
            init = body(index, init)
        return init
    return lax.fori_loop(first, last, body, init)


def full_spec(shape, buffered=True):
    zeros = (0,) * len(shape)
    if buffered:
        return pl.BlockSpec(shape, lambda *_: zeros, pipeline_mode=pl.Buffered(1))
    return pl.BlockSpec(shape, lambda *_: zeros)


def parted(parts, span, chan):
    return pl.BlockSpec((parts, span, chan), lambda m, _: (0, m, 0))


def call(kernel, grid, meta, in_specs, operands, out_specs, out_shape, scratch, flops, name):
    return pl.pallas_call(
        kernel,
        grid_spec=pltpu.PrefetchScalarGridSpec(
            num_scalar_prefetch=1,
            grid=grid,
            in_specs=in_specs,
            out_specs=out_specs,
            scratch_shapes=scratch,
        ),
        out_shape=out_shape,
        compiler_params=pltpu.CompilerParams(
            vmem_limit_bytes=vmem_limit, dimension_semantics=("arbitrary",) * len(grid)
        ),
        cost_estimate=pl.CostEstimate(
            flops=int(flops * 0.02), bytes_accessed=int(flops * 0.02 / 400), transcendentals=0
        ),
        name=name,
    )(meta, *operands)


def norm_kernel(batch_bits, shard_rows, seq_size, meta, x_ref, extra_ref, out_ref, perm_ref):
    width = x_ref.shape[2]
    chan = out_ref.shape[-1]

    @pl.when(pl.program_id(0) == 0)
    def _():
        lane = lax.broadcasted_iota(jnp.int32, (width, width), 1)
        piece = (lane & (chan - 1)) // shard_rows
        source = (
            (reverse_bits(piece, batch_bits) ^ meta[0]) * seq_size + lane // chan
        ) * shard_rows + (lane & (shard_rows - 1))
        row = lax.broadcasted_iota(jnp.int32, (width, width), 0)
        perm_ref[...] = jnp.where(row == source, 1.0, 0.0).astype(bf16)
        for d in range(out_ref.shape[0]):
            out_ref[d, pl.ds(out_ref.shape[1] - 16, 16), :] = extra_ref[...]

    span = x_ref.shape[1]
    rows = pl.ds(pl.multiple_of(pl.program_id(0) * span, span), span)
    normed, _ = layer_stats(x_ref[0].astype(f32))
    spread = dot(normed.astype(bf16), perm_ref[...]).astype(bf16)
    for d in range(out_ref.shape[0]):
        out_ref[d, rows, :] = spread[:, d * chan : (d + 1) * chan]


def norm_call(meta, x, extra, batch_bits, shard_rows, parts):
    micro, span, width = x.shape
    chan = width // parts
    return call(
        functools.partial(norm_kernel, batch_bits, shard_rows, parts),
        (micro,),
        meta,
        [pl.BlockSpec((1, span, width), lambda m, _: (m, 0, 0))]
        + [full_spec(extra.shape)],
        (x, extra),
        [full_spec((parts, micro * span + 16, chan)), full_spec((width, width))],
        [
            jax.ShapeDtypeStruct((parts, micro * span + 16, chan), bf16),
            jax.ShapeDtypeStruct((width, width), bf16),
        ],
        [],
        2 * micro * span * width * width,
        "norm_one",
    )


def kernel_kernel(meta, lift_re, lift_im, near_re, near_im, fwd_ref, out_ref, series, spec):
    modes, span_near, chan = near_re.shape
    far_count = lift_re.shape[1]
    blocks, _, span, _ = out_ref.shape
    group = 2

    def far_group(index, carry):
        def one_mode(n, acc):
            near_r, near_i = near_re[n], near_im[n]
            result = []
            for g in range(group):
                row = index * group + g
                a = lift_re[n, pl.ds(row, 1), :]
                b = lift_im[n, pl.ds(row, 1), :]
                result.append(acc[g] + (a * near_r - b * near_i))
            return tuple(result)

        zero = jnp.zeros((span_near, chan), f32)
        acc = lax.fori_loop(0, modes, one_mode, (zero,) * group, unroll=4)
        for g in range(group):
            start = pl.multiple_of((index * group + g) * span_near, span_near)
            series[pl.ds(start, span_near), :] = acc[g]
        return carry

    lax.fori_loop(0, far_count // group, far_group, 0)

    def one_pair(index):
        first = index * 2 * span
        pair = [series[pl.ds(first + k * span, span), :] for k in range(2)]
        both = dot(fwd_ref[...], stack_split(jnp.concatenate(pair, axis=1)))
        for k in range(2):
            spec[index * 2 + k] = both[:, k * chan : (k + 1) * chan]

    loop(blocks // 2, one_pair)
    rows = lax.broadcasted_iota(jnp.int32, (span, chan), 0)
    sign = 1.0 - 2.0 * (rows & 1).astype(f32)

    def one_block(d):
        real, imag = spec[d, :span], spec[d, span:]
        before = d - 1 if isinstance(d, int) else jnp.maximum(d - 1, 0)
        if isinstance(d, int) and d == 0:
            out_ref[0, 0], out_ref[0, 1] = real, imag
            return
        keep = 1.0 if isinstance(d, int) else jnp.where(d > 0, 1.0, 0.0)
        out_ref[d, 0] = real - keep * (sign * spec[before, span:])
        out_ref[d, 1] = imag + keep * (sign * spec[before, :span])

    loop(blocks, one_block)


def kernel_call(meta, lift, near, fwd, blocks, span):
    chan = near[0].shape[-1]
    operands = (lift[0], lift[1], near[0], near[1], fwd)
    return call(
        kernel_kernel,
        (1,),
        meta,
        [full_spec(a.shape) for a in operands],
        operands,
        full_spec((blocks, 2, span, chan)),
        jax.ShapeDtypeStruct((blocks, 2, span, chan), f32),
        [pltpu.VMEM((blocks * span, chan), f32), pltpu.VMEM((blocks, 2 * span, chan), f32)],
        1.1e10,
        "state_kernel",
    )


def mask_of(meta, m, block, span, chan):
    rows = block * span + lax.broadcasted_iota(jnp.int32, (span, chan), 0)
    return (rows < meta[1 + m]).astype(f32)


freq_tile = 64


def conv_kernel(
    meta,
    normed_ref,
    vec_ref,
    spec_ref,
    fwd_ref,
    inv_ref,
    drive_ref,
    mixed_ref,
    out_ref,
    drive,
    spectrum,
):
    m = pl.program_id(0)
    blocks, span, chan = drive.shape
    gain, bias, skip = vec_ref[0:1, :], vec_ref[1:2, :], vec_ref[2:3, :]

    def drive_pair(pair):
        values = []
        for k in range(2):
            block = 2 * pair + k
            normed = normed_ref[block].astype(f32)
            u = mask_of(meta, m, block, span, chan) * (normed * gain + bias)
            drive[block] = u
            values.append(u)
        both = dot(fwd_ref[...], stack_split(jnp.concatenate(values, axis=1)))
        for k in range(2):
            drive_ref[0, 2 * pair + k] = both[:, k * chan : (k + 1) * chan]

    loop(blocks // 2, drive_pair)

    def one_pair(index):
        for k in range(2):
            i = index * 2 + k

            def one_tile(tile, carry):
                low = pl.ds(pl.multiple_of(tile * freq_tile, freq_tile), freq_tile)
                high = pl.ds(pl.multiple_of(span + tile * freq_tile, freq_tile), freq_tile)

                def one_term(j, acc):
                    xr, xi = drive_ref[0, j, low], drive_ref[0, j, high]
                    gr, gi = spec_ref[i - j, 0, low], spec_ref[i - j, 1, low]
                    return (acc[0] + (xr * gr - xi * gi), acc[1] + (xr * gi + xi * gr))

                zero = jnp.zeros((freq_tile, chan), f32)
                acc = sum_loop(0, i + 1, one_term, (zero, zero))
                spectrum[k, low] = acc[0]
                spectrum[k, high] = acc[1]
                return carry

            lax.fori_loop(0, span // freq_tile, one_tile, 0, unroll=True)
        both = dot(
            inv_ref[...], stack_split(jnp.concatenate([spectrum[0], spectrum[1]], axis=1))
        )
        for k in range(2):
            i = index * 2 + k
            mixed = both[:, k * chan : (k + 1) * chan] + skip * drive[i]
            mixed_ref[0, i] = mixed
            out_ref[i] = gelu_value(mixed).astype(bf16)

    loop(blocks // 2, one_pair)


def conv_call(meta, micro, normed, vec, spec, fwd, inv):
    parts, _, chan = normed.shape
    span = spec.shape[2]
    wide = lambda rows: pl.BlockSpec((1, parts, rows, chan), lambda m, _: (m, 0, 0, 0))
    return call(
        conv_kernel,
        (micro,),
        meta,
        [parted(parts, span, chan)] + [full_spec(a.shape) for a in (vec, spec, fwd, inv)],
        (normed, vec, spec, fwd, inv),
        [wide(2 * span), wide(span), parted(parts, span, chan)],
        [
            jax.ShapeDtypeStruct((micro, parts, 2 * span, chan), f32),
            jax.ShapeDtypeStruct((micro, parts, span, chan), f32),
            jax.ShapeDtypeStruct((parts, micro * span, chan), bf16),
        ],
        [
            pltpu.VMEM((parts, span, chan), f32),
            pltpu.VMEM((2, 2 * span, chan), f32),
        ],
        1.5e10,
        "state_conv",
    )


def back_kernel(
    meta,
    grads_ref,
    normed_ref,
    drive_ref,
    mixed_ref,
    vec_ref,
    spec_ref,
    fwd_ref,
    inv_ref,
    extra_ref,
    out_ref,
    cross_ref,
    sums_ref,
    grad_mixed,
    grad_spec,
    spectrum,
):
    m = pl.program_id(0)
    blocks, span, chan = grad_mixed.shape
    gain, bias, skip = vec_ref[0:1, :], vec_ref[1:2, :], vec_ref[2:3, :]

    @pl.when(m == 0)
    def _():
        cross_ref[...] = jnp.zeros_like(cross_ref)
        sums_ref[...] = jnp.zeros_like(sums_ref)
        extra = extra_ref.shape[1]
        out_ref[:, pl.ds(out_ref.shape[1] - extra, extra), :] = extra_ref[...]

    def grad_pair(pair):
        values = []
        for k in range(2):
            block = 2 * pair + k
            normed = normed_ref[block].astype(f32)
            u = mask_of(meta, m, block, span, chan) * (normed * gain + bias)
            gm = grads_ref[block].astype(f32) * gelu_slope(mixed_ref[0, block])
            sums_ref[0:1, :] += jnp.sum(gm * u, axis=0, keepdims=True)
            grad_mixed[block] = gm
            values.append(gm)
        both = dot(fwd_ref[...], stack_split(jnp.concatenate(values, axis=1)))
        for k in range(2):
            grad_spec[2 * pair + k] = both[:, k * chan : (k + 1) * chan]

    loop(blocks // 2, grad_pair)

    def tiles_of(body):
        def one_tile(tile, carry):
            low = pl.ds(pl.multiple_of(tile * freq_tile, freq_tile), freq_tile)
            high = pl.ds(pl.multiple_of(span + tile * freq_tile, freq_tile), freq_tile)
            body(low, high)
            return carry

        lax.fori_loop(0, span // freq_tile, one_tile, 0, unroll=True)

    zero = jnp.zeros((freq_tile, chan), f32)

    def one_pair(index):
        for k in range(2):
            j = index * 2 + k

            def body(low, high):
                def one_term(i, acc):
                    mr, mi = grad_spec[i, low], grad_spec[i, high]
                    gr, gi = spec_ref[i - j, 0, low], spec_ref[i - j, 1, low]
                    return (acc[0] + (mr * gr + mi * gi), acc[1] + (mi * gr - mr * gi))

                acc = sum_loop(j, blocks, one_term, (zero, zero))
                spectrum[k, low] = acc[0]
                spectrum[k, high] = acc[1]

            tiles_of(body)
        both = dot(
            inv_ref[...], stack_split(jnp.concatenate([spectrum[0], spectrum[1]], axis=1))
        )
        for k in range(2):
            j = index * 2 + k
            grad_mixed[j] = both[:, k * chan : (k + 1) * chan] + skip * grad_mixed[j]

    loop(blocks // 2, one_pair)

    def finish(block):
        g = mask_of(meta, m, block, span, chan) * grad_mixed[block]
        normed = normed_ref[block].astype(f32)
        sums_ref[1:2, :] += jnp.sum(g * normed, axis=0, keepdims=True)
        sums_ref[2:3, :] += jnp.sum(g, axis=0, keepdims=True)
        out_ref[block, pl.ds(pl.multiple_of(m * span, span), span), :] = (g * gain).astype(bf16)

    loop(blocks, finish)

    def one_lag(d):
        def body(low, high):
            def one_term(j, acc):
                mr, mi = grad_spec[j + d, low], grad_spec[j + d, high]
                xr, xi = drive_ref[0, j, low], drive_ref[0, j, high]
                return (acc[0] + (mr * xr + mi * xi), acc[1] + (mi * xr - mr * xi))

            acc = sum_loop(0, blocks - d, one_term, (cross_ref[d, low], cross_ref[d, high]))
            cross_ref[d, low] = acc[0]
            cross_ref[d, high] = acc[1]

        tiles_of(body)

    loop(blocks, one_lag)


def back_call(meta, grads, normed, drive, mixed, vec, spec, fwd, inv, extra):
    parts, _, chan = normed.shape
    micro, _, span, _ = mixed.shape
    total = micro * span + extra.shape[1]
    mode = None if parts <= 8 else pl.Buffered(1)
    wide = lambda rows: pl.BlockSpec(
        (1, parts, rows, chan), lambda m, _: (m, 0, 0, 0), pipeline_mode=mode
    )
    return call(
        back_kernel,
        (micro,),
        meta,
        [parted(parts, span, chan)] * 2
        + [wide(2 * span), wide(span)]
        + [full_spec(a.shape) for a in (vec, spec, fwd, inv, extra)],
        (grads, normed, drive, mixed, vec, spec, fwd, inv, extra),
        [
            full_spec((parts, total, chan)),
            full_spec((parts, 2 * span, chan)),
            full_spec((8, chan)),
        ],
        [
            jax.ShapeDtypeStruct((parts, total, chan), bf16),
            jax.ShapeDtypeStruct((parts, 2 * span, chan), f32),
            jax.ShapeDtypeStruct((8, chan), f32),
        ],
        [
            pltpu.VMEM((parts, span, chan), f32),
            pltpu.VMEM((parts, 2 * span, chan), f32),
            pltpu.VMEM((2, 2 * span, chan), f32),
        ],
        2e10,
        "state_back",
    )


def modes_kernel(meta, cross_ref, far_re, far_im, near_re, near_im, inv_ref, out_ref, series):
    modes, span_near, chan = near_re.shape
    far_count = far_re.shape[1]
    blocks, double, _ = cross_ref.shape
    span = double // 2
    rows = lax.broadcasted_iota(jnp.int32, (span, chan), 0)
    sign = 1.0 - 2.0 * (rows & 1).astype(f32)

    def one_pair(index):
        pair = []
        for k in range(2):
            d = index * 2 + k
            real, imag = cross_ref[d, :span], cross_ref[d, span:]
            if isinstance(d, int):
                keep = 1.0 if d + 1 < blocks else 0.0
                after = min(d + 1, blocks - 1)
            else:
                keep = jnp.where(d + 1 < blocks, 1.0, 0.0)
                after = jnp.minimum(d + 1, blocks - 1)
            real = real + keep * (sign * cross_ref[after, span:])
            imag = imag - keep * (sign * cross_ref[after, :span])
            pair.append(jnp.concatenate([real, imag], axis=0))
        both = dot(inv_ref[...], stack_split(jnp.concatenate(pair, axis=1)))
        for k in range(2):
            series[pl.ds((index * 2 + k) * span, span), :] = both[:, k * chan : (k + 1) * chan]

    loop(blocks // 2, one_pair)
    group = 2

    def mode_group(index, carry):
        def one_far(i, acc):
            values = series[pl.ds(pl.multiple_of(i * span_near, span_near), span_near), :]
            result = []
            for g in range(group):
                n = index * group + g
                a = far_re[n, pl.ds(i, 1), :]
                b = far_im[n, pl.ds(i, 1), :]
                result.append((acc[g][0] + a * values, acc[g][1] + b * values))
            return tuple(result)

        zero = jnp.zeros((span_near, chan), f32)
        acc = lax.fori_loop(0, far_count, one_far, ((zero, zero),) * group, unroll=4)
        for g in range(group):
            n = index * group + g
            near_r, near_i = near_re[n], near_im[n]
            re, im = acc[g]
            out_ref[0, pl.ds(n, 1), :] = jnp.sum(re * near_r - im * near_i, axis=0, keepdims=True)
            out_ref[1, pl.ds(n, 1), :] = jnp.sum(re * near_i + im * near_r, axis=0, keepdims=True)
        return carry

    lax.fori_loop(0, modes // group, mode_group, 0)


def modes_call(meta, cross, far, near, inv):
    modes, _, chan = near[0].shape
    blocks, double, _ = cross.shape
    operands = (cross, far[0], far[1], near[0], near[1], inv)
    return call(
        modes_kernel,
        (1,),
        meta,
        [full_spec(a.shape) for a in operands],
        operands,
        full_spec((2, modes, chan)),
        jax.ShapeDtypeStruct((2, modes, chan), f32),
        [pltpu.VMEM((blocks * double // 2, chan), f32)],
        1.1e10,
        "state_modes",
    )


class Rows:
    def __init__(self, width, shard_rows, seq_size, batch_size, table, by_channel=False):
        self.width = width
        self.shard_rows = shard_rows
        self.seq_size = seq_size
        self.batch_size = batch_size
        self.table = table
        self.piece_rows = shard_rows * seq_size
        self.by_block = shard_rows % 16 == 0
        self.by_channel = by_channel

    def natural(self, meta, p, q):
        start = meta[self.table + p * self.seq_size + q] * self.shard_rows
        return pl.ds(pl.multiple_of(start, self.shard_rows), self.shard_rows)

    def order(self, meta, place):
        shape = (self.width, self.width)
        relative = lax.broadcasted_iota(jnp.int32, shape, 0)
        piece = relative // self.piece_rows
        position = (relative % self.piece_rows) // self.shard_rows
        seq = reverse_bits(position, bits_of(self.seq_size)) ^ meta[0]
        if self.by_channel:
            shard = seq * self.batch_size + piece
        else:
            batch = reverse_bits(piece, bits_of(self.batch_size)) ^ meta[place + 1]
            shard = batch * self.seq_size + seq
        source = shard * self.shard_rows + relative % self.shard_rows
        return jnp.where(lax.broadcasted_iota(jnp.int32, shape, 1) == source, 1.0, 0.0).astype(bf16)

    def to_natural(self, meta, place, parts, target):
        if self.by_block:
            for p, part in enumerate(parts):
                for q in range(self.seq_size):
                    target[self.natural(meta, p, q), :] = part[
                        pl.ds(q * self.shard_rows, self.shard_rows), :
                    ]
        else:
            whole = jnp.concatenate([part[...] for part in parts], axis=0)
            target[...] = dot_left_t(self.order(meta, place), whole).astype(bf16)

    def to_relative(self, meta, place, value, scratch, store):
        if self.by_block:
            scratch[...] = value.astype(bf16)
        else:
            moved = dot(self.order(meta, place), value.astype(bf16))
        for p in range(self.batch_size):
            for q in range(self.seq_size):
                if self.by_block:
                    block = scratch[self.natural(meta, p, q), :]
                else:
                    start = (p * self.seq_size + q) * self.shard_rows
                    block = moved[start : start + self.shard_rows].astype(bf16)
                store(p, q, block)


def gate_kernel(pieces, order, meta, *refs):
    active_ref, x_ref, cot_ref, vec_ref, glu_bias_ref = refs[:5]
    weights = refs[5 : 5 + pieces]
    act_ref, resid_ref, gated_ref, norm_ref, norm_t_ref, cot_out, weight_scr = refs[5 + pieces :]
    m = pl.program_id(0)
    _, span, width = x_ref.shape
    micro = pl.num_programs(0)

    @pl.when(m == 0)
    def _():
        order.to_natural(meta, 1 + micro, weights, weight_scr)

    act = jnp.concatenate([active_ref[d] for d in range(active_ref.shape[0])], axis=1)
    act_ref[...] = act
    gated = dot(act, weight_scr[...]) + glu_bias_ref[...]
    gated_ref[0] = gated
    residual = x_ref[0].astype(f32) + gated[:, :width] * jax.nn.sigmoid(gated[:, width:])
    resid_ref[0] = residual
    normed, _ = layer_stats(residual)
    norm_two = (normed * vec_ref[0:1, :] + vec_ref[1:2, :]).astype(bf16)
    norm_ref[...] = norm_two
    norm_t_ref[...] = norm_two.T
    rows = meta[1 + micro] + lax.broadcasted_iota(jnp.int32, (span, width), 0)
    cot_out[...] = jnp.where(rows < meta[1 + m], cot_ref[0].astype(f32), 0.0).astype(bf16)


def gate_call(meta, order, active, x, cot, vec, glu_bias, weights):
    parts, _, chan = active.shape
    pieces = len(weights)
    micro, span, width = x.shape
    tokens = micro * span
    tile = lambda cols: pl.BlockSpec((1, span, cols), lambda m, _: (m, 0, 0))
    flat = pl.BlockSpec((span, width), lambda m, _: (m, 0))
    return call(
        functools.partial(gate_kernel, pieces, order),
        (micro,),
        meta,
        [parted(parts, span, chan), tile(width), tile(width)]
        + [full_spec(a.shape) for a in (vec, glu_bias, *weights)],
        (active, x, cot, vec, glu_bias, *weights),
        [
            flat,
            tile(width),
            tile(2 * width),
            flat,
            pl.BlockSpec((width, span), lambda m, _: (0, m)),
            flat,
        ],
        [
            jax.ShapeDtypeStruct((tokens, width), bf16),
            jax.ShapeDtypeStruct((micro, span, width), f32),
            jax.ShapeDtypeStruct((micro, span, 2 * width), f32),
            jax.ShapeDtypeStruct((tokens, width), bf16),
            jax.ShapeDtypeStruct((width, tokens), bf16),
            jax.ShapeDtypeStruct((tokens, width), bf16),
        ],
        [pltpu.VMEM((width, 2 * width), bf16)],
        6 * tokens * width * width,
        "gated_unit",
    )


def ff_block_of(piece_ff):
    return min(1024, piece_ff)


def ffn_kernel(pieces, batch_pieces, sub, order, out_table, place, first, second, meta, *refs):
    refs = list(refs)
    take = lambda count: [refs.pop(0) for _ in range(count)]
    half = batch_pieces // 2
    (cot_ref,) = take(1)
    w_out = take(pieces)
    if first:
        norm_ref, bias_ref = take(2)
        w_in = take(batch_pieces)
    else:
        spread_ref, hidden_ref = take(2)
    if second:
        (norm_t_ref,) = take(1)
    if first:
        back_ref, grad_bias = take(2)
        if not second:
            spread_ref, hidden_ref = take(2)
    if second:
        (out_ref,) = take(1)
        grad_out, grad_in = take(pieces), take(half)
        (grad_in_send,) = take(1)
    (out_scr,) = take(1)
    if first:
        (in_scr,) = take(1)
    if second:
        (grad_in_scr,) = take(1)
    k = pl.program_id(0)
    s = pl.program_id(1)
    ff_block = out_scr.shape[0]
    subs = ff_block // sub
    start = jnp.logical_and(k == 0, s == 0)

    def sub_rows(t):
        return pl.ds(pl.multiple_of(meta[out_table + s * subs + t] * sub, sub), sub)

    for piece in range(pieces):

        @pl.when(k == piece)
        def _():
            for t in range(subs):
                out_scr[pl.ds(t * sub, sub), :] = w_out[piece][sub_rows(t), :]

    def accumulate(ref, part):
        @pl.when(start)
        def _():
            ref[...] = part

        @pl.when(jnp.logical_not(start))
        def _():
            ref[...] += part

    if first:
        order.to_natural(meta, place, w_in, in_scr)
        hidden = dot(norm_ref[...], in_scr[...]) + bias_ref[0]
        spread, slope = gelu_both(hidden)
        spread = spread.astype(bf16)
        grad_hidden = (dot_right_t(cot_ref[...], out_scr[...]) * slope).astype(bf16)
        grad_bias[0] = jnp.sum(grad_hidden.astype(f32), axis=0, keepdims=True)
        if not second:
            spread_ref[...] = spread
            hidden_ref[...] = grad_hidden
        accumulate(back_ref, dot_right_t(grad_hidden, in_scr[...]))
    else:
        spread, grad_hidden = spread_ref[...], hidden_ref[...]

    if second:
        accumulate(out_ref, dot(spread, out_scr[...]))

        def store(p, q, block):
            if p < half:
                grad_in[p][q, 0] = block
            else:
                grad_in_send[p - half, q, 0] = block

        order.to_relative(meta, place, dot(norm_t_ref[...], grad_hidden), grad_in_scr, store)
        part = dot_left_t(spread, cot_ref[...]).astype(bf16)
        for piece in range(pieces):

            @pl.when(k == piece)
            def _():
                for t in range(subs):
                    grad_out[piece][sub_rows(t), :] = part[t * sub : (t + 1) * sub, :]


def ffn_call(meta, order, out_table, place, base, column, cot, w_out, norm=None, bias=None, w_in=None, norm_t=None, kept=None):
    first, second = norm is not None, norm_t is not None
    pieces, batch_pieces = len(w_out), order.batch_size
    tokens, width = cot.shape
    piece_ff = w_out[0].shape[0]
    ff_block = ff_block_of(piece_ff)
    steps = piece_ff // ff_block
    sub = piece_ff // order.seq_size
    rows = order.piece_rows
    half = batch_pieces // 2
    seq_size, low = order.seq_size, order.shard_rows
    block = lambda k, s, meta: meta[base + k] + s
    wide = full_spec((tokens, width))
    step_columns = pl.BlockSpec((tokens, ff_block), lambda k, s, meta: (0, k * steps + s))
    activations = jax.ShapeDtypeStruct((tokens, pieces * piece_ff), bf16)
    total = jax.ShapeDtypeStruct((tokens, width), f32)
    operands = [cot, *w_out]
    in_specs = [wide] + [full_spec(a.shape) for a in w_out]
    outs, out_specs, scratch = [], [], [pltpu.VMEM((ff_block, width), bf16)]
    if first:
        operands += [norm, bias, *w_in]
        in_specs += [wide]
        in_specs += [pl.BlockSpec((1, 1, ff_block), lambda k, s, meta: (block(k, s, meta), 0, 0))]
        in_specs += [
            pl.BlockSpec((rows, ff_block), lambda k, s, meta: (0, block(k, s, meta)))
            for _ in w_in
        ]
        outs += [total, jax.ShapeDtypeStruct((pieces * steps, 1, ff_block), f32)]
        out_specs += [wide]
        out_specs += [
            pl.BlockSpec((1, 1, ff_block), lambda k, s, meta: (meta[column + k] * steps + s, 0, 0))
        ]
        scratch += [pltpu.VMEM((width, ff_block), bf16)]
        if not second:
            outs += [activations] * 2
            out_specs += [step_columns] * 2
    else:
        operands += kept
        in_specs += [step_columns] * 2
    if second:
        operands += [norm_t]
        in_specs += [full_spec(norm_t.shape)]
        outs += [total] + [jax.ShapeDtypeStruct(a.shape, bf16) for a in w_out]
        outs += [jax.ShapeDtypeStruct((seq_size, pieces, low, piece_ff), bf16)] * half
        outs += [jax.ShapeDtypeStruct((half, seq_size, pieces, low, piece_ff), bf16)]
        out_specs += [wide] + [full_spec(a.shape) for a in w_out]
        out_specs += [
            pl.BlockSpec((seq_size, 1, low, ff_block), lambda k, s, meta: (0, meta[column + k], 0, s))
        ] * half
        out_specs += [
            pl.BlockSpec(
                (half, seq_size, 1, low, ff_block),
                lambda k, s, meta: (0, 0, meta[column + k], 0, s),
            )
        ]
        scratch += [pltpu.VMEM((width, ff_block), bf16)]
    results = call(
        functools.partial(
            ffn_kernel, pieces, batch_pieces, sub, order, out_table, place, first, second
        ),
        (pieces, steps),
        meta,
        in_specs,
        operands,
        out_specs,
        outs,
        scratch,
        6 * (first + second) * tokens * width * piece_ff * pieces,
        "feed_forward",
    )
    head = results[: 2 * first + 2 * (first and not second)]
    tail = results[len(head) :]
    return head, tail[:1], tail[1 : 1 + pieces], tail[1 + pieces : -1], tail[-1:]


def gate_back_kernel(pieces, halves, order, meta, *refs):
    back = refs[:halves]
    resid_ref, gated_ref, cot_ref, vec_ref = refs[halves : halves + 4]
    weights = refs[halves + 4 : halves + 4 + pieces]
    rest = refs[halves + 4 + pieces :]
    grad_resid_ref, grad_gated_ref, glu_bias_ref, sums_ref, moved_ref, weight_scr = rest
    m = pl.program_id(0)
    count = pl.num_programs(0)
    width = cot_ref.shape[1]

    @pl.when(m == 0)
    def _():
        glu_bias_ref[...] = jnp.zeros_like(glu_bias_ref)
        sums_ref[...] = jnp.zeros_like(sums_ref)
        order.to_natural(meta, 1 + count, weights, weight_scr)

    residual = resid_ref[0]
    grad_norm = back[0][...]
    for h in range(1, halves):
        grad_norm = grad_norm + back[h][...]
    grad_out = cot_ref[...].astype(f32)
    normed, scale = layer_stats(residual)
    sums_ref[0:1, :] += jnp.sum(grad_out, axis=0, keepdims=True)
    sums_ref[1:2, :] += jnp.sum(grad_norm * normed, axis=0, keepdims=True)
    sums_ref[2:3, :] += jnp.sum(grad_norm, axis=0, keepdims=True)
    grad_resid = grad_out + norm_back(grad_norm * vec_ref[0:1, :], normed, scale)
    grad_resid_ref[0] = grad_resid
    gated = gated_ref[0]
    gate = jax.nn.sigmoid(gated[:, width:])
    grad_left = grad_resid * gate
    grad_right = grad_left * gated[:, :width] * (1.0 - gate)
    grad_gated = jnp.concatenate([grad_left, grad_right], axis=1).astype(bf16)
    grad_gated_ref[...] = grad_gated
    glu_bias_ref[0:1, :] += jnp.sum(grad_gated.astype(f32), axis=0, keepdims=True)
    moved = dot_right_t(grad_gated, weight_scr[...]).astype(bf16)
    chan = moved_ref.shape[-1]
    for d in range(moved_ref.shape[0]):
        moved_ref[d] = moved[:, d * chan : (d + 1) * chan]


def gate_back_call(meta, order, parts, back, resid, gated, cot, vec, weights):
    halves, pieces = len(back), len(weights)
    micro, span, width = resid.shape
    tokens = micro * span
    chan = width // parts
    tile = lambda cols: pl.BlockSpec((1, span, cols), lambda m, _: (m, 0, 0))
    flat = lambda cols: pl.BlockSpec((span, cols), lambda m, _: (m, 0))
    return call(
        functools.partial(gate_back_kernel, pieces, halves, order),
        (micro,),
        meta,
        [flat(width)] * halves
        + [tile(width), tile(2 * width), flat(width)]
        + [full_spec(a.shape) for a in (vec, *weights)],
        (*back, resid, gated, cot, vec, *weights),
        [
            tile(width),
            flat(2 * width),
            full_spec((8, 2 * width)),
            full_spec((8, width)),
            parted(parts, span, chan),
        ],
        [
            jax.ShapeDtypeStruct((micro, span, width), f32),
            jax.ShapeDtypeStruct((tokens, 2 * width), bf16),
            jax.ShapeDtypeStruct((8, 2 * width), f32),
            jax.ShapeDtypeStruct((8, width), f32),
            jax.ShapeDtypeStruct((parts, micro * span, chan), bf16),
        ],
        [pltpu.VMEM((width, 2 * width), bf16)],
        4 * tokens * width * width,
        "gated_back",
    )


def gate_weight_kernel(pieces, order, place, meta, act_ref, grad_ref, *refs):
    grad_keep, grad_send, scratch = refs[: pieces // 2], refs[-2], refs[-1]

    def store(p, q, block):
        if p < pieces // 2:
            grad_keep[p][q] = block
        else:
            grad_send[p - pieces // 2, q] = block

    order.to_relative(meta, place, dot_left_t(act_ref[...], grad_ref[...]), scratch, store)


def gate_weight_call(meta, order, place, act, grad_gated):
    tokens, width = act.shape
    pieces, parts, low = order.batch_size, order.seq_size, order.shard_rows
    cols = width // 2
    outs = call(
        functools.partial(gate_weight_kernel, pieces, order, place),
        (4,),
        meta,
        [full_spec(act.shape), pl.BlockSpec((tokens, cols), lambda c, _: (0, c))],
        (act, grad_gated),
        [pl.BlockSpec((parts, low, cols), lambda c, _: (0, 0, c))] * (pieces // 2)
        + [pl.BlockSpec((pieces // 2, parts, low, cols), lambda c, _: (0, 0, 0, c))],
        [jax.ShapeDtypeStruct((parts, low, 2 * width), bf16)] * (pieces // 2)
        + [jax.ShapeDtypeStruct((pieces // 2, parts, low, 2 * width), bf16)],
        [pltpu.VMEM((width, cols), bf16)],
        4 * tokens * width * width,
        "gated_weight",
    )
    return outs[:-1], outs[-1]


def input_kernel(meta, moved_ref, x_ref, grad_resid_ref, perm_ref, out_ref):
    e = jnp.concatenate([moved_ref[d] for d in range(moved_ref.shape[0])], axis=1)
    e = dot_right_t(e, perm_ref[...])
    normed, scale = layer_stats(x_ref[0].astype(f32))
    out_ref[0] = (grad_resid_ref[0] + norm_back(e, normed, scale)).astype(bf16)


def input_call(meta, moved, x, grad_resid, perm):
    parts, _, chan = moved.shape
    micro, span, width = x.shape
    tile = lambda cols: pl.BlockSpec((1, span, cols), lambda m, _: (m, 0, 0))
    return call(
        input_kernel,
        (micro,),
        meta,
        [parted(parts, span, chan), tile(width), tile(width), full_spec(perm.shape)],
        (moved, x, grad_resid, perm),
        tile(width),
        jax.ShapeDtypeStruct((micro, span, width), bf16),
        [],
        2 * micro * span * width * width,
        "input_grad",
    )


def mode_tables(step_len, mode_count, length):
    order = jnp.arange(mode_count, dtype=f32)[:, None]
    rate = order * step_len

    def power(offsets):
        turns = 0.5 * rate[:, None, :] * offsets[None, :, None]
        angle = 2.0 * math.pi * (turns - jnp.round(turns))
        fading = jnp.exp(-0.5 * step_len[:, None, :] * offsets[None, :, None])
        return fading * jnp.cos(angle), fading * jnp.sin(angle)

    def outer(far, near):
        a, b = far[0][:, :, None], far[1][:, :, None]
        c, d = near[0][:, None], near[1][:, None]
        shape = (mode_count, far[0].shape[1] * near[0].shape[1], step_len.shape[-1])
        return (a * c - b * d).reshape(shape), (a * d + b * c).reshape(shape)

    ramp = jnp.arange(8, dtype=f32)
    near = outer(power(8.0 * ramp), power(ramp))
    far_count = length // near_span
    far = outer(
        power(8.0 * near_span * jnp.arange(far_count // 8, dtype=f32)), power(near_span * ramp)
    )

    def wave(scale):
        turns = scale * rate
        return 2.0 * math.pi * (turns - jnp.round(turns))

    decay = -0.5 * step_len
    turn_rate = math.pi * order
    step_im = jnp.exp(decay) * jnp.sin(wave(0.5))
    minus_one = jnp.expm1(decay) * jnp.cos(wave(0.5)) - 2.0 * jnp.sin(wave(0.25)) ** 2
    denominator = 0.25 + turn_rate**2
    input_mult = (
        (-0.5 * minus_one + step_im * turn_rate) / denominator,
        (-0.5 * step_im - minus_one * turn_rate) / denominator,
    )
    return near, far, input_mult


def cmul(a, b):
    return a[0] * b[0] - a[1] * b[1], a[0] * b[1] + a[1] * b[0]


def per_device(
    inputs,
    lengths,
    cotangent,
    norm1_gain,
    norm1_bias,
    step_size,
    state_out,
    skip_gain,
    glu_weight,
    glu_bias,
    norm2_gain,
    norm2_bias,
    ffn_in_weight,
    ffn_in_bias,
    ffn_out_weight,
    ffn_out_bias,
):
    micro, _, span, width = inputs.shape
    batch_size, seq_size = lax.axis_size("batch"), lax.axis_size("seq")
    batch_bits, seq_bits = bits_of(batch_size), bits_of(seq_size)
    devices = batch_size * seq_size
    shard_rows = width // devices
    chan = width // seq_size
    length = span * seq_size
    mode_count = state_out.shape[2]
    ff = ffn_in_weight.shape[1]
    me_b, me_s = lax.axis_index("batch"), lax.axis_index("seq")
    me = me_b * seq_size + me_s

    piece_ff = ff // batch_size
    place_at = 1 + micro
    in_table = 8
    out_table = in_table + devices
    base_table = out_table + seq_size
    column_table = base_table + batch_size
    chan_table = column_table + batch_size
    pieces = np.arange(batch_size)
    natural_piece = reverse_bits(pieces, batch_bits) ^ me_b
    piece_of = reverse_bits(jnp.arange(batch_size, dtype=jnp.int32) ^ me_b, batch_bits)

    def meta_of(parts):
        lengths, me_b, me_s = parts
        place = np.arange(devices)
        of_piece = reverse_bits(place // seq_size, batch_bits) ^ me_b
        of_seq = reverse_bits(place % seq_size, seq_bits) ^ me_s
        halves = np.concatenate([pieces[pieces % 2 == 0], pieces[pieces % 2 == 1]])
        of_group = reverse_bits(halves, batch_bits) ^ me_b
        table = jnp.concatenate(
            [
                of_piece * seq_size + of_seq,
                reverse_bits(np.arange(seq_size) ^ me_s, seq_bits),
                of_group * (piece_ff // ff_block_of(piece_ff)),
                of_group & (batch_size // 2 - 1),
                of_seq * batch_size + place // seq_size,
            ]
        )
        head = jnp.stack([me_s, *lengths[:, 0], me_s * span, me_b])
        blank = jnp.zeros((8 - head.shape[0],), jnp.int32)
        return jnp.concatenate([head, blank, table]).astype(jnp.int32)

    order = Rows(width, shard_rows, seq_size, batch_size, in_table)
    chan_order = Rows(width, shard_rows, seq_size, batch_size, chan_table, by_channel=True)

    x = inputs[:, 0]
    cot = cotangent[:, 0]

    top = batch_bits - 1
    half = batch_size // 2

    def over_low(pieces):
        for bit in reversed(range(top)):
            pieces = pieces + swap_batch(pieces, bit)
        return pieces

    def weave(low, high):
        return [piece for pair in zip(low, high) for piece in pair]

    def join(*parts):
        return jnp.concatenate(parts, axis=0)

    def near_swap(value):
        return swap(value, "seq", 1)

    def middle_swap(value):
        return swap(value, "seq", 2)

    def last_swap(value):
        return swap(value, "seq", seq_size // 2)

    def top_swap(value):
        return swap(value, "batch", 1 << top)

    counts = [2 * shard_rows, shard_rows, shard_rows, shard_rows, 4 * shard_rows]
    starts = [sum(counts[:k]) for k in range(len(counts))]
    small_size = sum(counts)
    in_1 = gather_first(ffn_in_weight)
    vectors = (norm1_gain, norm1_bias, skip_gain, step_size)
    vectors = vectors + (glu_bias, norm2_gain, norm2_bias, ffn_out_bias, ffn_in_bias)
    vectors = jnp.concatenate([v.reshape(-1, shard_rows) for v in vectors], axis=0)
    vectors = jnp.concatenate(gather_batch(vectors), axis=1)
    coefs = gather_batch(state_out)
    normed, perm = norm_call(
        me_b[None].astype(jnp.int32),
        x,
        jnp.pad(vectors[4:], ((0, 20 - vectors.shape[0]), (0, 0))),
        batch_bits,
        shard_rows,
        seq_size,
    )
    normed, in_1, one, coefs = together((normed, in_1, vectors[:4], coefs))
    in_w = gather_more(join(ffn_in_weight[None], in_1), 2)
    in_2 = middle_swap(in_w)
    glu_1 = gather_first(after(glu_weight, in_w))
    meta = meta_of(after((lengths, me_b, me_s), in_w))
    one = one.astype(f32)
    vec_one = jnp.concatenate([one[:3], jnp.zeros((5, chan), f32)], axis=0)
    coefs = jnp.concatenate(coefs, axis=1)
    coefs = jnp.swapaxes(coefs, 1, 2).astype(f32)
    near, far, input_mult = mode_tables(one[3:4], mode_count, length)
    joint = cmul(coefs, input_mult)
    lift = cmul((joint[0][:, None], joint[1][:, None]), far)
    fwd_np, inv_np = transform_tables(span)
    fwd, inv = jnp.asarray(fwd_np), jnp.asarray(inv_np)
    in_2, glu_1, lift, near = together((in_2, glu_1, lift, near))

    normed = exchange(normed)
    in_w = join(in_w, in_2)
    in_3 = near_swap(in_w)
    glu_w = gather_more(join(glu_weight[None], glu_1), 2)
    glu_2 = middle_swap(glu_w)
    spec = kernel_call(meta, after(lift, in_w, glu_w), near, fwd, seq_size, span)
    small_all = normed[:, micro * span :, :].astype(f32)
    small_all = small_all.reshape(seq_size, 16, batch_size, shard_rows)
    small_all = jnp.take(jnp.transpose(small_all, (2, 0, 1, 3)), piece_of, axis=0)
    glu_bias_all, gain_two, bias_two, out_bias, in_bias = [
        small_all[:, :, s : s + c].reshape(-1) for s, c in ((0, 2), (2, 1), (3, 1), (4, 1), (5, 4))
    ]
    vec_two = jnp.concatenate(
        [gain_two[None], bias_two[None], out_bias[None], jnp.zeros((5, width), f32)]
    )
    normed, in_3, glu_2, spec, ffn_out_weight, vec_two, glu_bias_all, in_bias = together(
        (normed, in_3, glu_2, spec, ffn_out_weight, vec_two, glu_bias_all, in_bias)
    )

    in_w = join(in_w, in_3).reshape(-1, ff)
    in_top = top_swap(in_w)
    glu_w = join(glu_w, glu_2)
    glu_3 = near_swap(glu_w)
    out_1 = gather_direct(ffn_out_weight)
    drive_spec, mixed, active_own = conv_call(
        meta, micro, normed, vec_one, after(spec, glu_w, in_w), fwd, inv
    )
    active_own, glu_3, out_1 = together((active_own, glu_3, out_1))

    out_w = gather_more(join(ffn_out_weight[None], *out_1), 1)
    out_3 = near_swap(out_w)
    active = exchange(after(active_own, out_w))
    glu_w = join(glu_w, after(glu_3, out_w)).reshape(-1, 2 * width)
    glu_top = top_swap(after(glu_w, in_top))
    in_parts = weave(over_low([in_w]), over_low([in_top]))
    glu_parts = weave(over_low([glu_w]), over_low([glu_top]))
    active, out_3, glu_parts = together((active, out_3, glu_parts))
    out_w = join(out_w, out_3).reshape(-1, width)
    out_top = top_swap(out_w)
    out_low = over_low([out_w])
    active = after(active, out_w)

    act, resid, gated, norm_two, norm_two_t, cot_out = gate_call(
        meta, chan_order, active, x, cot, vec_two, glu_bias_all[None], glu_parts
    )

    in_bias_blocks = in_bias.reshape(-1, 1, ff_block_of(piece_ff))

    def ffn_half(which, weights, **parts):
        return ffn_call(
            meta,
            order,
            out_table,
            place_at,
            base_table + which * half,
            column_table + which * half,
            cot_out,
            weights,
            **parts,
        )

    def low_rest(values):
        for bit in range(1, top):
            keep, send = values[: len(values) // 2], values[len(values) // 2 :]
            came = swap(jnp.stack([Sum(*v).total().astype(bf16) for v in send]), "batch", 1 << bit)
            values = [v + [came[i]] for i, v in enumerate(keep)]
        return values

    def low_sum(keep, came):
        return low_rest([[v, came[i]] for i, v in enumerate(keep)])

    def out_send(parts):
        return parts[half // 2][None] if half == 2 else jnp.stack(parts[half // 2 :])

    def rounded(terms):
        return Sum(*terms).total().astype(bf16)

    (back_a, bias_a), (out_a,), grad_out_a, keep_in_a, (send_in_a,) = ffn_half(
        0, out_low, norm=norm_two, bias=in_bias_blocks, w_in=in_parts, norm_t=norm_two_t
    )
    out_high = over_low([after(out_top, back_a)])
    in_a_came = swap(send_in_a, "batch", 1)
    out_a_came = swap(out_send(grad_out_a), "batch", 1)
    in_a_own, in_a_other = low_sum(keep_in_a, in_a_came)
    in_a_other = rounded(in_a_other)
    in_b_top = top_swap(in_a_other)
    (back_b, bias_b), (out_b,), grad_out_b, keep_in_b, (send_in_b,) = ffn_half(
        1,
        out_high,
        norm=after(norm_two, back_a, in_a_other),
        bias=in_bias_blocks,
        w_in=in_parts,
        norm_t=norm_two_t,
    )
    back_b, in_b_top, out_a_came = together((back_b, in_b_top, out_a_came))

    grad_resid, grad_gated, grad_glu_bias, sums, moved = gate_back_call(
        meta,
        chan_order,
        seq_size,
        [back_a, back_b],
        resid,
        gated,
        cot_out,
        vec_two,
        glu_parts,
    )
    grad_out_b, send_in_b = after((grad_out_b, send_in_b), moved)
    out_b_came = swap(out_send(grad_out_b), "batch", 1)
    in_b_came = swap(send_in_b, "batch", 1)

    grads_in = exchange(moved)
    (out_b_sum,) = low_sum(grad_out_b[: half // 2], out_b_came)
    out_b_sum = rounded(out_b_sum)
    out_a_top = top_swap(out_b_sum)
    keep_glu, send_glu = gate_weight_call(
        meta, chan_order, place_at, act, after(grad_gated, out_b_sum)
    )
    in_b_own, in_b_other = low_sum(keep_in_b, in_b_came)
    in_b_other = rounded([after(in_b_other[0], send_glu), *in_b_other[1:]])
    in_a_top = top_swap(in_b_other)
    sum_in_b = Sum(*in_b_own, in_b_top)
    in_b_near = sum_in_b.upper()
    in_b_near_came = near_swap(in_b_near)

    lower = (me_b >> top) == 0

    def halves(a, b, axis):
        return jnp.concatenate([jnp.where(lower, a, b), jnp.where(lower, b, a)], axis=axis)

    in_bias_sums = halves(bias_a.reshape(-1), bias_b.reshape(-1), 0)
    small_grads = jnp.concatenate(
        [
            value.reshape(devices, -1)
            for value in (grad_glu_bias[0], sums[1], sums[2], sums[0], in_bias_sums)
        ],
        axis=1,
    )
    small_grads = small_grads.reshape(batch_size, seq_size, -1)
    small_grads = jnp.moveaxis(small_grads, 1, 0).reshape(seq_size, -1)
    high = lax.reduce_precision(small_grads, 8, 7)
    rest = (small_grads - high).astype(bf16)
    extra_rows = -(-2 * small_grads.shape[1] // (16 * chan)) * 16
    blank = jnp.zeros((seq_size, extra_rows * chan - 2 * small_grads.shape[1]), bf16)
    extra = jnp.concatenate([high.astype(bf16), rest, blank], axis=1)
    extra = extra.reshape(seq_size, extra_rows, chan)
    (out_a_sum,) = low_sum(grad_out_a[: half // 2], out_a_came)
    out_a_sum = [v.reshape(seq_size, -1, width) for v in out_a_sum]
    grads_in, extra, out_a_sum, in_a_own, near, far, input_mult = together(
        (grads_in, extra, out_a_sum, in_a_own, near, far, input_mult)
    )

    moved_back, cross, state_sums = back_call(
        meta,
        after(grads_in, in_b_other, in_b_near),
        normed,
        drive_spec,
        mixed,
        vec_one,
        spec,
        fwd,
        inv,
        extra,
    )
    moved_back, cross, in_b_near_came, out_a_top = together(
        (moved_back, cross, in_b_near_came, out_a_top)
    )

    moved_back = exchange(moved_back)
    glu_came = swap(after(send_glu, cross), "batch", 1)
    sum_out = Sum(*out_a_sum, out_a_top.reshape(seq_size, -1, width))
    out_near = sum_out.upper()
    out_near_came = near_swap(out_near)
    sum_in_b.keep(after(in_b_near_came, out_near))
    in_b_middle = sum_in_b.upper()
    in_b_middle_came = middle_swap(in_b_middle)
    glu_own, glu_other = low_sum(keep_glu, after(glu_came, in_b_middle))
    glu_other = rounded(glu_other)
    glu_top_came = top_swap(glu_other)
    sum_in_a = Sum(*in_a_own, after(in_a_top, glu_other))
    in_a_near = sum_in_a.upper()
    in_a_near_came = near_swap(in_a_near)
    raw_modes = modes_call(meta, after(cross, in_a_near), far, near, inv)
    in_b_middle_came, in_a_near_came, out_near_came, glu_top_came = after(
        (in_b_middle_came, in_a_near_came, out_near_came, glu_top_came), raw_modes
    )
    sum_in_b.keep(in_b_middle_came)
    sum_in_b.middle()
    in_b_last = sum_in_b.upper()
    in_b_last_came = last_swap(in_b_last)
    sum_in_a.keep(after(in_a_near_came, in_b_last))
    in_a_middle = sum_in_a.upper()
    in_a_middle_came = middle_swap(in_a_middle)
    sum_glu = Sum(*glu_own, after(glu_top_came, in_a_middle))
    glu_near = sum_glu.upper()
    glu_near_came = near_swap(glu_near)
    sum_out.keep(after(out_near_came, glu_near))
    out_middle = sum_out.upper()
    out_middle_came = middle_swap(out_middle)

    input_grad = input_call(meta, after(moved_back, out_middle), x, grad_resid, perm)
    input_grad, in_a_middle_came, glu_near_came, out_middle_came = together(
        (input_grad, in_a_middle_came, glu_near_came, out_middle_came)
    )
    sum_out.keep(out_middle_came)
    sum_out.middle()
    out_last = sum_out.upper()
    out_last_came = last_swap(out_last)
    sum_glu.keep(after(glu_near_came, out_last))
    glu_middle = sum_glu.upper()
    glu_middle_came = middle_swap(glu_middle)
    sum_in_a.keep(after(in_a_middle_came, glu_middle))
    sum_in_a.middle()
    in_a_last = sum_in_a.upper()
    in_a_last_came = last_swap(in_a_last)
    sum_glu.keep(after(glu_middle_came, in_a_last))
    sum_glu.middle()
    glu_last = sum_glu.upper()
    glu_last_came = last_swap(glu_last)
    out_a, out_b, resid = after((out_a, out_b, resid), glu_last)
    output = resid + (out_a + out_b + vec_two[2:3]).reshape(resid.shape)
    output = output.astype(bf16)
    in_a_last_came, out_last_came, in_b_last_came = after(
        (in_a_last_came, out_last_came, in_b_last_came), output
    )
    raw_modes, state_sums = after((raw_modes, state_sums), input_grad)

    def finish(value, came):
        value.keep(came)
        return value.total()[0]

    z = cmul((raw_modes[0], raw_modes[1]), input_mult)
    state_grads = jnp.concatenate([z[0], -z[1], state_sums[:3]], axis=0).T
    state_grads = reduce_batch(state_grads.reshape(batch_size, shard_rows, -1))
    grad_state = jnp.stack([state_grads[:, :mode_count], state_grads[:, mode_count : 2 * mode_count]])
    grad_out_total = finish(sum_out, out_last_came)
    far_in = halves(finish(sum_in_a, in_a_last_came), finish(sum_in_b, in_b_last_came), 0)
    grad_in_total = jnp.concatenate([far_in[b] for b in range(batch_size)], axis=1)
    grad_glu_total = finish(sum_glu, glu_last_came)

    small_came = moved_back[:, micro * span :, :].reshape(seq_size, -1).astype(f32)
    small_came = jnp.sum(small_came, axis=0)
    size = batch_size * small_size
    small_came = (small_came[:size] + small_came[size : 2 * size]).reshape(batch_size, -1)
    own = reduce_batch(jnp.take(small_came, natural_piece, axis=0))
    grad_glu_bias_own, grad_gain_two, grad_bias_two, grad_out_bias, grad_in_bias_own = [
        own[s : s + c] for s, c in zip(starts, counts)
    ]

    return (
        output[:, None],
        input_grad[:, None],
        state_grads[:, 2 * mode_count + 1],
        state_grads[:, 2 * mode_count + 2],
        grad_state,
        state_grads[:, 2 * mode_count],
        grad_glu_total,
        grad_glu_bias_own,
        grad_gain_two,
        grad_bias_two,
        grad_in_total,
        grad_in_bias_own,
        grad_out_total,
        grad_out_bias,
    )


def solution(mesh):
    both = ("batch", "seq")
    rows = P(None, "batch", "seq", None)
    vector = P(both)
    matrix = P(both, None)
    state = P(None, both, None)
    return jax.shard_map(
        per_device,
        mesh=mesh,
        in_specs=(
            rows,
            P(None, "batch"),
            rows,
            vector,
            vector,
            vector,
            state,
            vector,
            matrix,
            vector,
            vector,
            vector,
            matrix,
            vector,
            matrix,
            vector,
        ),
        out_specs=(
            rows,
            rows,
            vector,
            vector,
            state,
            vector,
            matrix,
            vector,
            vector,
            vector,
            matrix,
            vector,
            matrix,
            vector,
        ),
        check_vma=False,
    )
```
